512 devices in a mesh: section: 32 (over x, z_hi, core), dp: 16 (over y, z_lo).
Axes of the slice: x: 4, y: 8, z: 8 (z_hi: 4, z_lo: 2; z = z_hi * 2 + z_lo), core: 2. Of those that a mesh axis runs over, the one named last changes fastest.
Arguments:
- layer_input: bfloat16 [32, 128, 12288], P('section', None, 'dp'), may hold values from -6 to 6
- fresh_input: bfloat16 [128, 12288], P(None, 'dp'), may hold values from -6 to 6
- out_grad: bfloat16 [32, 128, 12288], P('section', None, 'dp'), may hold values from -6 to 6
- held_stash: bfloat16 [32, 2, 128, 12288], P('section', None, None, 'dp'), may hold values from -6 to 6
- norm_gain: bfloat16 [32, 12288], P('section', 'dp'), may hold values from 0.099609375 to 1.8984375
- down_proj: bfloat16 [32, 12288, 512], P('section', 'dp'), may hold values from -0.0546875 to 0.0546875
- up_proj: bfloat16 [32, 512, 12288], P('section', None, 'dp'), may hold values from -0.25 to 0.25
- fetch_slot: int32 [32, 2], replicated, may hold values from 0 to 1
- evict_slot: int32 [32, 2], replicated, may hold values from 0 to 1
Outputs:
- next_output: bfloat16 [32, 128, 12288], P('section', None, 'dp')
- input_grad: bfloat16 [32, 128, 12288], P('section', None, 'dp')
- stash_out: bfloat16 [32, 2, 128, 12288], P('section', None, None, 'dp')
- gain_grad: float32 [32, 12288], P('section', 'dp')
- down_grad: bfloat16 [32, 12288, 512], P('section', 'dp')
- up_grad: bfloat16 [32, 512, 12288], P('section', None, 'dp')
The draws below stay inside these ranges and needn't reach their ends.
All inputs are finite; a program needn't handle non-finite values.
Results may differ from the reference program's by a relative error of at most 0.007.
Values may be sent and summed in bfloat16 or wider, within the bound.
No kernel may reach another device: no remote copies, remote signals or barrier semaphores. Data moves between devices by JAX's collectives and lax.ppermute only.
A program may use at most 64 MiB of HBM per device.

```python
import jax
import jax.numpy as jnp
from jax import lax

D = 12288
RANK = 512
ROWS = 128
SLOTS = 2
TICKS = 2
N_SECTION = 32


def place_ends(values, key, low, high):
    longest = values.shape.index(max(values.shape))
    spots = []
    for shift in (0, 1):
        where = [jax.random.randint(jax.random.fold_in(key, axis), (), 0, length) for axis, length in enumerate(values.shape)]
        where[longest] = (where[longest] + shift) % values.shape[longest]
        spots.append(tuple(where))
    return values.at[spots[0]].set(low).at[spots[1]].set(high)


def block_levels(stream_key, shape, split, low, largest):
    def one(axis_at, shards_of):
        heights = jax.random.uniform(jax.random.fold_in(jax.random.fold_in(stream_key, 6), axis_at), (shards_of,), jnp.float32, low / len(split), largest / len(split))
        return jnp.repeat(jnp.exp(heights), shape[axis_at] // shards_of).reshape((-1,) + (1,) * (len(shape) - axis_at - 1))

    loudness = one(*split[0])
    for cut in split[1:]:
        loudness = loudness * one(*cut)
    return loudness


def noise(key, extent, width, most, shards=(), kind=jnp.bfloat16):
    drawn = width * jax.random.normal(key, extent, jnp.float32)
    if shards:
        drawn = drawn * block_levels(key, extent, shards, -0.22, 0.18)
    return jnp.clip(drawn, -most, most).astype(kind)


def setup_inputs(seed: int = 0) -> dict:
    keys = jax.random.split(jax.random.key(seed), 10)
    return {
        "layer_input": noise(keys[0], (N_SECTION, ROWS, D), 1.0, 6.0, ((0, 32), (2, 16))),
        "fresh_input": noise(keys[1], (ROWS, D), 1.0, 6.0, ((1, 16),)),
        "out_grad": noise(keys[2], (N_SECTION, ROWS, D), 1.0, 6.0, ((0, 32), (2, 16))),
        "held_stash": noise(keys[3], (N_SECTION, SLOTS, ROWS, D), 1.0, 6.0, ((0, 32), (3, 16))),
        "norm_gain": jnp.clip(1.0 + 0.18 * jax.random.normal(keys[4], (N_SECTION, D), jnp.float32), 0.099609375, 1.8984375).astype(jnp.bfloat16),
        "down_proj": noise(keys[5], (N_SECTION, D, RANK), D ** -0.5, 0.0546875, ((0, 32), (1, 16))),
        "up_proj": noise(keys[6], (N_SECTION, RANK, D), RANK ** -0.5, 0.25, ((0, 32), (2, 16))),
        "fetch_slot": place_ends(jax.random.randint(keys[7], (N_SECTION, TICKS), 0, SLOTS), jax.random.fold_in(keys[7], 1), 0, SLOTS - 1).astype(jnp.int32),
        "evict_slot": place_ends(jax.random.randint(keys[8], (N_SECTION, TICKS), 0, SLOTS), jax.random.fold_in(keys[8], 1), 0, SLOTS - 1).astype(jnp.int32),
    }


def normalize(tokens, scale_gain):
    values = tokens.astype(jnp.float32)
    center_mean = lax.optimization_barrier(jnp.mean(values, axis=-1, keepdims=True))
    variance = lax.optimization_barrier(jnp.mean(values * values, axis=-1, keepdims=True)) - center_mean * center_mean
    inverse = lax.rsqrt(variance + 1e-05)
    normed = (values - center_mean) * inverse
    scaled = (normed * scale_gain).astype(jnp.bfloat16)
    return (normed, inverse, scaled)

def layer_forward(tokens, scale_gain, down_weight, up_weight):
    normed, inverse, scaled = normalize(tokens, scale_gain)
    hidden = jnp.dot(scaled, down_weight, preferred_element_type=jnp.float32)
    active = jax.nn.gelu(hidden).astype(jnp.bfloat16)
    return (tokens.astype(jnp.float32) + jnp.dot(active, up_weight, preferred_element_type=jnp.float32)).astype(jnp.bfloat16)

def layer_backward(tokens, upstream, scale_gain, down_weight, up_weight):
    normed, inverse, scaled = normalize(tokens, scale_gain)
    hidden = jnp.dot(scaled, down_weight, preferred_element_type=jnp.float32)
    active = jax.nn.gelu(hidden).astype(jnp.bfloat16)
    gelu_slope = jax.jvp(jax.nn.gelu, (hidden,), (jnp.ones_like(hidden),))[1]
    grad_active = lax.dot_general(upstream, up_weight, (((1,), (1,)), ((), ())), preferred_element_type=jnp.float32)
    grad_hidden = (grad_active * gelu_slope).astype(jnp.bfloat16)
    grad_scaled = lax.dot_general(grad_hidden, down_weight, (((1,), (1,)), ((), ())), preferred_element_type=jnp.float32)
    grad_normed = grad_scaled * scale_gain
    grad_rows = inverse * (grad_normed - lax.optimization_barrier(jnp.mean(grad_normed, axis=-1, keepdims=True)) - normed * lax.optimization_barrier(jnp.mean(grad_normed * normed, axis=-1, keepdims=True)))
    tokens_grad = (upstream.astype(jnp.float32) + grad_rows).astype(jnp.bfloat16)
    gain_term = lax.optimization_barrier(jnp.sum(grad_scaled * normed, axis=0))
    down_term = lax.dot_general(scaled, grad_hidden, (((0,), (0,)), ((), ())), preferred_element_type=jnp.float32)
    up_term = lax.dot_general(active, upstream, (((0,), (0,)), ((), ())), preferred_element_type=jnp.float32)
    return (tokens_grad, gain_term, down_term, up_term)

def reference(layer_input, fresh_input, out_grad, held_stash, norm_gain, down_proj, up_proj, fetch_slot, evict_slot):
    gains = norm_gain.astype(jnp.float32)
    sections = jnp.arange(layer_input.shape[0])
    stash = held_stash[::-1]
    first_out = lax.map(lambda items: layer_forward(items[0], items[1], items[2], items[3]), (layer_input, gains, down_proj, up_proj))
    first_fetch = stash[sections, fetch_slot[:, 0]]
    stash = stash.at[sections, evict_slot[:, 0]].set(layer_input)
    first_back = lax.map(lambda items: layer_backward(items[0], items[1], items[2], items[3], items[4]), (first_fetch, out_grad, gains, down_proj, up_proj))
    second_in = jnp.concatenate([fresh_input[None], first_out[:-1]], axis=0)
    second_up = jnp.concatenate([first_back[0][1:], first_out[-1:]], axis=0)
    next_output = lax.map(lambda items: layer_forward(items[0], items[1], items[2], items[3]), (second_in, gains, down_proj, up_proj))
    second_fetch = stash[sections, fetch_slot[:, 1]]
    stash = stash.at[sections, evict_slot[:, 1]].set(second_in)
    second_back = lax.map(lambda items: layer_backward(items[0], items[1], items[2], items[3], items[4]), (second_fetch, second_up, gains, down_proj, up_proj))
    gain_grad = first_back[1] + second_back[1]
    down_grad = (first_back[2] + second_back[2]).astype(jnp.bfloat16)
    up_grad = (first_back[3] + second_back[3]).astype(jnp.bfloat16)
    return (next_output, second_back[0], stash[::-1], gain_grad, down_grad, up_grad)
```

```python
import jax
import jax.numpy as jnp
from jax import lax
from jax.sharding import PartitionSpec as P

BF16 = jnp.bfloat16
F32 = jnp.float32
EPS = 1e-05


def rounded(value):
    return lax.reduce_precision(value, 8, 7)


def pieces(value):
    high = rounded(value)
    middle = rounded(value - high)
    low = rounded(value - high - middle)
    return [high.astype(BF16), middle.astype(BF16), low.astype(BF16)]


def joined(high, middle, low):
    return high.astype(F32) + middle.astype(F32) + low.astype(F32)


def across(block, width=None):
    return lax.all_to_all(block, "dp", 0, 0, tiled=True)


def mirrored(value):
    sections = lax.axis_size("section")
    return lax.ppermute(value, "section", [(i, sections - 1 - i) for i in range(sections)])


def shifted(value, by):
    sections = lax.axis_size("section")
    pairs = [(i, i + by) for i in range(sections) if 0 <= i + by < sections]
    return lax.ppermute(value, "section", pairs)


def lanes(columns, rows):
    block = jnp.concatenate(columns, axis=1)
    return jnp.pad(block, ((0, 0), (0, 128 - block.shape[1])))


def row_sums(values):
    return [jnp.sum(values, axis=1, keepdims=True), jnp.sum(values * values, axis=1, keepdims=True)]


def hidden_part(tokens, weight, column_sum):
    values = tokens.astype(F32)
    one, two = row_sums(values)
    local = one / values.shape[1]
    part = jnp.dot(tokens, weight, preferred_element_type=F32) - local * column_sum
    return part.astype(BF16), pieces(one) + pieces(two)


def slope_part(upstream, up_weight):
    return lax.dot_general(upstream, up_weight, (((1,), (1,)), ((), ())), preferred_element_type=F32).astype(BF16)


def summed(block, groups):
    rows = block.shape[0] // groups
    return jnp.sum(block.astype(F32).reshape(groups, rows, block.shape[1]), axis=0)


def finish_hidden(part, sums, column_sums, width):
    peers = column_sums.shape[0]
    one = joined(sums[:, 0], sums[:, 1], sums[:, 2]).reshape(peers, -1)
    two = joined(sums[:, 3], sums[:, 4], sums[:, 5]).reshape(peers, -1)
    mean = jnp.sum(one, axis=0) / width
    inverse = lax.rsqrt(jnp.sum(two, axis=0) / width - mean * mean + EPS)
    local = one / (width // peers) - mean[None]
    total = summed(part, peers) + lax.dot_general(
        local, column_sums, (((0,), (0,)), ((), ())), precision=lax.Precision.HIGHEST, preferred_element_type=F32
    )
    return total * inverse[:, None], mean[:, None], inverse[:, None]


def gelu_slope(hidden):
    return jax.jvp(jax.nn.gelu, (hidden,), (jnp.ones_like(hidden),))[1]


def to_all(block, peers):
    return jnp.tile(block, (peers, 1))


def back_stats(grad_hidden, hidden, mean, inverse, column_exact, width):
    grad = grad_hidden.astype(F32)
    first = jnp.sum(grad * column_exact, axis=1, keepdims=True) / width
    second = jnp.sum(grad * hidden, axis=1, keepdims=True) / width
    return pieces(mean) + pieces(inverse) + pieces(first) + pieces(second)


def unpack_stats(block):
    return [joined(block[:, 3 * i : 3 * i + 1], block[:, 3 * i + 1 : 3 * i + 2], block[:, 3 * i + 2 : 3 * i + 3]) for i in range(4)]


def backward(tokens, upstream, grad_hidden, active, stats, gain, down_weight):
    mean, inverse, first, second = stats
    normed = (tokens.astype(F32) - mean) * inverse
    scaled = (normed * gain).astype(BF16)
    grad_scaled = lax.dot_general(grad_hidden, down_weight, (((1,), (1,)), ((), ())), preferred_element_type=F32)
    grad_rows = inverse * (grad_scaled * gain - first - normed * second)
    tokens_grad = (upstream.astype(F32) + grad_rows).astype(BF16)
    gain_term = jnp.sum(grad_scaled * normed, axis=0)
    down_term = lax.dot_general(scaled, grad_hidden, (((0,), (0,)), ((), ())), preferred_element_type=F32)
    return tokens_grad, gain_term, down_term


def up_term(active, upstream):
    return lax.dot_general(active, upstream, (((0,), (0,)), ((), ())), preferred_element_type=F32)


def on_device(layer_input, fresh_input, out_grad, held_stash, norm_gain, down_proj, up_proj, fetch_slot, evict_slot):
    sections = lax.axis_size("section")
    peers = lax.axis_size("dp")
    place = lax.axis_index("section")
    partner = sections - 1 - place
    tokens0, grad0, stash = layer_input[0], out_grad[0], held_stash[0]
    gain = norm_gain[0].astype(F32)[None]
    down_weight, up_weight = down_proj[0], up_proj[0]
    rows, features = tokens0.shape
    rank = up_weight.shape[0]
    width = features * peers
    block_rows = rows // peers

    partner_fetch = lax.dynamic_slice(fetch_slot, (partner, 0), (1, 2))[0]
    partner_evict = lax.dynamic_slice(evict_slot, (partner, 0), (1, 2))[0]
    own_fetch = lax.dynamic_slice(fetch_slot, (place, 0), (1, 2))[0]
    own_evict = lax.dynamic_slice(evict_slot, (place, 0), (1, 2))[0]

    fetched0 = mirrored(jnp.where(partner_fetch[0] == 0, stash[0], stash[1]))
    both = mirrored(jnp.stack([jnp.where(partner_fetch[1] == 0, stash[0], stash[1]), tokens0], 0))
    fetched1 = jnp.where(own_fetch[1] == own_evict[0], tokens0, both[0])
    partner_tokens0 = both[1]

    exact = gain.T * down_weight.astype(F32)
    weight = exact.astype(BF16)
    column_sum = jnp.sum(rounded(exact), axis=0, keepdims=True)
    column_exact = jnp.sum(exact, axis=0, keepdims=True)
    columns = jnp.concatenate(pieces(column_sum) + pieces(column_exact), axis=0)
    columns = to_all(jnp.pad(columns, ((0, block_rows - 6), (0, 0))), peers)

    part, sums = hidden_part(tokens0, weight, column_sum)
    got = across(jnp.concatenate([part, slope_part(grad0, up_weight), columns, lanes(sums, rows)], axis=1))
    all_columns = got[:, 2 * rank : 3 * rank].reshape(peers, block_rows, rank)
    column_sums = joined(all_columns[:, 0], all_columns[:, 1], all_columns[:, 2])
    column_exact = jnp.sum(joined(all_columns[:, 3], all_columns[:, 4], all_columns[:, 5]), axis=0, keepdims=True)
    hidden_f0 = finish_hidden(got[:, :rank], got[:, 3 * rank :], column_sums, width)[0]
    slope0 = summed(got[:, rank : 2 * rank], peers)
    active_f0 = jax.nn.gelu(hidden_f0).astype(BF16)

    part, sums = hidden_part(fetched0, weight, column_sum)
    got = across(jnp.concatenate([part, lanes(sums, rows)], axis=1))
    hidden_b0, mean0, inverse0 = finish_hidden(got[:, :rank], got[:, rank:], column_sums, width)
    active_b0 = jax.nn.gelu(hidden_b0).astype(BF16)
    grad_hidden0 = (slope0 * gelu_slope(hidden_b0)).astype(BF16)
    stats = back_stats(grad_hidden0, hidden_b0, mean0, inverse0, column_exact, width)
    got = across(
        to_all(jnp.concatenate([active_f0, grad_hidden0, lanes(stats, block_rows)], axis=1), peers)
    )
    stats0 = unpack_stats(got[:, 2 * rank :])
    active_f0, grad_hidden0 = got[:, :rank], got[:, rank : 2 * rank]
    first_out = (tokens0.astype(F32) + jnp.dot(active_f0, up_weight, preferred_element_type=F32)).astype(BF16)
    first_grad, gain_term0, down_term0 = backward(fetched0, grad0, grad_hidden0, None, stats0, gain, down_weight)

    before_out = shifted(first_out, 1)
    after_grad = shifted(first_grad, -1)
    tokens1 = jnp.where(place == 0, fresh_input, before_out)
    grad1 = jnp.where(place == sections - 1, first_out, after_grad)
    partner_tokens1 = mirrored(tokens1)

    part, sums = hidden_part(tokens1, weight, column_sum)
    part_b, sums_b = hidden_part(fetched1, weight, column_sum)
    got = across(
        jnp.concatenate(
            [part, slope_part(grad1, up_weight), part_b, to_all(active_b0, peers), lanes(sums + sums_b, rows)], axis=1
        )
    )
    sums = got[:, 4 * rank :]
    hidden_f1 = finish_hidden(got[:, :rank], sums[:, :6], column_sums, width)[0]
    slope1 = summed(got[:, rank : 2 * rank], peers)
    hidden_b1, mean1, inverse1 = finish_hidden(got[:, 2 * rank : 3 * rank], sums[:, 6:12], column_sums, width)
    active_b0 = got[:, 3 * rank : 4 * rank]
    up_term0 = up_term(active_b0, grad0)
    active_f1 = jax.nn.gelu(hidden_f1).astype(BF16)
    active_b1 = jax.nn.gelu(hidden_b1).astype(BF16)
    grad_hidden1 = (slope1 * gelu_slope(hidden_b1)).astype(BF16)
    stats = back_stats(grad_hidden1, hidden_b1, mean1, inverse1, column_exact, width)
    got = across(
        to_all(jnp.concatenate([active_f1, grad_hidden1, active_b1, lanes(stats, block_rows)], axis=1), peers)
    )
    stats1 = unpack_stats(got[:, 3 * rank :])
    active_f1, grad_hidden1, active_b1 = got[:, :rank], got[:, rank : 2 * rank], got[:, 2 * rank : 3 * rank]
    next_output = (tokens1.astype(F32) + jnp.dot(active_f1, up_weight, preferred_element_type=F32)).astype(BF16)
    input_grad, gain_term1, down_term1 = backward(fetched1, grad1, grad_hidden1, None, stats1, gain, down_weight)

    stash = lax.dynamic_update_index_in_dim(stash, partner_tokens0, partner_evict[0], 0)
    stash = lax.dynamic_update_index_in_dim(stash, partner_tokens1, partner_evict[1], 0)
    down_grad = (down_term0 + down_term1).astype(BF16)
    up_grad = (up_term0 + up_term(active_b1, grad1)).astype(BF16)
    return (
        next_output[None],
        input_grad[None],
        stash[None],
        (gain_term0 + gain_term1)[None],
        down_grad[None],
        up_grad[None],
    )


def solution(mesh):
    placed = (
        P("section", None, "dp"),
        P(None, "dp"),
        P("section", None, "dp"),
        P("section", None, None, "dp"),
        P("section", "dp"),
        P("section", "dp", None),
        P("section", None, "dp"),
        P(),
        P(),
    )
    return jax.shard_map(
        on_device,
        mesh=mesh,
        in_specs=placed,
        out_specs=(
            P("section", None, "dp"),
            P("section", None, "dp"),
            P("section", None, None, "dp"),
            P("section", "dp"),
            P("section", "dp", None),
            P("section", None, "dp"),
        ),
        check_vma=False,
    )
```

```python
import math

import jax
import jax.numpy as jnp
from jax import lax
from jax.experimental import pallas as pl
from jax.experimental.pallas import tpu as pltpu
from jax.sharding import PartitionSpec as P

BF16 = jnp.bfloat16
F32 = jnp.float32
EPS = 1e-05
LANES = 128
ROOT = math.sqrt(2 / math.pi)
CUBE = 0.044715


def across(block):
    return lax.all_to_all(block, "dp", 0, 0, tiled=True)


def mirrored(value):
    sections = lax.axis_size("section")
    return lax.ppermute(value, "section", [(i, sections - 1 - i) for i in range(sections)])


def shifted(value, by):
    sections = lax.axis_size("section")
    pairs = [(i, i + by) for i in range(sections) if 0 <= i + by < sections]
    return lax.ppermute(value, "section", pairs)


def pieces(value):
    high = value.astype(BF16).astype(F32)
    middle = (value - high).astype(BF16).astype(F32)
    return [high, middle, value - high - middle]


def in_lanes(columns):
    rows = columns[0].shape[0]
    lane = lax.broadcasted_iota(jnp.int32, (rows, LANES), 1)
    block = jnp.zeros((rows, LANES), F32)
    for i, column in enumerate(columns):
        block = jnp.where(lane == i, column, block)
    return block


def from_lanes(block, first):
    lane = lax.broadcasted_iota(jnp.int32, block.shape, 1)
    return jnp.sum(jnp.where((lane >= first) & (lane < first + 3), block, 0.0), axis=1, keepdims=True)


def row_sums(values):
    one = jnp.sum(values, axis=1, keepdims=True)
    two = jnp.sum(values * values, axis=1, keepdims=True)
    return one, two


def hidden_part(tokens, weight, column_sum):
    values = tokens.astype(F32)
    one, two = row_sums(values)
    part = jnp.dot(tokens, weight, preferred_element_type=F32)
    return part - (one / values.shape[1]) * column_sum, pieces(one) + pieces(two)


def times_transposed(left, right):
    return lax.dot_general(left, right, (((1,), (1,)), ((), ())), preferred_element_type=F32)


def transposed_times(left, right):
    return lax.dot_general(left, right, (((0,), (0,)), ((), ())), preferred_element_type=F32)


def summed(block, peers):
    return jnp.sum(block.astype(F32).reshape(peers, -1, block.shape[1]), axis=0)


def finish_hidden(part, sums, first, column_sums, width):
    peers = len(column_sums)
    one = from_lanes(sums, first).reshape(peers, -1, 1)
    two = from_lanes(sums, first + 3).reshape(peers, -1, 1)
    mean = jnp.sum(one, axis=0) / width
    inverse = lax.rsqrt(jnp.sum(two, axis=0) / width - mean * mean + EPS)
    total = summed(part, peers)
    for peer in range(peers):
        total = total + (one[peer] / (width // peers) - mean) * column_sums[peer]
    return total * inverse, mean, inverse


def gelu(hidden):
    return hidden * (0.5 * (1.0 + jnp.tanh(ROOT * (hidden + CUBE * (hidden * hidden * hidden)))))


def gelu_and_slope(hidden):
    bent = jnp.tanh(ROOT * (hidden + CUBE * (hidden * hidden * hidden)))
    half = 0.5 * (1.0 + bent)
    slope = half + hidden * (0.5 * (1.0 - bent * bent)) * (ROOT * (1.0 + 3.0 * CUBE * (hidden * hidden)))
    return hidden * half, slope


def back_stats(grad_hidden, hidden, mean, inverse, column_exact, width):
    grad = grad_hidden.astype(F32)
    first = jnp.sum(grad * column_exact, axis=1, keepdims=True) / width
    second = jnp.sum(grad * hidden, axis=1, keepdims=True) / width
    return in_lanes(pieces(mean) + pieces(inverse) + pieces(first) + pieces(second))


def to_all(block, peers):
    rows, columns = block.shape
    return jnp.broadcast_to(block[None], (peers, rows, columns)).reshape(peers * rows, columns).astype(BF16)


def backward(tokens, upstream, grad_hidden, sums, gain, down_weight):
    mean, inverse, first, second = [from_lanes(sums, 3 * i) for i in range(4)]
    normed = (tokens.astype(F32) - mean) * inverse
    grad_scaled = times_transposed(grad_hidden, down_weight)
    grad_rows = inverse * (grad_scaled * gain - first - normed * second)
    tokens_grad = (upstream.astype(F32) + grad_rows).astype(BF16)
    gain_term = jnp.sum(grad_scaled * normed, axis=0, keepdims=True)
    return tokens_grad, (normed * gain).astype(BF16), gain_term


def start_kernel(tokens, upstream, gain, down, up, payload, weight, column_sum, *, peers, rank):
    rows = tokens.shape[0]
    features = tokens.shape[1]
    tall = jnp.broadcast_to(gain[...].astype(F32), (LANES, features)).T
    exact = down[...].astype(F32) * jnp.concatenate([tall] * (rank // LANES), axis=1)
    rounded = exact.astype(BF16)
    weight[...] = rounded
    one = jnp.sum(rounded.astype(F32), axis=0, keepdims=True)
    column_sum[...] = one
    two = jnp.sum(exact, axis=0, keepdims=True)
    row = lax.broadcasted_iota(jnp.int32, (rows // peers, rank), 0)
    block = jnp.zeros((rows // peers, rank), F32)
    for i, piece in enumerate(pieces(one) + pieces(two)):
        block = jnp.where(row == i, piece, block)
    part, sums = hidden_part(tokens[...], rounded, one)
    payload[:, :rank] = part.astype(BF16)
    payload[:, rank : 2 * rank] = times_transposed(upstream[...], up[...]).astype(BF16)
    payload[:, 2 * rank : 3 * rank] = to_all(block, peers)
    payload[:, 3 * rank :] = in_lanes(sums).astype(BF16)


def fetched_kernel(tokens, weight, column_sum, payload, zero, *, rank):
    part, sums = hidden_part(tokens[...], weight[...], column_sum[...])
    payload[:, :rank] = part.astype(BF16)
    payload[:, rank:] = in_lanes(sums).astype(BF16)
    zero[0] = 0


def middle_kernel(got_a, got_b, payload, columns, active_back, *, peers, rank, width):
    blocks = got_a[:, 2 * rank : 3 * rank].astype(F32).reshape(peers, -1, rank)
    row = lax.broadcasted_iota(jnp.int32, blocks.shape[1:], 0)
    column_sums, column_exact = [], jnp.zeros(blocks.shape[1:], F32)
    for peer in range(peers):
        column_sums.append(jnp.sum(jnp.where(row < 3, blocks[peer], 0.0), axis=0, keepdims=True))
        columns[peer : peer + 1, :] = column_sums[peer]
        column_exact = column_exact + jnp.where((row >= 3) & (row < 6), blocks[peer], 0.0)
    column_exact = jnp.sum(column_exact, axis=0, keepdims=True)
    columns[peers : peers + 1, :] = column_exact
    hidden_f = finish_hidden(got_a[:, :rank], got_a[:, 3 * rank :].astype(F32), 0, column_sums, width)[0]
    slope = summed(got_a[:, rank : 2 * rank], peers)
    hidden, mean, inverse = finish_hidden(got_b[:, :rank], got_b[:, rank:].astype(F32), 0, column_sums, width)
    active, bent = gelu_and_slope(hidden)
    active_back[...] = active.astype(BF16).astype(F32)
    grad_hidden = (slope * bent).astype(BF16)
    payload[:, :rank] = to_all(gelu(hidden_f), peers)
    payload[:, rank : 2 * rank] = to_all(grad_hidden.astype(F32), peers)
    payload[:, 2 * rank :] = to_all(back_stats(grad_hidden, hidden, mean, inverse, column_exact, width), peers)


def first_kernel(got, tokens, fetched, upstream, gain, down, up, out, grad, scaled, gain_term, *, rank):
    out[...] = (
        tokens[...].astype(F32) + jnp.dot(got[:, :rank], up[...], preferred_element_type=F32)
    ).astype(BF16)
    grad[...], scaled[...], gain_term[...] = backward(
        fetched[...], upstream[...], got[:, rank : 2 * rank], got[:, 2 * rank :].astype(F32), gain[...].astype(F32), down[...]
    )


def side_kernel(flag, arrived, tokens, weight, column_sum, active_back, payload, fetched, *, peers, rank):
    chosen = jnp.where(flag[0] == 1, tokens[...], arrived[...])
    fetched[...] = chosen
    part, sums = hidden_part(chosen, weight[...], column_sum[...])
    payload[:, :rank] = part.astype(BF16)
    payload[:, rank : 2 * rank] = to_all(active_back[...], peers)
    payload[:, 2 * rank :] = in_lanes(sums).astype(BF16)


def second_kernel(before, after, fresh, own, weight, column_sum, up, payload, tokens, upstream, *, rank):
    place = lax.axis_index("section")
    tokens[...] = jnp.where(place == 0, fresh[...], before[...])
    upstream[...] = jnp.where(place == lax.axis_size("section") - 1, own[...], after[...])
    part, sums = hidden_part(tokens[...], weight[...], column_sum[...])
    payload[:, :rank] = part.astype(BF16)
    payload[:, rank : 2 * rank] = times_transposed(upstream[...], up[...]).astype(BF16)
    payload[:, 2 * rank :] = in_lanes(sums).astype(BF16)


def late_kernel(got, side, columns, payload, *, peers, rank, width):
    column_sums = [columns[peer : peer + 1, :] for peer in range(peers)]
    hidden_f = finish_hidden(got[:, :rank], got[:, 2 * rank :].astype(F32), 0, column_sums, width)[0]
    slope = summed(got[:, rank : 2 * rank], peers)
    hidden, mean, inverse = finish_hidden(side[:, :rank], side[:, 2 * rank :].astype(F32), 0, column_sums, width)
    active, bent = gelu_and_slope(hidden)
    grad_hidden = (slope * bent).astype(BF16)
    payload[:, :rank] = to_all(gelu(hidden_f), peers)
    payload[:, rank : 2 * rank] = to_all(grad_hidden.astype(F32), peers)
    payload[:, 2 * rank : 3 * rank] = to_all(active, peers)
    stats = back_stats(grad_hidden, hidden, mean, inverse, columns[peers : peers + 1, :], width)
    payload[:, 3 * rank :] = to_all(stats, peers)


def last_kernel(
    got, got0, side, tokens, fetched, upstream, upstream0, scaled0, gain_term0, gain, down, up,
    out, grad, gain_grad, down_grad, up_grad, *, rank
):
    out[...] = (
        tokens[...].astype(F32) + jnp.dot(got[:, :rank], up[...], preferred_element_type=F32)
    ).astype(BF16)
    grad[...], scaled, gain_term = backward(
        fetched[...], upstream[...], got[:, rank : 2 * rank], got[:, 3 * rank :].astype(F32), gain[...].astype(F32), down[...]
    )
    gain_grad[...] = gain_term0[...] + gain_term
    down_grad[...] = transposed_times(
        jnp.concatenate([scaled0[...], scaled], axis=0),
        jnp.concatenate([got0[:, rank : 2 * rank], got[:, rank : 2 * rank]], axis=0),
    ).astype(BF16)
    up_grad[...] = transposed_times(
        jnp.concatenate([side[:, rank : 2 * rank], got[:, 2 * rank : 3 * rank]], axis=0),
        jnp.concatenate([upstream0[...], upstream[...]], axis=0),
    ).astype(BF16)


def call(body, outs, operands, products=1, smem=(), name=None):
    spaces = [pltpu.SMEM if i in smem else pltpu.VMEM for i in range(len(operands))]
    moved = sum(math.prod(o.shape) * o.dtype.itemsize for o in list(outs) + list(operands))
    results = pl.pallas_call(
        body,
        out_shape=tuple(outs),
        in_specs=[pl.BlockSpec(memory_space=s) for s in spaces],
        out_specs=tuple(pl.BlockSpec(memory_space=pltpu.SMEM if o.dtype == jnp.int32 else pltpu.VMEM) for o in outs),
        compiler_params=pltpu.CompilerParams(vmem_limit_bytes=40 * 2**20),
        cost_estimate=pl.CostEstimate(flops=products * 2 * 128 * 768 * 512, bytes_accessed=moved, transcendentals=0),
        name=name,
    )(*operands)
    return results


def bound(body, **sizes):
    def run(*refs):
        body(*refs, **sizes)

    return run


def on_device(layer_input, fresh_input, out_grad, held_stash, norm_gain, down_proj, up_proj, fetch_slot, evict_slot):
    sections = lax.axis_size("section")
    peers = lax.axis_size("dp")
    place = lax.axis_index("section")
    partner = sections - 1 - place
    tokens0, grad0, stash = layer_input[0], out_grad[0], held_stash[0]
    down, up = down_proj[0], up_proj[0]
    rows, features = tokens0.shape
    rank = up.shape[0]
    width = features * peers
    own = rows // peers

    def shape(*dims, dtype=BF16):
        return jax.ShapeDtypeStruct(dims, dtype)

    partner_fetch = lax.dynamic_slice(fetch_slot, (partner, 0), (1, 2))[0]
    partner_evict = lax.dynamic_slice(evict_slot, (partner, 0), (1, 2))[0]
    own_fetch = lax.dynamic_slice(fetch_slot, (place, 0), (1, 2))[0]
    own_evict = lax.dynamic_slice(evict_slot, (place, 0), (1, 2))[0]
    same = (own_fetch[1:] == own_evict[:1]).astype(jnp.int32)

    fetched0 = mirrored(jnp.where(partner_fetch[0] == 0, stash[0], stash[1]))
    payload, weight, column_sum = call(
        bound(start_kernel, peers=peers, rank=rank),
        [shape(rows, 3 * rank + LANES), shape(features, rank), shape(1, rank, dtype=F32)],
        [tokens0, grad0, norm_gain, down, up],
        products=2,
        name="start",
    )
    got_a = across(payload)
    payload, zero = call(
        bound(fetched_kernel, rank=rank),
        [shape(rows, rank + LANES), shape(1, dtype=jnp.int32)],
        [fetched0, weight, column_sum],
        name="fetched",
    )
    got_b = across(payload)
    both = mirrored(jnp.stack([jnp.where(partner_fetch[1] + zero[0] == 0, stash[0], stash[1]), tokens0], 0))
    payload, columns, active_back = call(
        bound(middle_kernel, peers=peers, rank=rank, width=width),
        [shape(rows, 2 * rank + LANES), shape(peers + 8, rank, dtype=F32), shape(own, rank, dtype=F32)],
        [got_a, got_b],
        name="middle",
    )
    got0 = across(payload)
    first_out, first_grad, scaled0, gain_term0 = call(
        bound(first_kernel, rank=rank),
        [shape(rows, features), shape(rows, features), shape(rows, features), shape(1, features, dtype=F32)],
        [got0, tokens0, fetched0, grad0, norm_gain, down, up],
        products=2,
        name="first",
    )
    before_out = shifted(first_out, 1)
    after_grad = shifted(first_grad, -1)
    payload, fetched1 = call(
        bound(side_kernel, peers=peers, rank=rank),
        [shape(rows, 2 * rank + LANES), shape(rows, features)],
        [same, both[0], tokens0, weight, column_sum, active_back],
        smem=(0,),
        name="side",
    )
    side = across(payload)
    payload, tokens1, grad1 = call(
        bound(second_kernel, rank=rank),
        [shape(rows, 2 * rank + LANES), shape(rows, features), shape(rows, features)],
        [before_out, after_grad, fresh_input, first_out, weight, column_sum, up],
        products=2,
        name="second",
    )
    got = across(payload)
    partner_tokens1 = mirrored(tokens1)
    (payload,) = call(
        bound(late_kernel, peers=peers, rank=rank, width=width),
        [shape(rows, 3 * rank + LANES)],
        [got, side, columns],
        name="late",
    )
    got1 = across(payload)
    next_output, input_grad, gain_grad, down_grad, up_grad = call(
        bound(last_kernel, rank=rank),
        [
            shape(rows, features),
            shape(rows, features),
            shape(1, features, dtype=F32),
            shape(features, rank),
            shape(rank, features),
        ],
        [got1, got0, side, tokens1, fetched1, grad1, grad0, scaled0, gain_term0, norm_gain, down, up],
        products=6,
        name="last",
    )
    slots = lax.broadcasted_iota(jnp.int32, (stash.shape[0], 1, 1), 0)
    stash = jnp.where(slots == partner_evict[0], both[1][None], stash)
    stash = jnp.where(slots == partner_evict[1], partner_tokens1[None], stash)
    return (next_output[None], input_grad[None], stash[None], gain_grad, down_grad[None], up_grad[None])


def solution(mesh):
    placed = (
        P("section", None, "dp"),
        P(None, "dp"),
        P("section", None, "dp"),
        P("section", None, None, "dp"),
        P("section", "dp"),
        P("section", "dp", None),
        P("section", None, "dp"),
        P(),
        P(),
    )
    return jax.shard_map(
        on_device,
        mesh=mesh,
        in_specs=placed,
        out_specs=(
            P("section", None, "dp"),
            P("section", None, "dp"),
            P("section", None, None, "dp"),
            P("section", "dp"),
            P("section", "dp", None),
            P("section", None, "dp"),
        ),
        check_vma=False,
    )
```

```python
import math

import jax
import jax.numpy as jnp
from jax import lax
from jax.experimental import pallas as pl
from jax.experimental.pallas import tpu as pltpu
from jax.sharding import PartitionSpec as P

BF16 = jnp.bfloat16
F32 = jnp.float32
EPS = 1e-05
LANES = 128
ROOT = math.sqrt(2 / math.pi)
CUBE = 0.044715


def across(block):
    return lax.all_to_all(block, "dp", 0, 0, tiled=True)


def mirrored(value):
    sections = lax.axis_size("section")
    return lax.ppermute(value, "section", [(i, sections - 1 - i) for i in range(sections)])


def shifted(value, by):
    sections = lax.axis_size("section")
    pairs = [(i, i + by) for i in range(sections) if 0 <= i + by < sections]
    return lax.ppermute(value, "section", pairs)


def pieces(value):
    high = value.astype(BF16).astype(F32)
    middle = (value - high).astype(BF16).astype(F32)
    return [high, middle, value - high - middle]


def in_lanes(columns):
    rows = columns[-1].shape[0]
    lane = lax.broadcasted_iota(jnp.int32, (rows, LANES), 1)
    block = jnp.zeros((rows, LANES), F32)
    for i, column in enumerate(columns):
        block = jnp.where(lane == i, column, block)
    return block


def from_lanes(block, first):
    lane = lax.broadcasted_iota(jnp.int32, block.shape, 1)
    return jnp.sum(jnp.where((lane >= first) & (lane < first + 3), block, 0.0), axis=1, keepdims=True)


def row_sums(values):
    one = jnp.sum(values, axis=1, keepdims=True)
    two = jnp.sum(values * values, axis=1, keepdims=True)
    return one, two


def hidden_part(tokens, weight, column_sum):
    values = tokens.astype(F32)
    one, two = row_sums(values)
    part = jnp.dot(tokens, weight, preferred_element_type=F32)
    return part - (one / values.shape[1]) * column_sum, pieces(one) + pieces(two)


def times_transposed(left, right):
    return lax.dot_general(left, right, (((1,), (1,)), ((), ())), preferred_element_type=F32)


def transposed_times(left, right):
    return lax.dot_general(left, right, (((0,), (0,)), ((), ())), preferred_element_type=F32)


def summed(block, peers):
    return jnp.sum(block.astype(F32).reshape(peers, -1, block.shape[1]), axis=0)


def finish_hidden(part, sums, first, column_sums, width):
    peers = len(column_sums)
    one = from_lanes(sums, first).reshape(peers, -1, 1)
    two = from_lanes(sums, first + 3).reshape(peers, -1, 1)
    mean = jnp.sum(one, axis=0) / width
    inverse = lax.rsqrt(jnp.sum(two, axis=0) / width - mean * mean + EPS)
    total = summed(part, peers)
    for peer in range(peers):
        total = total + (one[peer] / (width // peers) - mean) * column_sums[peer]
    return total * inverse, mean, inverse


def gelu(hidden):
    return hidden * (0.5 * (1.0 + jnp.tanh(ROOT * (hidden + CUBE * (hidden * hidden * hidden)))))


def gelu_and_slope(hidden):
    bent = jnp.tanh(ROOT * (hidden + CUBE * (hidden * hidden * hidden)))
    half = 0.5 * (1.0 + bent)
    slope = half + hidden * (0.5 * (1.0 - bent * bent)) * (ROOT * (1.0 + 3.0 * CUBE * (hidden * hidden)))
    return hidden * half, slope


def back_stats(grad_hidden, hidden, mean, inverse, column_exact, width):
    grad = grad_hidden.astype(F32)
    first = jnp.sum(grad * column_exact, axis=1, keepdims=True) / width
    second = jnp.sum(grad * hidden, axis=1, keepdims=True) / width
    return in_lanes(pieces(mean) + pieces(inverse) + pieces(first) + pieces(second))


def to_all(block, peers):
    rows, columns = block.shape
    return jnp.broadcast_to(block[None], (peers, rows, columns)).reshape(peers * rows, columns).astype(BF16)


def backward(tokens, upstream, grad_hidden, sums, gain, down_weight):
    mean, inverse, first, second = [from_lanes(sums, 3 * i) for i in range(4)]
    normed = (tokens.astype(F32) - mean) * inverse
    grad_scaled = times_transposed(grad_hidden, down_weight)
    grad_rows = inverse * (grad_scaled * gain - first - normed * second)
    tokens_grad = (upstream.astype(F32) + grad_rows).astype(BF16)
    gain_term = jnp.sum(grad_scaled * normed, axis=0, keepdims=True)
    return tokens_grad, (normed * gain).astype(BF16), gain_term


def copies(pairs, sems):
    started = [pltpu.make_async_copy(source, target, sems.at[i]) for i, (source, target) in enumerate(pairs)]
    for one in started:
        one.start()
    return started


def pick_kernel(fetch, stash, first, second, sems):
    partner = lax.axis_size("section") - 1 - lax.axis_index("section")
    for one in copies(
        [(stash.at[0, fetch[0, partner]], first), (stash.at[0, fetch[1, partner]], second)], sems
    ):
        one.wait()


def start_kernel(tokens, upstream, gain, down, up, payload, weight, column_sum, *, peers, rank):
    rows, features = tokens.shape
    tall = jnp.broadcast_to(gain[...].astype(F32), (LANES, features)).T
    exact = down[...].astype(F32) * jnp.concatenate([tall] * (rank // LANES), axis=1)
    rounded = exact.astype(BF16)
    weight[...] = rounded
    one = jnp.sum(rounded.astype(F32), axis=0, keepdims=True)
    column_sum[...] = one
    two = jnp.sum(exact, axis=0, keepdims=True)
    half = rank // 2
    row = lax.broadcasted_iota(jnp.int32, (rows // peers, half), 0)
    block = jnp.zeros((rows // peers, half), F32)
    for i, piece in enumerate(pieces(one)[:2] + pieces(two)[:2]):
        block = jnp.where(row == 2 * i, piece[:, :half], block)
        block = jnp.where(row == 2 * i + 1, piece[:, half:], block)
    part, sums = hidden_part(tokens[...], rounded, one)
    payload[:, :rank] = part.astype(BF16)
    payload[:, rank : 2 * rank] = times_transposed(upstream[...], up[...]).astype(BF16)
    payload[:, 2 * rank : 2 * rank + half] = to_all(block, peers)
    payload[:, 2 * rank + half :] = in_lanes(sums).astype(BF16)


def fetched_kernel(tokens, weight, column_sum, after, payload, *, rank):
    part, sums = hidden_part(tokens[...], weight[...], column_sum[...])
    payload[:, :rank] = part.astype(BF16)
    payload[:, rank:] = in_lanes(sums).astype(BF16)


def middle_kernel(got, got_b, payload, columns_out, active_back, columns, sems, *, peers, rank, width):
    half = rank // 2
    blocks = got[:, 2 * rank : 2 * rank + half].astype(F32).reshape(peers, -1, half)
    row = lax.broadcasted_iota(jnp.int32, blocks.shape[1:], 0)

    def joined(block, first):
        left = jnp.sum(jnp.where((row == first) | (row == first + 2), block, 0.0), axis=0, keepdims=True)
        right = jnp.sum(jnp.where((row == first + 1) | (row == first + 3), block, 0.0), axis=0, keepdims=True)
        return jnp.concatenate([left, right], axis=1)

    column_sums = []
    for peer in range(peers):
        column_sums.append(joined(blocks[peer], 0))
        columns[peer : peer + 1, :] = column_sums[peer]
    column_exact = joined(jnp.sum(blocks, axis=0), 4)
    columns[peers : peers + 1, :] = column_exact
    columns[peers + 1 :, :] = jnp.zeros((7, rank), F32)
    (saved,) = copies([(columns, columns_out)], sems)
    sums = got[:, 2 * rank + half :].astype(F32)
    hidden_f = finish_hidden(got[:, :rank], sums, 0, column_sums, width)[0]
    slope = summed(got[:, rank : 2 * rank], peers)
    hidden, mean, inverse = finish_hidden(got_b[:, :rank], got_b[:, rank:].astype(F32), 0, column_sums, width)
    active, bent = gelu_and_slope(hidden)
    active_back[...] = active
    grad_hidden = (slope * bent).astype(BF16)
    payload[:, :rank] = to_all(gelu(hidden_f), peers)
    payload[:, rank : 2 * rank] = to_all(grad_hidden.astype(F32), peers)
    payload[:, 2 * rank :] = to_all(back_stats(grad_hidden, hidden, mean, inverse, column_exact, width), peers)
    saved.wait()


def first_kernel(got, tokens, fetched, upstream, gain, down, up, out, grad, *, rank):
    out[...] = (
        tokens[...].astype(F32) + jnp.dot(got[:, :rank], up[...], preferred_element_type=F32)
    ).astype(BF16)
    grad[...] = backward(
        fetched[...], upstream[...], got[:, rank : 2 * rank], got[:, 2 * rank :].astype(F32), gain[...].astype(F32), down[...]
    )[0]


def side_kernel(
    fetch, evict, arrived, tokens, weight, column_sum, got, fetched0, upstream, gain, down, after,
    payload, fetched_out, scaled_out, gain_term, chosen, scaled, sems, *, rank
):
    place = lax.axis_index("section")
    chosen[...] = jnp.where(fetch[1, place] == evict[0, place], tokens[...], arrived[...])
    (saved,) = copies([(chosen, fetched_out)], sems)
    part, sums = hidden_part(chosen[...], weight[...], column_sum[...])
    payload[:, :rank] = part.astype(BF16)
    payload[:, rank:] = in_lanes([0.0] * 6 + sums).astype(BF16)
    scaled[...], gain_term[...] = backward(
        fetched0[...], upstream[...], got[:, rank : 2 * rank], got[:, 2 * rank :].astype(F32), gain[...].astype(F32), down[...]
    )[1:]
    last = pltpu.make_async_copy(scaled, scaled_out, sems.at[1])
    last.start()
    saved.wait()
    last.wait()


def second_kernel(
    before, after, fresh, own, weight, column_sum, up, side, payload, tokens_out, upstream_out,
    tokens, upstream, sems, *, rank
):
    place = lax.axis_index("section")
    tokens[...] = jnp.where(place == 0, fresh[...], before[...])
    upstream[...] = jnp.where(place == lax.axis_size("section") - 1, own[...], after[...])
    saved = copies([(tokens, tokens_out), (upstream, upstream_out)], sems)
    part, sums = hidden_part(tokens[...], weight[...], column_sum[...])
    payload[:, :rank] = part.astype(BF16)
    payload[:, rank : 2 * rank] = times_transposed(upstream[...], up[...]).astype(BF16)
    payload[:, 2 * rank : 3 * rank] = side[:, :rank]
    payload[:, 3 * rank :] = (side[:, rank:].astype(F32) + in_lanes(sums)).astype(BF16)
    for one in saved:
        one.wait()


def late_kernel(got, columns, active_back, after, payload, *, peers, rank, width):
    column_sums = [columns[peer : peer + 1, :] for peer in range(peers)]
    sums = got[:, 3 * rank :].astype(F32)
    hidden_f = finish_hidden(got[:, :rank], sums, 0, column_sums, width)[0]
    slope = summed(got[:, rank : 2 * rank], peers)
    hidden, mean, inverse = finish_hidden(got[:, 2 * rank : 3 * rank], sums, 6, column_sums, width)
    active, bent = gelu_and_slope(hidden)
    grad_hidden = (slope * bent).astype(BF16)
    payload[:, :rank] = to_all(gelu(hidden_f), peers)
    payload[:, rank : 2 * rank] = to_all(grad_hidden.astype(F32), peers)
    payload[:, 2 * rank : 3 * rank] = to_all(active, peers)
    payload[:, 3 * rank : 4 * rank] = to_all(active_back[...], peers)
    stats = back_stats(grad_hidden, hidden, mean, inverse, columns[peers : peers + 1, :], width)
    payload[:, 4 * rank :] = to_all(stats, peers)


def last_kernel(
    evict, stash, partner0, partner1, got, got0, tokens_in, fetched_in, upstream_in, upstream0, scaled_in, gain_term0,
    gain, down, up, out, grad, gain_grad, down_grad, up_grad, stash_out,
    tokens, fetched, upstream, scaled0, sems, slot_sems, *, rank
):
    slots = stash.shape[1]
    partner = lax.axis_size("section") - 1 - lax.axis_index("section")
    early, late = evict[0, partner], evict[1, partner]
    for i in range(slots):
        for source, taken in (
            (partner1, late == i),
            (partner0, (late != i) & (early == i)),
            (stash.at[0, i], (late != i) & (early != i)),
        ):
            @pl.when(taken)
            def _():
                pltpu.make_async_copy(source, stash_out.at[0, i], slot_sems.at[i]).start()

    loads = copies(
        [(tokens_in, tokens), (fetched_in, fetched), (upstream_in, upstream), (scaled_in, scaled0)], sems
    )
    product = jnp.dot(got[:, :rank], up[...], preferred_element_type=F32)
    loads[0].wait()
    out[...] = (tokens[...].astype(F32) + product).astype(BF16)
    loads[1].wait()
    loads[2].wait()
    grad[...], scaled, gain_term = backward(
        fetched[...], upstream[...], got[:, rank : 2 * rank], got[:, 4 * rank :].astype(F32), gain[...].astype(F32), down[...]
    )
    gain_grad[...] = gain_term0[...] + gain_term
    loads[3].wait()
    down_grad[...] = transposed_times(
        jnp.concatenate([scaled0[...], scaled], axis=0),
        jnp.concatenate([got0[:, rank : 2 * rank], got[:, rank : 2 * rank]], axis=0),
    ).astype(BF16)
    up_grad[...] = transposed_times(
        jnp.concatenate([got[:, 3 * rank : 4 * rank], got[:, 2 * rank : 3 * rank]], axis=0),
        jnp.concatenate([upstream0[...], upstream[...]], axis=0),
    ).astype(BF16)
    for i in range(slots):
        pltpu.make_async_copy(stash.at[0, i], stash_out.at[0, i], slot_sems.at[i]).wait()


def call(body, outs, operands, products=1, smem=(), left=(), left_outs=(), scratch=(), name=None):
    spaces = [pltpu.SMEM if i in smem else pl.ANY if i in left else pltpu.VMEM for i in range(len(operands))]
    out_spaces = [pl.ANY if i in left_outs else pltpu.VMEM for i in range(len(outs))]
    moved = sum(math.prod(o.shape) * o.dtype.itemsize for o in list(outs) + list(operands))
    return pl.pallas_call(
        body,
        out_shape=tuple(outs),
        in_specs=[pl.BlockSpec(memory_space=s) for s in spaces],
        out_specs=tuple(pl.BlockSpec(memory_space=s) for s in out_spaces),
        scratch_shapes=list(scratch),
        compiler_params=pltpu.CompilerParams(vmem_limit_bytes=16 * 2**20),
        cost_estimate=pl.CostEstimate(flops=products * 2 * 128 * 768 * 512, bytes_accessed=moved, transcendentals=0),
        name=name,
    )(*operands)


def bound(body, **sizes):
    def run(*refs):
        body(*refs, **sizes)

    return run


def on_device(layer_input, fresh_input, out_grad, held_stash, norm_gain, down_proj, up_proj, fetch_slot, evict_slot):
    peers = lax.axis_size("dp")
    tokens0, grad0 = layer_input[0], out_grad[0]
    down, up = down_proj[0], up_proj[0]
    rows, features = tokens0.shape
    rank = up.shape[0]
    width = features * peers
    own = rows // peers

    def shape(*dims, dtype=BF16):
        return jax.ShapeDtypeStruct(dims, dtype)

    half = rank // 2
    tile = pltpu.VMEM((rows, features), BF16)
    sems = pltpu.SemaphoreType.DMA
    fetch, evict = fetch_slot.T, evict_slot.T

    picked0, picked1 = call(
        pick_kernel,
        [shape(rows, features), shape(rows, features)],
        [fetch, held_stash],
        smem=(0,),
        left=(1,),
        scratch=[sems((2,))],
        name="pick",
    )
    fetched0 = mirrored(picked0)
    payload, weight, column_sum = call(
        bound(start_kernel, peers=peers, rank=rank),
        [shape(rows, 2 * rank + half + LANES), shape(features, rank), shape(1, rank, dtype=F32)],
        [tokens0, grad0, norm_gain, down, up],
        products=2,
        name="start",
    )
    got_a = across(payload)
    (payload,) = call(
        bound(fetched_kernel, rank=rank),
        [shape(rows, rank + LANES)],
        [fetched0, weight, column_sum, got_a],
        left=(3,),
        name="fetched",
    )
    got_b = across(payload)
    arrived1 = mirrored(picked1)
    payload, columns, active_back = call(
        bound(middle_kernel, peers=peers, rank=rank, width=width),
        [shape(rows, 2 * rank + LANES), shape(peers + 8, rank, dtype=F32), shape(own, rank, dtype=F32)],
        [got_a, got_b],
        left_outs=(1,),
        scratch=[pltpu.VMEM((peers + 8, rank), F32), sems((1,))],
        name="middle",
    )
    got0 = across(payload)
    first_out, first_grad = call(
        bound(first_kernel, rank=rank),
        [shape(rows, features), shape(rows, features)],
        [got0, tokens0, fetched0, grad0, norm_gain, down, up],
        products=2,
        name="first",
    )
    before_out = shifted(first_out, 1)
    after_grad = shifted(first_grad, -1)
    side, fetched1, scaled0, gain_term0 = call(
        bound(side_kernel, rank=rank),
        [shape(rows, rank + LANES), shape(rows, features), shape(rows, features), shape(1, features, dtype=F32)],
        [fetch, evict, arrived1, tokens0, weight, column_sum, got0, fetched0, grad0, norm_gain, down, first_out],
        smem=(0, 1),
        left=(11,),
        left_outs=(1, 2),
        scratch=[tile, tile, sems((2,))],
        products=2,
        name="side",
    )
    payload, tokens1, grad1 = call(
        bound(second_kernel, rank=rank),
        [shape(rows, 3 * rank + LANES), shape(rows, features), shape(rows, features)],
        [before_out, after_grad, fresh_input, first_out, weight, column_sum, up, side],
        left_outs=(1, 2),
        scratch=[tile, tile, sems((2,))],
        products=2,
        name="second",
    )
    got = across(payload)
    partner0 = mirrored(tokens0)
    (payload,) = call(
        bound(late_kernel, peers=peers, rank=rank, width=width),
        [shape(rows, 4 * rank + LANES)],
        [got, columns, active_back, partner0],
        left=(3,),
        name="late",
    )
    got1 = across(payload)
    partner1 = mirrored(tokens1)
    next_output, input_grad, gain_grad, down_grad, up_grad, stash = call(
        bound(last_kernel, rank=rank),
        [
            shape(rows, features),
            shape(rows, features),
            shape(1, features, dtype=F32),
            shape(features, rank),
            shape(rank, features),
            shape(*held_stash.shape),
        ],
        [
            evict, held_stash, partner0, partner1, got1, got0, tokens1, fetched1, grad1, grad0, scaled0, gain_term0,
            norm_gain, down, up,
        ],
        smem=(0,),
        left=(1, 2, 3, 6, 7, 8, 10),
        left_outs=(5,),
        scratch=[tile, tile, tile, tile, sems((4,)), sems((held_stash.shape[1],))],
        products=6,
        name="last",
    )
    return (next_output[None], input_grad[None], stash, gain_grad, down_grad[None], up_grad[None])


def solution(mesh):
    placed = (
        P("section", None, "dp"),
        P(None, "dp"),
        P("section", None, "dp"),
        P("section", None, None, "dp"),
        P("section", "dp"),
        P("section", "dp", None),
        P("section", None, "dp"),
        P(),
        P(),
    )
    return jax.shard_map(
        on_device,
        mesh=mesh,
        in_specs=placed,
        out_specs=(
            P("section", None, "dp"),
            P("section", None, "dp"),
            P("section", None, None, "dp"),
            P("section", "dp"),
            P("section", "dp", None),
            P("section", None, "dp"),
        ),
        check_vma=False,
    )
```

```python
import math

import jax
import jax.numpy as jnp
from jax import lax
from jax.experimental import pallas as pl
from jax.experimental.pallas import tpu as pltpu
from jax.sharding import PartitionSpec as P

BF16 = jnp.bfloat16
F32 = jnp.float32
EPS = 1e-05
LANES = 128
LONG = 6
ROOT = math.sqrt(2 / math.pi)
CUBE = 0.044715


def across(block):
    return lax.all_to_all(block, "dp", 0, 0, tiled=True)


def mirrored(value):
    sections = lax.axis_size("section")
    return lax.ppermute(value, "section", [(i, sections - 1 - i) for i in range(sections)])


def shifted(value, by):
    sections = lax.axis_size("section")
    pairs = [(i, i + by) for i in range(sections) if 0 <= i + by < sections]
    return lax.ppermute(value, "section", pairs)


def pieces(value):
    high = value.astype(BF16).astype(F32)
    middle = (value - high).astype(BF16).astype(F32)
    return [high, middle, value - high - middle]


def in_lanes(columns):
    rows = columns[-1].shape[0]
    lane = lax.broadcasted_iota(jnp.int32, (rows, LANES), 1)
    block = jnp.zeros((rows, LANES), F32)
    for i, column in enumerate(columns):
        block = jnp.where(lane == i, column, block)
    return block


def from_lanes(block, first):
    lane = lax.broadcasted_iota(jnp.int32, block.shape, 1)
    return jnp.sum(jnp.where((lane >= first) & (lane < first + 3), block, 0.0), axis=1, keepdims=True)


def row_sums(values):
    one = jnp.sum(values, axis=1, keepdims=True)
    two = jnp.sum(values * values, axis=1, keepdims=True)
    return one, two


def hidden_part(tokens, weight, column_sum):
    values = tokens.astype(F32)
    one, two = row_sums(values)
    part = jnp.dot(tokens, weight, preferred_element_type=F32)
    return part - (one / values.shape[1]) * column_sum, pieces(one) + pieces(two)


def times_transposed(left, right):
    return lax.dot_general(left, right, (((1,), (1,)), ((), ())), preferred_element_type=F32)


def transposed_times(left, right):
    return lax.dot_general(left, right, (((0,), (0,)), ((), ())), preferred_element_type=F32)


def summed(block, peers):
    return jnp.sum(block.astype(F32).reshape(peers, -1, block.shape[1]), axis=0)


def finish_hidden(part, sums, first, column_sums, width):
    peers = len(column_sums)
    one = from_lanes(sums, first).reshape(peers, -1, 1)
    two = from_lanes(sums, first + 3).reshape(peers, -1, 1)
    mean = jnp.sum(one, axis=0) / width
    inverse = lax.rsqrt(jnp.sum(two, axis=0) / width - mean * mean + EPS)
    total = summed(part, peers)
    for peer in range(peers):
        total = total + (one[peer] / (width // peers) - mean) * column_sums[peer]
    return total * inverse, mean, inverse


def gelu(hidden):
    return hidden * (0.5 * (1.0 + jnp.tanh(ROOT * (hidden + CUBE * (hidden * hidden * hidden)))))


def gelu_and_slope(hidden):
    bent = jnp.tanh(ROOT * (hidden + CUBE * (hidden * hidden * hidden)))
    half = 0.5 * (1.0 + bent)
    slope = half + hidden * (0.5 * (1.0 - bent * bent)) * (ROOT * (1.0 + 3.0 * CUBE * (hidden * hidden)))
    return hidden * half, slope


def back_stats(grad_hidden, hidden, mean, inverse, column_exact, width):
    grad = grad_hidden.astype(F32)
    first = jnp.sum(grad * column_exact, axis=1, keepdims=True) / width
    second = jnp.sum(grad * hidden, axis=1, keepdims=True) / width
    return in_lanes(pieces(mean) + pieces(inverse) + pieces(first) + pieces(second))


def to_all(block, peers):
    rows, columns = block.shape
    return jnp.broadcast_to(block[None], (peers, rows, columns)).reshape(peers * rows, columns).astype(BF16)


def backward(tokens, upstream, grad_hidden, sums, gain, down_weight):
    mean, inverse, first, second = [from_lanes(sums, 3 * i) for i in range(4)]
    normed = (tokens.astype(F32) - mean) * inverse
    grad_scaled = times_transposed(grad_hidden, down_weight)
    grad_rows = inverse * (grad_scaled * gain - first - normed * second)
    tokens_grad = (upstream.astype(F32) + grad_rows).astype(BF16)
    gain_term = jnp.sum(grad_scaled * normed, axis=0, keepdims=True)
    return tokens_grad, (normed * gain).astype(BF16), gain_term


def copies(pairs, sems):
    started = [pltpu.make_async_copy(source, target, sems.at[i]) for i, (source, target) in enumerate(pairs)]
    for one in started:
        one.start()
    return started


def pick_kernel(fetch, stash, first, second, sems):
    partner = lax.axis_size("section") - 1 - lax.axis_index("section")
    for one in copies(
        [(stash.at[0, fetch[0, partner]], first), (stash.at[0, fetch[1, partner]], second)], sems
    ):
        one.wait()


def start_kernel(tokens, upstream, gain, down, up, after, payload, weight, column_sum, *, peers, rank):
    rows, features = tokens.shape
    tall = jnp.broadcast_to(gain[...].astype(F32), (LANES, features)).T
    exact = down[...].astype(F32) * jnp.concatenate([tall] * (rank // LANES), axis=1)
    rounded = exact.astype(BF16)
    weight[...] = rounded
    one = jnp.sum(rounded.astype(F32), axis=0, keepdims=True)
    column_sum[...] = one
    two = jnp.sum(exact, axis=0, keepdims=True)
    half = rank // 2
    row = lax.broadcasted_iota(jnp.int32, (rows // peers, half), 0)
    block = jnp.zeros((rows // peers, half), F32)
    for i, piece in enumerate(pieces(one)[:2] + pieces(two)[:2]):
        block = jnp.where(row == 2 * i, piece[:, :half], block)
        block = jnp.where(row == 2 * i + 1, piece[:, half:], block)
    part, sums = hidden_part(tokens[...], rounded, one)
    payload[:, :rank] = part.astype(BF16)
    payload[:, rank : 2 * rank] = times_transposed(upstream[...], up[...]).astype(BF16)
    payload[:, 2 * rank : 2 * rank + half] = to_all(block, peers)
    payload[:, 2 * rank + half :] = in_lanes(sums).astype(BF16)


def fetched_kernel(tokens, weight, column_sum, part, sums):
    part[...], columns = hidden_part(tokens[...], weight[...], column_sum[...])
    sums[...] = in_lanes(columns)


def join_kernel(part, sums, after, payload, *, rank):
    payload[:, :rank] = part[...].astype(BF16)
    payload[:, rank:] = sums[...].astype(BF16)


def middle_kernel(got, got_b, payload, columns_out, active_back, columns, sems, *, peers, rank, width):
    half = rank // 2
    blocks = got[:, 2 * rank : 2 * rank + half].astype(F32).reshape(peers, -1, half)
    row = lax.broadcasted_iota(jnp.int32, blocks.shape[1:], 0)

    def joined(block, first):
        left = jnp.sum(jnp.where((row == first) | (row == first + 2), block, 0.0), axis=0, keepdims=True)
        right = jnp.sum(jnp.where((row == first + 1) | (row == first + 3), block, 0.0), axis=0, keepdims=True)
        return jnp.concatenate([left, right], axis=1)

    column_sums = []
    for peer in range(peers):
        column_sums.append(joined(blocks[peer], 0))
        columns[peer : peer + 1, :] = column_sums[peer]
    column_exact = joined(jnp.sum(blocks, axis=0), 4)
    columns[peers : peers + 1, :] = column_exact
    columns[peers + 1 :, :] = jnp.zeros((7, rank), F32)
    (saved,) = copies([(columns, columns_out)], sems)
    sums = got[:, 2 * rank + half :].astype(F32)
    hidden_f = finish_hidden(got[:, :rank], sums, 0, column_sums, width)[0]
    slope = summed(got[:, rank : 2 * rank], peers)
    hidden, mean, inverse = finish_hidden(got_b[:, :rank], got_b[:, rank:].astype(F32), 0, column_sums, width)
    active, bent = gelu_and_slope(hidden)
    active_back[...] = active
    grad_hidden = (slope * bent).astype(BF16)
    payload[:, :rank] = to_all(gelu(hidden_f), peers)
    payload[:, rank : 2 * rank] = to_all(grad_hidden.astype(F32), peers)
    payload[:, 2 * rank :] = to_all(back_stats(grad_hidden, hidden, mean, inverse, column_exact, width), peers)
    saved.wait()


def first_kernel(got, tokens, fetched, upstream, gain, down, up, after, out, grad, out_kept, sems, *, rank):
    out[...] = (
        tokens[...].astype(F32) + jnp.dot(got[:, :rank], up[...], preferred_element_type=F32)
    ).astype(BF16)
    (saved,) = copies([(out, out_kept)], sems)
    grad[...] = backward(
        fetched[...], upstream[...], got[:, rank : 2 * rank], got[:, 2 * rank :].astype(F32), gain[...].astype(F32), down[...]
    )[0]
    saved.wait()


def other_kernel(
    fetch, evict, arrived, tokens, weight, column_sum, payload, kept, chosen, sems, *, rank
):
    place = lax.axis_index("section")
    chosen[...] = jnp.where(fetch[1, place] == evict[0, place], tokens[...], arrived[...])
    (saved,) = copies([(chosen, kept.at[pl.ds(0, tokens.shape[0])])], sems)
    part, sums = hidden_part(chosen[...], weight[...], column_sum[...])
    payload[:, :rank] = part.astype(BF16)
    payload[:, rank:] = in_lanes([0.0] * 6 + sums).astype(BF16)
    saved.wait()


def terms_kernel(
    kept_in, got, fetched, upstream, gain, down, after, kept, gain_term, scaled, sems, *, rank
):
    scaled[...], gain_term[...] = backward(
        fetched[...], upstream[...], got[:, rank : 2 * rank], got[:, 2 * rank :].astype(F32), gain[...].astype(F32), down[...]
    )[1:]
    rows = scaled.shape[0]
    (saved,) = copies([(scaled, kept.at[pl.ds(rows, rows)])], sems)
    saved.wait()


def second_kernel(
    kept_in, before, after, fresh, own, weight, column_sum, up, side, payload, kept, tokens, upstream, sems, *, rank
):
    place = lax.axis_index("section")
    rows = before.shape[0]
    tokens[...] = jnp.where(place == 0, fresh[...], before[...])
    first = pltpu.make_async_copy(tokens, kept.at[pl.ds(2 * rows, rows)], sems.at[0])
    first.start()
    upstream[...] = after[...]

    @pl.when(place == lax.axis_size("section") - 1)
    def _():
        late = pltpu.make_async_copy(own, upstream, sems.at[2])
        late.start()
        late.wait()

    second = pltpu.make_async_copy(upstream, kept.at[pl.ds(3 * rows, rows)], sems.at[1])
    second.start()
    part, sums = hidden_part(tokens[...], weight[...], column_sum[...])
    payload[:, :rank] = part.astype(BF16)
    payload[:, rank : 2 * rank] = times_transposed(upstream[...], up[...]).astype(BF16)
    payload[:, 2 * rank : 3 * rank] = side[:, :rank]
    payload[:, 3 * rank :] = (side[:, rank:].astype(F32) + in_lanes(sums)).astype(BF16)
    first.wait()
    second.wait()


def late_kernel(got, columns, active_back, payload, *, peers, rank, width):
    column_sums = [columns[peer : peer + 1, :] for peer in range(peers)]
    sums = got[:, 3 * rank :].astype(F32)
    hidden_f = finish_hidden(got[:, :rank], sums, 0, column_sums, width)[0]
    slope = summed(got[:, rank : 2 * rank], peers)
    hidden, mean, inverse = finish_hidden(got[:, 2 * rank : 3 * rank], sums, 6, column_sums, width)
    active, bent = gelu_and_slope(hidden)
    grad_hidden = (slope * bent).astype(BF16)
    payload[:, :rank] = to_all(gelu(hidden_f), peers)
    payload[:, rank : 2 * rank] = to_all(grad_hidden.astype(F32), peers)
    payload[:, 2 * rank : 3 * rank] = to_all(active, peers)
    payload[:, 3 * rank : 4 * rank] = to_all(active_back[...], peers)
    stats = back_stats(grad_hidden, hidden, mean, inverse, columns[peers : peers + 1, :], width)
    payload[:, 4 * rank :] = to_all(stats, peers)


def stash_kernel(evict, stash, partner0, partner1, fresh, stash_out, done, sems):
    slots = stash.shape[1]
    partner = lax.axis_size("section") - 1 - lax.axis_index("section")
    early, late = evict[0, partner], evict[1, partner]
    for i in range(slots):
        for source, taken in (
            (partner1, (late == i) & (partner != 0)),
            (fresh, (late == i) & (partner == 0)),
            (partner0, (late != i) & (early == i)),
            (stash.at[0, i], (late != i) & (early != i)),
        ):
            @pl.when(taken)
            def _():
                pltpu.make_async_copy(source, stash_out.at[0, i], sems.at[i]).start()

    for i in range(slots):
        pltpu.make_async_copy(stash.at[0, i], stash_out.at[0, i], sems.at[i]).wait()
    done[...] = jnp.zeros_like(done)


def last_kernel(
    kept_in, own, done, got, got0, upstream0, gain_term0, gain, down, up,
    up_grad_out, out_out, grad, gain_grad, down_grad, kept, out, up_grad, sems, *, rank
):
    rows = upstream0.shape[0]
    (load,) = copies([(kept_in, kept)], sems)
    product = jnp.dot(got[:, :rank], up[...], preferred_element_type=F32)
    load.wait()
    out[...] = (kept[2 * rows : 3 * rows].astype(F32) + product).astype(BF16)
    first = pltpu.make_async_copy(out, out_out, sems.at[1])
    first.start()
    upstream = kept[3 * rows :]
    up_grad[...] = transposed_times(
        jnp.concatenate([got[:, 3 * rank : 4 * rank], got[:, 2 * rank : 3 * rank]], axis=0),
        jnp.concatenate([upstream0[...], upstream], axis=0),
    ).astype(BF16)
    second = pltpu.make_async_copy(up_grad, up_grad_out, sems.at[2])
    second.start()
    grad[...], scaled, gain_term = backward(
        kept[:rows], upstream, got[:, rank : 2 * rank], got[:, 4 * rank :].astype(F32), gain[...].astype(F32), down[...]
    )
    gain_grad[...] = gain_term0[...] + gain_term
    down_grad[...] = transposed_times(
        jnp.concatenate([kept[rows : 2 * rows], scaled], axis=0),
        jnp.concatenate([got0[:, rank : 2 * rank], got[:, rank : 2 * rank]], axis=0),
    ).astype(BF16)
    first.wait()
    second.wait()


def call(body, outs, operands, cost=1, smem=(), left=(), left_outs=(), scratch=(), aliases=(), name=None):
    spaces = [pltpu.SMEM if i in smem else pltpu.HBM if i in left else pltpu.VMEM for i in range(len(operands))]
    out_spaces = [pltpu.HBM if i in left_outs else pltpu.VMEM for i in range(len(outs))]
    return pl.pallas_call(
        body,
        out_shape=tuple(outs),
        in_specs=[pl.BlockSpec(memory_space=s) for s in spaces],
        out_specs=tuple(pl.BlockSpec(memory_space=s) for s in out_spaces),
        scratch_shapes=list(scratch),
        compiler_params=pltpu.CompilerParams(vmem_limit_bytes=16 * 2**20),
        cost_estimate=pl.CostEstimate(flops=cost * 2**31, bytes_accessed=cost * 2**20, transcendentals=0),
        input_output_aliases=dict(aliases),
        name=name,
    )(*operands)


def bound(body, **sizes):
    def run(*refs):
        body(*refs, **sizes)

    return run


def on_device(layer_input, fresh_input, out_grad, held_stash, norm_gain, down_proj, up_proj, fetch_slot, evict_slot):
    peers = lax.axis_size("dp")
    tokens0, grad0 = layer_input[0], out_grad[0]
    down, up = down_proj[0], up_proj[0]
    rows, features = tokens0.shape
    rank = up.shape[0]
    width = features * peers
    own = rows // peers

    def shape(*dims, dtype=BF16):
        return jax.ShapeDtypeStruct(dims, dtype)

    half = rank // 2
    tile = pltpu.VMEM((rows, features), BF16)
    sems = pltpu.SemaphoreType.DMA
    fetch, evict = fetch_slot.T, evict_slot.T

    picked0, picked1 = call(
        pick_kernel,
        [shape(rows, features), shape(rows, features)],
        [fetch, held_stash],
        smem=(0,),
        left=(1,),
        scratch=[sems((2,))],
        name="pick",
    )
    fetched0 = mirrored(picked0)
    payload, weight, column_sum = call(
        bound(start_kernel, peers=peers, rank=rank),
        [shape(rows, 2 * rank + half + LANES), shape(features, rank), shape(1, rank, dtype=F32)],
        [tokens0, grad0, norm_gain, down, up, picked1],
        left=(5,),
        cost=LONG,
        name="start",
    )
    got_a = across(payload)
    part, sums = call(
        fetched_kernel,
        [shape(rows, rank, dtype=F32), shape(rows, LANES, dtype=F32)],
        [fetched0, weight, column_sum],
        cost=LONG,
        name="fetched",
    )
    (payload,) = call(
        bound(join_kernel, rank=rank),
        [shape(rows, rank + LANES)],
        [part, sums, got_a],
        left=(2,),
        name="join",
    )
    got_b = across(payload)
    arrived1 = mirrored(picked1)
    payload, columns, active_back = call(
        bound(middle_kernel, peers=peers, rank=rank, width=width),
        [shape(rows, 2 * rank + LANES), shape(peers + 8, rank, dtype=F32), shape(own, rank, dtype=F32)],
        [got_a, got_b],
        left_outs=(1,),
        scratch=[pltpu.VMEM((peers + 8, rank), F32), sems((1,))],
        name="middle",
    )
    got0 = across(payload)
    other, kept = call(
        bound(other_kernel, rank=rank),
        [shape(rows, rank + LANES), shape(rank, features)],
        [fetch, evict, arrived1, tokens0, weight, column_sum],
        smem=(0, 1),
        left_outs=(1,),
        scratch=[tile, sems((1,))],
        cost=LONG,
        name="other",
    )
    first_out, first_grad, own_out = call(
        bound(first_kernel, rank=rank),
        [shape(rows, features)] * 3,
        [got0, tokens0, fetched0, grad0, norm_gain, down, up, other],
        left=(7,),
        left_outs=(2,),
        scratch=[sems((1,))],
        name="first",
    )
    before_out = shifted(first_out, 1)
    after_grad = shifted(first_grad, -1)
    partner0 = mirrored(tokens0)
    kept, gain_term0 = call(
        bound(terms_kernel, rank=rank),
        [shape(rank, features), shape(1, features, dtype=F32)],
        [kept, got0, fetched0, grad0, norm_gain, down, partner0],
        left=(0, 6),
        left_outs=(0,),
        aliases=[(0, 0)],
        scratch=[tile, sems((1,))],
        cost=LONG,
        name="terms",
    )
    payload, kept = call(
        bound(second_kernel, rank=rank),
        [shape(rows, 3 * rank + LANES), shape(rank, features)],
        [kept, before_out, after_grad, fresh_input, own_out, weight, column_sum, up, other],
        left=(0, 4),
        left_outs=(1,),
        aliases=[(0, 1)],
        scratch=[tile, tile, sems((3,))],
        name="second",
    )
    got = across(payload)
    sections = lax.axis_size("section")
    partner1 = lax.ppermute(own_out, "section", [(i, sections - 2 - i) for i in range(sections - 1)])
    (payload,) = call(
        bound(late_kernel, peers=peers, rank=rank, width=width),
        [shape(rows, 4 * rank + LANES)],
        [got, columns, active_back],
        name="late",
    )
    got1 = across(payload)
    stash, done = call(
        stash_kernel,
        [shape(*held_stash.shape), shape(8, LANES, dtype=F32)],
        [evict, held_stash, partner0, partner1, fresh_input],
        smem=(0,),
        left=(1, 2, 3, 4),
        left_outs=(0,),
        scratch=[sems((held_stash.shape[1],))],
        cost=LONG,
        name="stash",
    )
    up_grad, next_output, input_grad, gain_grad, down_grad = call(
        bound(last_kernel, rank=rank),
        [
            shape(rank, features),
            shape(rows, features),
            shape(rows, features),
            shape(1, features, dtype=F32),
            shape(features, rank),
        ],
        [kept, own_out, done, got1, got0, grad0, gain_term0, norm_gain, down, up],
        left=(0, 1, 2),
        left_outs=(0, 1),
        aliases=[(0, 0), (1, 1)],
        scratch=[pltpu.VMEM((4 * rows, features), BF16), tile, pltpu.VMEM((rank, features), BF16), sems((3,))],
        name="last",
    )
    return (next_output[None], input_grad[None], stash, gain_grad, down_grad[None], up_grad[None])


def solution(mesh):
    placed = (
        P("section", None, "dp"),
        P(None, "dp"),
        P("section", None, "dp"),
        P("section", None, None, "dp"),
        P("section", "dp"),
        P("section", "dp", None),
        P("section", None, "dp"),
        P(),
        P(),
    )
    return jax.shard_map(
        on_device,
        mesh=mesh,
        in_specs=placed,
        out_specs=(
            P("section", None, "dp"),
            P("section", None, "dp"),
            P("section", None, None, "dp"),
            P("section", "dp"),
            P("section", "dp", None),
            P("section", None, "dp"),
        ),
        check_vma=False,
    )
```

```python
import math

import jax
import jax.numpy as jnp
from jax import lax
from jax.experimental import pallas as pl
from jax.experimental.pallas import tpu as pltpu
from jax.sharding import PartitionSpec as P

BF16 = jnp.bfloat16
F32 = jnp.float32
EPS = 1e-05
LANES = 128
LONG = 6
ROOT = math.sqrt(2 / math.pi)
CUBE = 0.044715


def across(block):
    return lax.all_to_all(block, "dp", 0, 0, tiled=True)


def mirrored(value):
    sections = lax.axis_size("section")
    return lax.ppermute(value, "section", [(i, sections - 1 - i) for i in range(sections)])


def shifted(value, by):
    sections = lax.axis_size("section")
    pairs = [(i, i + by) for i in range(sections) if 0 <= i + by < sections]
    return lax.ppermute(value, "section", pairs)


def pieces(value):
    high = value.astype(BF16).astype(F32)
    middle = (value - high).astype(BF16).astype(F32)
    return [high, middle, value - high - middle]


def in_lanes(columns):
    rows = columns[-1].shape[0]
    lane = lax.broadcasted_iota(jnp.int32, (rows, LANES), 1)
    block = jnp.zeros((rows, LANES), F32)
    for i, column in enumerate(columns):
        block = jnp.where(lane == i, column, block)
    return block


def from_lanes(block, first):
    lane = lax.broadcasted_iota(jnp.int32, block.shape, 1)
    return jnp.sum(jnp.where((lane >= first) & (lane < first + 3), block, 0.0), axis=1, keepdims=True)


def row_sums(values):
    one = jnp.sum(values, axis=1, keepdims=True)
    two = jnp.sum(values * values, axis=1, keepdims=True)
    return one, two


def hidden_part(tokens, weight, column_sum):
    values = tokens.astype(F32)
    one, two = row_sums(values)
    part = jnp.dot(tokens, weight, preferred_element_type=F32)
    return part - (one / values.shape[1]) * column_sum, pieces(one) + pieces(two)


def times_transposed(left, right):
    return lax.dot_general(left, right, (((1,), (1,)), ((), ())), preferred_element_type=F32)


def transposed_times(left, right):
    return lax.dot_general(left, right, (((0,), (0,)), ((), ())), preferred_element_type=F32)


def summed(block, peers):
    return jnp.sum(block.astype(F32).reshape(peers, -1, block.shape[1]), axis=0)


def finish_hidden(part, sums, first, column_sums, width):
    peers = len(column_sums)
    one = from_lanes(sums, first).reshape(peers, -1, 1)
    two = from_lanes(sums, first + 3).reshape(peers, -1, 1)
    mean = jnp.sum(one, axis=0) / width
    inverse = lax.rsqrt(jnp.sum(two, axis=0) / width - mean * mean + EPS)
    total = summed(part, peers)
    for peer in range(peers):
        total = total + (one[peer] / (width // peers) - mean) * column_sums[peer]
    return total * inverse, mean, inverse


def gelu(hidden):
    return hidden * (0.5 * (1.0 + jnp.tanh(ROOT * (hidden + CUBE * (hidden * hidden * hidden)))))


def gelu_and_slope(hidden):
    bent = jnp.tanh(ROOT * (hidden + CUBE * (hidden * hidden * hidden)))
    half = 0.5 * (1.0 + bent)
    slope = half + hidden * (0.5 * (1.0 - bent * bent)) * (ROOT * (1.0 + 3.0 * CUBE * (hidden * hidden)))
    return hidden * half, slope


def back_stats(grad_hidden, hidden, mean, inverse, column_exact, width):
    grad = grad_hidden.astype(F32)
    first = jnp.sum(grad * column_exact, axis=1, keepdims=True) / width
    second = jnp.sum(grad * hidden, axis=1, keepdims=True) / width
    return in_lanes(pieces(mean) + pieces(inverse) + pieces(first) + pieces(second))


def to_all(block, peers):
    rows, columns = block.shape
    return jnp.broadcast_to(block[None], (peers, rows, columns)).reshape(peers * rows, columns).astype(BF16)


def backward(tokens, upstream, grad_hidden, sums, gain, down_weight):
    mean, inverse, first, second = [from_lanes(sums, 3 * i) for i in range(4)]
    normed = (tokens.astype(F32) - mean) * inverse
    grad_scaled = times_transposed(grad_hidden, down_weight)
    grad_rows = inverse * (grad_scaled * gain - first - normed * second)
    tokens_grad = (upstream.astype(F32) + grad_rows).astype(BF16)
    gain_term = jnp.sum(grad_scaled * normed, axis=0, keepdims=True)
    return tokens_grad, (normed * gain).astype(BF16), gain_term


def copies(pairs, sems):
    started = [pltpu.make_async_copy(source, target, sems.at[i]) for i, (source, target) in enumerate(pairs)]
    for one in started:
        one.start()
    return started


def pick_kernel(fetch, stash, first, second, sems):
    partner = lax.axis_size("section") - 1 - lax.axis_index("section")
    for one in copies(
        [(stash.at[0, fetch[0, partner]], first), (stash.at[0, fetch[1, partner]], second)], sems
    ):
        one.wait()


def start_kernel(tokens, upstream, gain, down, up, other, payload, weight, column_sum, both, *, peers, rank):
    both[0] = other[...]
    both[1] = tokens[...]
    rows, features = tokens.shape
    tall = jnp.broadcast_to(gain[...].astype(F32), (LANES, features)).T
    exact = down[...].astype(F32) * jnp.concatenate([tall] * (rank // LANES), axis=1)
    rounded = exact.astype(BF16)
    weight[...] = rounded
    one = jnp.sum(rounded.astype(F32), axis=0, keepdims=True)
    column_sum[...] = one
    two = jnp.sum(exact, axis=0, keepdims=True)
    half = rank // 2
    row = lax.broadcasted_iota(jnp.int32, (rows // peers, half), 0)
    block = jnp.zeros((rows // peers, half), F32)
    for i, piece in enumerate(pieces(one)[:2] + pieces(two)[:2]):
        block = jnp.where(row == 2 * i, piece[:, :half], block)
        block = jnp.where(row == 2 * i + 1, piece[:, half:], block)
    part, sums = hidden_part(tokens[...], rounded, one)
    payload[:, :rank] = part.astype(BF16)
    payload[:, rank : 2 * rank] = times_transposed(upstream[...], up[...]).astype(BF16)
    payload[:, 2 * rank : 2 * rank + half] = to_all(block, peers)
    payload[:, 2 * rank + half :] = in_lanes(sums).astype(BF16)


def fetched_kernel(tokens, weight, column_sum, early, payload, *, rank):
    part, sums = hidden_part(tokens[...], weight[...], column_sum[...])
    block = early.shape[1] - LANES
    payload[:, :block] = early[:, :block]
    payload[:, block : block + rank] = part.astype(BF16)
    payload[:, block + rank :] = (early[:, block:].astype(F32) + in_lanes([0.0] * 6 + sums)).astype(BF16)


def middle_kernel(got, payload, columns_out, active_back, columns, sems, *, peers, rank, width):
    half = rank // 2
    blocks = got[:, 2 * rank : 2 * rank + half].astype(F32).reshape(peers, -1, half)
    row = lax.broadcasted_iota(jnp.int32, blocks.shape[1:], 0)

    def joined(block, first):
        left = jnp.sum(jnp.where((row == first) | (row == first + 2), block, 0.0), axis=0, keepdims=True)
        right = jnp.sum(jnp.where((row == first + 1) | (row == first + 3), block, 0.0), axis=0, keepdims=True)
        return jnp.concatenate([left, right], axis=1)

    column_sums = []
    for peer in range(peers):
        column_sums.append(joined(blocks[peer], 0))
        columns[peer : peer + 1, :] = column_sums[peer]
    column_exact = joined(jnp.sum(blocks, axis=0), 4)
    columns[peers : peers + 1, :] = column_exact
    columns[peers + 1 :, :] = jnp.zeros((7, rank), F32)
    (saved,) = copies([(columns, columns_out)], sems)
    sums = got[:, 3 * rank + half :].astype(F32)
    hidden_f = finish_hidden(got[:, :rank], sums, 0, column_sums, width)[0]
    slope = summed(got[:, rank : 2 * rank], peers)
    hidden, mean, inverse = finish_hidden(
        got[:, 2 * rank + half : 3 * rank + half], sums, 6, column_sums, width
    )
    active, bent = gelu_and_slope(hidden)
    active_back[...] = active
    grad_hidden = (slope * bent).astype(BF16)
    payload[:, :rank] = to_all(gelu(hidden_f), peers)
    payload[:, rank : 2 * rank] = to_all(grad_hidden.astype(F32), peers)
    payload[:, 2 * rank :] = to_all(back_stats(grad_hidden, hidden, mean, inverse, column_exact, width), peers)
    saved.wait()


def first_kernel(got, tokens, fetched, upstream, gain, down, up, after, out, grad, *, rank):
    out[...] = (
        tokens[...].astype(F32) + jnp.dot(got[:, :rank], up[...], preferred_element_type=F32)
    ).astype(BF16)
    grad[...] = backward(
        fetched[...], upstream[...], got[:, rank : 2 * rank], got[:, 2 * rank :].astype(F32), gain[...].astype(F32), down[...]
    )[0]


def other_kernel(
    fetch, evict, arrived, tokens, weight, column_sum, payload, kept, chosen, sems, *, rank
):
    place = lax.axis_index("section")
    chosen[...] = jnp.where(fetch[1, place] == evict[0, place], tokens[...], arrived[0])
    (saved,) = copies([(chosen, kept.at[pl.ds(0, tokens.shape[0])])], sems)
    part, sums = hidden_part(chosen[...], weight[...], column_sum[...])
    payload[:, :rank] = part.astype(BF16)
    payload[:, rank:] = in_lanes([0.0] * 6 + sums).astype(BF16)
    saved.wait()


def terms_kernel(
    kept_in, got, fetched, upstream, gain, down, kept, gain_term, scaled, sems, *, rank
):
    scaled[...], gain_term[...] = backward(
        fetched[...], upstream[...], got[:, rank : 2 * rank], got[:, 2 * rank :].astype(F32), gain[...].astype(F32), down[...]
    )[1:]
    rows = scaled.shape[0]
    (saved,) = copies([(scaled, kept.at[pl.ds(rows, rows)])], sems)
    saved.wait()


def second_kernel(
    kept_in, before, after, fresh, own, weight, column_sum, up, side, payload, kept, tokens_out, tokens, upstream, sems,
    *, rank
):
    place = lax.axis_index("section")
    rows = before.shape[0]
    tokens[...] = jnp.where(place == 0, fresh[...], before[...])
    first = pltpu.make_async_copy(tokens, tokens_out, sems.at[0])
    first.start()
    upstream[...] = jnp.where(place == lax.axis_size("section") - 1, own[...], after[...])
    second = pltpu.make_async_copy(upstream, kept.at[pl.ds(2 * rows, rows)], sems.at[1])
    second.start()
    part, sums = hidden_part(tokens[...], weight[...], column_sum[...])
    payload[:, :rank] = part.astype(BF16)
    payload[:, rank : 2 * rank] = times_transposed(upstream[...], up[...]).astype(BF16)
    payload[:, 2 * rank : 3 * rank] = side[:, :rank]
    payload[:, 3 * rank :] = (side[:, rank:].astype(F32) + in_lanes(sums)).astype(BF16)
    first.wait()
    second.wait()


def late_kernel(got, columns, active_back, payload, *, peers, rank, width):
    column_sums = [columns[peer : peer + 1, :] for peer in range(peers)]
    sums = got[:, 3 * rank :].astype(F32)
    hidden_f = finish_hidden(got[:, :rank], sums, 0, column_sums, width)[0]
    slope = summed(got[:, rank : 2 * rank], peers)
    hidden, mean, inverse = finish_hidden(got[:, 2 * rank : 3 * rank], sums, 6, column_sums, width)
    active, bent = gelu_and_slope(hidden)
    grad_hidden = (slope * bent).astype(BF16)
    payload[:, :rank] = to_all(gelu(hidden_f), peers)
    payload[:, rank : 2 * rank] = to_all(grad_hidden.astype(F32), peers)
    payload[:, 2 * rank : 3 * rank] = to_all(active, peers)
    payload[:, 3 * rank : 4 * rank] = to_all(active_back[...], peers)
    stats = back_stats(grad_hidden, hidden, mean, inverse, columns[peers : peers + 1, :], width)
    payload[:, 4 * rank :] = to_all(stats, peers)


def stash_kernel(evict, stash, arrived, partner1, stash_out, done, sems):
    slots = stash.shape[1]
    partner = lax.axis_size("section") - 1 - lax.axis_index("section")
    early, late = evict[0, partner], evict[1, partner]
    for i in range(slots):
        for source, taken in (
            (partner1, late == i),
            (arrived.at[1], (late != i) & (early == i)),
            (stash.at[0, i], (late != i) & (early != i)),
        ):
            @pl.when(taken)
            def _():
                pltpu.make_async_copy(source, stash_out.at[0, i], sems.at[i]).start()

    for i in range(slots):
        pltpu.make_async_copy(stash.at[0, i], stash_out.at[0, i], sems.at[i]).wait()
    done[...] = jnp.zeros_like(done)


def last_kernel(
    kept_in, tokens_in, done, got, got0, upstream0, gain_term0, gain, down, up,
    up_grad_out, out_out, grad_out, gain_grad, down_grad_out, kept, tokens, up_grad, out, grad, down_grad, sems, *, rank
):
    rows = upstream0.shape[0]
    span = pl.ds(2 * rows, rows)
    loads = copies(
        [
            (kept_in.at[span], kept.at[span]),
            (tokens_in, tokens),
            (kept_in.at[pl.ds(0, 2 * rows)], kept.at[pl.ds(0, 2 * rows)]),
        ],
        sems,
    )
    product = jnp.dot(got[:, :rank], up[...], preferred_element_type=F32)
    loads[0].wait()
    upstream = kept[2 * rows : 3 * rows]
    up_grad[...] = transposed_times(
        jnp.concatenate([got[:, 3 * rank : 4 * rank], got[:, 2 * rank : 3 * rank]], axis=0),
        jnp.concatenate([upstream0[...], upstream], axis=0),
    ).astype(BF16)
    loads[1].wait()
    out[...] = (tokens[...].astype(F32) + product).astype(BF16)
    loads[2].wait()
    stores = [
        pltpu.make_async_copy(up_grad, up_grad_out, sems.at[3]),
        pltpu.make_async_copy(out, out_out, sems.at[4]),
        pltpu.make_async_copy(down_grad, down_grad_out, sems.at[5]),
        pltpu.make_async_copy(grad, grad_out, sems.at[6]),
    ]
    stores[0].start()
    stores[1].start()
    grad[...], scaled, gain_term = backward(
        kept[:rows], upstream, got[:, rank : 2 * rank], got[:, 4 * rank :].astype(F32), gain[...].astype(F32), down[...]
    )
    stores[3].start()
    gain_grad[...] = gain_term0[...] + gain_term
    down_grad[...] = transposed_times(
        jnp.concatenate([kept[rows : 2 * rows], scaled], axis=0),
        jnp.concatenate([got0[:, rank : 2 * rank], got[:, rank : 2 * rank]], axis=0),
    ).astype(BF16)
    stores[2].start()
    for one in stores:
        one.wait()


def call(body, outs, operands, cost=1, smem=(), left=(), left_outs=(), scratch=(), aliases=(), name=None):
    spaces = [pltpu.SMEM if i in smem else pltpu.HBM if i in left else pltpu.VMEM for i in range(len(operands))]
    out_spaces = [pltpu.HBM if i in left_outs else pltpu.VMEM for i in range(len(outs))]
    return pl.pallas_call(
        body,
        out_shape=tuple(outs),
        in_specs=[pl.BlockSpec(memory_space=s) for s in spaces],
        out_specs=tuple(pl.BlockSpec(memory_space=s) for s in out_spaces),
        scratch_shapes=list(scratch),
        compiler_params=pltpu.CompilerParams(vmem_limit_bytes=16 * 2**20),
        cost_estimate=pl.CostEstimate(flops=cost * 2**31, bytes_accessed=cost * 2**20, transcendentals=0),
        input_output_aliases=dict(aliases),
        name=name,
    )(*operands)


def bound(body, **sizes):
    def run(*refs):
        body(*refs, **sizes)

    return run


def on_device(layer_input, fresh_input, out_grad, held_stash, norm_gain, down_proj, up_proj, fetch_slot, evict_slot):
    peers = lax.axis_size("dp")
    tokens0, grad0 = layer_input[0], out_grad[0]
    down, up = down_proj[0], up_proj[0]
    rows, features = tokens0.shape
    rank = up.shape[0]
    width = features * peers
    own = rows // peers

    def shape(*dims, dtype=BF16):
        return jax.ShapeDtypeStruct(dims, dtype)

    half = rank // 2
    tile = pltpu.VMEM((rows, features), BF16)
    sems = pltpu.SemaphoreType.DMA
    fetch, evict = fetch_slot.T, evict_slot.T

    picked, other = call(
        pick_kernel,
        [shape(rows, features), shape(rows, features)],
        [fetch, held_stash],
        smem=(0,),
        left=(1,),
        scratch=[sems((2,))],
        name="pick",
    )
    fetched0 = mirrored(picked)
    early, weight, column_sum, both = call(
        bound(start_kernel, peers=peers, rank=rank),
        [shape(rows, 2 * rank + half + LANES), shape(features, rank), shape(1, rank, dtype=F32), shape(2, rows, features)],
        [tokens0, grad0, norm_gain, down, up, other],
        name="start",
    )
    (payload,) = call(
        bound(fetched_kernel, rank=rank),
        [shape(rows, 3 * rank + half + LANES)],
        [fetched0, weight, column_sum, early],
        name="fetched",
    )
    got = across(payload)
    both = mirrored(both)
    payload, columns, active_back = call(
        bound(middle_kernel, peers=peers, rank=rank, width=width),
        [shape(rows, 2 * rank + LANES), shape(peers + 8, rank, dtype=F32), shape(own, rank, dtype=F32)],
        [got],
        left_outs=(1,),
        scratch=[pltpu.VMEM((peers + 8, rank), F32), sems((1,))],
        name="middle",
    )
    got0 = across(payload)
    other, kept = call(
        bound(other_kernel, rank=rank),
        [shape(rows, rank + LANES), shape(rank, features)],
        [fetch, evict, both, tokens0, weight, column_sum],
        smem=(0, 1),
        left_outs=(1,),
        scratch=[tile, sems((1,))],
        cost=LONG,
        name="other",
    )
    first_out, first_grad = call(
        bound(first_kernel, rank=rank),
        [shape(rows, features)] * 2,
        [got0, tokens0, fetched0, grad0, norm_gain, down, up, other],
        left=(7,),
        name="first",
    )
    before_out = shifted(first_out, 1)
    after_grad = shifted(first_grad, -1)
    kept, gain_term0 = call(
        bound(terms_kernel, rank=rank),
        [shape(rank, features), shape(1, features, dtype=F32)],
        [kept, got0, fetched0, grad0, norm_gain, down],
        left=(0,),
        left_outs=(0,),
        aliases=[(0, 0)],
        scratch=[tile, sems((1,))],
        cost=LONG,
        name="terms",
    )
    payload, kept, tokens1 = call(
        bound(second_kernel, rank=rank),
        [shape(rows, 3 * rank + LANES), shape(rank, features), shape(rows, features)],
        [kept, before_out, after_grad, fresh_input, first_out, weight, column_sum, up, other],
        left=(0,),
        left_outs=(1, 2),
        aliases=[(0, 1)],
        scratch=[tile, tile, sems((2,))],
        name="second",
    )
    got = across(payload)
    partner1 = mirrored(tokens1)
    (payload,) = call(
        bound(late_kernel, peers=peers, rank=rank, width=width),
        [shape(rows, 4 * rank + LANES)],
        [got, columns, active_back],
        name="late",
    )
    got1 = across(payload)
    stash, done = call(
        stash_kernel,
        [shape(*held_stash.shape), shape(8, LANES, dtype=F32)],
        [evict, held_stash, both, partner1],
        smem=(0,),
        left=(1, 2, 3),
        left_outs=(0,),
        scratch=[sems((held_stash.shape[1],))],
        cost=LONG,
        name="stash",
    )
    up_grad, next_output, input_grad, gain_grad, down_grad = call(
        bound(last_kernel, rank=rank),
        [
            shape(rank, features),
            shape(rows, features),
            shape(rows, features),
            shape(1, features, dtype=F32),
            shape(features, rank),
        ],
        [kept, tokens1, done, got1, got0, grad0, gain_term0, norm_gain, down, up],
        left=(0, 1, 2),
        left_outs=(0, 1, 2, 4),
        aliases=[(0, 0), (1, 1)],
        scratch=[
            pltpu.VMEM((3 * rows, features), BF16),
            tile,
            pltpu.VMEM((rank, features), BF16),
            tile,
            tile,
            pltpu.VMEM((features, rank), BF16),
            sems((7,)),
        ],
        name="last",
    )
    return (next_output[None], input_grad[None], stash, gain_grad, down_grad[None], up_grad[None])


def solution(mesh):
    placed = (
        P("section", None, "dp"),
        P(None, "dp"),
        P("section", None, "dp"),
        P("section", None, None, "dp"),
        P("section", "dp"),
        P("section", "dp", None),
        P("section", None, "dp"),
        P(),
        P(),
    )
    return jax.shard_map(
        on_device,
        mesh=mesh,
        in_specs=placed,
        out_specs=(
            P("section", None, "dp"),
            P("section", None, "dp"),
            P("section", None, None, "dp"),
            P("section", "dp"),
            P("section", "dp", None),
            P("section", None, "dp"),
        ),
        check_vma=False,
    )
```

```python
import math

import jax
import jax.numpy as jnp
from jax import lax
from jax.experimental import pallas as pl
from jax.experimental.pallas import tpu as pltpu
from jax.sharding import PartitionSpec as P

BF16 = jnp.bfloat16
F32 = jnp.float32
EPS = 1e-05
LANES = 128
LONG = 6
CHUNKS = 4
ROOT = math.sqrt(2 / math.pi)
CUBE = 0.044715


def across(block):
    return lax.all_to_all(block, "dp", 0, 0, tiled=True)


def mirrored(value):
    sections = lax.axis_size("section")
    return lax.ppermute(value, "section", [(i, sections - 1 - i) for i in range(sections)])


def shifted(value, by):
    sections = lax.axis_size("section")
    pairs = [(i, i + by) for i in range(sections) if 0 <= i + by < sections]
    return lax.ppermute(value, "section", pairs)


def pieces(value):
    high = value.astype(BF16).astype(F32)
    middle = (value - high).astype(BF16).astype(F32)
    return [high, middle, value - high - middle]


def in_lanes(columns):
    rows = columns[-1].shape[0]
    lane = lax.broadcasted_iota(jnp.int32, (rows, LANES), 1)
    block = jnp.zeros((rows, LANES), F32)
    for i, column in enumerate(columns):
        block = jnp.where(lane == i, column, block)
    return block


def from_lanes(block, first):
    lane = lax.broadcasted_iota(jnp.int32, block.shape, 1)
    return jnp.sum(jnp.where((lane >= first) & (lane < first + 3), block, 0.0), axis=1, keepdims=True)


def row_sums(values):
    one = jnp.sum(values, axis=1, keepdims=True)
    two = jnp.sum(values * values, axis=1, keepdims=True)
    return one, two


def hidden_part(tokens, weight, column_sum):
    values = tokens.astype(F32)
    one, two = row_sums(values)
    part = jnp.dot(tokens, weight, preferred_element_type=F32)
    return part - (one / values.shape[1]) * column_sum, pieces(one) + pieces(two)


def times_transposed(left, right):
    return lax.dot_general(left, right, (((1,), (1,)), ((), ())), preferred_element_type=F32)


def transposed_times(left, right):
    return lax.dot_general(left, right, (((0,), (0,)), ((), ())), preferred_element_type=F32)


def summed(block, peers):
    return jnp.sum(block.astype(F32).reshape(peers, -1, block.shape[1]), axis=0)


def finish_hidden(part, sums, first, column_sums, width):
    peers = len(column_sums)
    one = from_lanes(sums, first).reshape(peers, -1, 1)
    two = from_lanes(sums, first + 3).reshape(peers, -1, 1)
    mean = jnp.sum(one, axis=0) / width
    inverse = lax.rsqrt(jnp.sum(two, axis=0) / width - mean * mean + EPS)
    total = summed(part, peers)
    for peer in range(peers):
        total = total + (one[peer] / (width // peers) - mean) * column_sums[peer]
    return total * inverse, mean, inverse


def gelu(hidden):
    return hidden * (0.5 * (1.0 + jnp.tanh(ROOT * (hidden + CUBE * (hidden * hidden * hidden)))))


def gelu_and_slope(hidden):
    bent = jnp.tanh(ROOT * (hidden + CUBE * (hidden * hidden * hidden)))
    half = 0.5 * (1.0 + bent)
    slope = half + hidden * (0.5 * (1.0 - bent * bent)) * (ROOT * (1.0 + 3.0 * CUBE * (hidden * hidden)))
    return hidden * half, slope


def back_stats(grad_hidden, hidden, mean, inverse, column_exact, width):
    grad = grad_hidden.astype(F32)
    first = jnp.sum(grad * column_exact, axis=1, keepdims=True) / width
    second = jnp.sum(grad * hidden, axis=1, keepdims=True) / width
    return in_lanes(pieces(mean) + pieces(inverse) + pieces(first) + pieces(second))


def to_all(block, peers):
    rows, columns = block.shape
    return jnp.broadcast_to(block[None], (peers, rows, columns)).reshape(peers * rows, columns).astype(BF16)


def backward(tokens, upstream, grad_hidden, sums, gain, down_weight):
    mean, inverse, first, second = [from_lanes(sums, 3 * i) for i in range(4)]
    normed = (tokens.astype(F32) - mean) * inverse
    grad_scaled = times_transposed(grad_hidden, down_weight)
    grad_rows = inverse * (grad_scaled * gain - first - normed * second)
    tokens_grad = (upstream.astype(F32) + grad_rows).astype(BF16)
    gain_term = jnp.sum(grad_scaled * normed, axis=0, keepdims=True)
    return tokens_grad, (normed * gain).astype(BF16), gain_term


def copies(pairs, sems):
    started = [pltpu.make_async_copy(source, target, sems.at[i]) for i, (source, target) in enumerate(pairs)]
    for one in started:
        one.start()
    return started


def pick_kernel(fetch, stash, first, second):
    partner = lax.axis_size("section") - 1 - lax.axis_index("section")
    first[...] = stash[0, fetch[0, partner]]
    second[...] = stash[0, fetch[1, partner]]


def chunks(source, target, count):
    step = source.shape[0] // count
    return [(source.at[pl.ds(i * step, step)], target.at[pl.ds(i * step, step)]) for i in range(count)]


def start_kernel(tokens, upstream, gain, down, up, other, payload, weight, column_sum, both, *, peers, rank):
    both[0] = other[...]
    both[1] = tokens[...]
    rows, features = tokens.shape
    tall = jnp.broadcast_to(gain[...].astype(F32), (LANES, features)).T
    exact = down[...].astype(F32) * jnp.concatenate([tall] * (rank // LANES), axis=1)
    rounded = exact.astype(BF16)
    weight[...] = rounded
    one = jnp.sum(rounded.astype(F32), axis=0, keepdims=True)
    column_sum[...] = one
    two = jnp.sum(exact, axis=0, keepdims=True)
    half = rank // 2
    row = lax.broadcasted_iota(jnp.int32, (rows // peers, half), 0)
    block = jnp.zeros((rows // peers, half), F32)
    for i, piece in enumerate(pieces(one)[:2] + pieces(two)[:2]):
        block = jnp.where(row == 2 * i, piece[:, :half], block)
        block = jnp.where(row == 2 * i + 1, piece[:, half:], block)
    part, sums = hidden_part(tokens[...], rounded, one)
    payload[:, :rank] = part.astype(BF16)
    payload[:, rank : 2 * rank] = times_transposed(upstream[...], up[...]).astype(BF16)
    payload[:, 2 * rank : 2 * rank + half] = to_all(block, peers)
    payload[:, 2 * rank + half :] = in_lanes(sums).astype(BF16)


def fetched_kernel(tokens, weight, column_sum, early, payload, *, rank):
    part, sums = hidden_part(tokens[...], weight[...], column_sum[...])
    block = early.shape[1] - LANES
    payload[:, :block] = early[:, :block]
    payload[:, block : block + rank] = part.astype(BF16)
    payload[:, block + rank :] = (early[:, block:].astype(F32) + in_lanes([0.0] * 6 + sums)).astype(BF16)


def middle_kernel(got, payload, columns_out, active_back, columns, sems, *, peers, rank, width):
    half = rank // 2
    blocks = got[:, 2 * rank : 2 * rank + half].astype(F32).reshape(peers, -1, half)
    row = lax.broadcasted_iota(jnp.int32, blocks.shape[1:], 0)

    def joined(block, first):
        left = jnp.sum(jnp.where((row == first) | (row == first + 2), block, 0.0), axis=0, keepdims=True)
        right = jnp.sum(jnp.where((row == first + 1) | (row == first + 3), block, 0.0), axis=0, keepdims=True)
        return jnp.concatenate([left, right], axis=1)

    column_sums = []
    for peer in range(peers):
        column_sums.append(joined(blocks[peer], 0))
        columns[peer : peer + 1, :] = column_sums[peer]
    column_exact = joined(jnp.sum(blocks, axis=0), 4)
    columns[peers : peers + 1, :] = column_exact
    columns[peers + 1 :, :] = jnp.zeros((7, rank), F32)
    (saved,) = copies([(columns, columns_out)], sems)
    sums = got[:, 3 * rank + half :].astype(F32)
    hidden_f = finish_hidden(got[:, :rank], sums, 0, column_sums, width)[0]
    slope = summed(got[:, rank : 2 * rank], peers)
    hidden, mean, inverse = finish_hidden(
        got[:, 2 * rank + half : 3 * rank + half], sums, 6, column_sums, width
    )
    active, bent = gelu_and_slope(hidden)
    active_back[...] = active
    grad_hidden = (slope * bent).astype(BF16)
    payload[:, :rank] = to_all(gelu(hidden_f), peers)
    payload[:, rank : 2 * rank] = to_all(grad_hidden.astype(F32), peers)
    payload[:, 2 * rank :] = to_all(back_stats(grad_hidden, hidden, mean, inverse, column_exact, width), peers)
    saved.wait()


def first_kernel(got, tokens, fetched, upstream, gain, down, up, after, out, grad, *, rank):
    out[...] = (
        tokens[...].astype(F32) + jnp.dot(got[:, :rank], up[...], preferred_element_type=F32)
    ).astype(BF16)
    grad[...] = backward(
        fetched[...], upstream[...], got[:, rank : 2 * rank], got[:, 2 * rank :].astype(F32), gain[...].astype(F32), down[...]
    )[0]


def other_kernel(
    fetch, evict, arrived, tokens, weight, column_sum, payload, kept, chosen, sems, *, rank
):
    place = lax.axis_index("section")
    chosen[...] = jnp.where(fetch[1, place] == evict[0, place], tokens[...], arrived[0])
    (saved,) = copies([(chosen, kept.at[pl.ds(0, tokens.shape[0])])], sems)
    part, sums = hidden_part(chosen[...], weight[...], column_sum[...])
    payload[:, :rank] = part.astype(BF16)
    payload[:, rank:] = in_lanes([0.0] * 6 + sums).astype(BF16)
    saved.wait()


def terms_kernel(
    kept_in, got, fetched, upstream, gain, down, kept, gain_term, scaled, sems, *, rank
):
    scaled[...], gain_term[...] = backward(
        fetched[...], upstream[...], got[:, rank : 2 * rank], got[:, 2 * rank :].astype(F32), gain[...].astype(F32), down[...]
    )[1:]
    rows = scaled.shape[0]
    (saved,) = copies([(scaled, kept.at[pl.ds(rows, rows)])], sems)
    saved.wait()


def second_kernel(
    kept_in, before, after, fresh, own, weight, column_sum, up, side, payload, kept, tokens_out, tokens, upstream, sems,
    *, rank
):
    place = lax.axis_index("section")
    rows = before.shape[0]
    tokens[...] = jnp.where(place == 0, fresh[...], before[...])
    first = pltpu.make_async_copy(tokens, tokens_out, sems.at[0])
    first.start()
    upstream[...] = jnp.where(place == lax.axis_size("section") - 1, own[...], after[...])
    second = pltpu.make_async_copy(upstream, kept.at[pl.ds(2 * rows, rows)], sems.at[1])
    second.start()
    part, sums = hidden_part(tokens[...], weight[...], column_sum[...])
    payload[:, :rank] = part.astype(BF16)
    payload[:, rank : 2 * rank] = times_transposed(upstream[...], up[...]).astype(BF16)
    payload[:, 2 * rank : 3 * rank] = side[:, :rank]
    payload[:, 3 * rank :] = (side[:, rank:].astype(F32) + in_lanes(sums)).astype(BF16)
    first.wait()
    second.wait()


def late_kernel(got, columns, active_back, payload, *, peers, rank, width):
    column_sums = [columns[peer : peer + 1, :] for peer in range(peers)]
    sums = got[:, 3 * rank :].astype(F32)
    hidden_f = finish_hidden(got[:, :rank], sums, 0, column_sums, width)[0]
    slope = summed(got[:, rank : 2 * rank], peers)
    hidden, mean, inverse = finish_hidden(got[:, 2 * rank : 3 * rank], sums, 6, column_sums, width)
    active, bent = gelu_and_slope(hidden)
    grad_hidden = (slope * bent).astype(BF16)
    payload[:, :rank] = to_all(gelu(hidden_f), peers)
    payload[:, rank : 2 * rank] = to_all(grad_hidden.astype(F32), peers)
    payload[:, 2 * rank : 3 * rank] = to_all(active, peers)
    payload[:, 3 * rank : 4 * rank] = to_all(active_back[...], peers)
    stats = back_stats(grad_hidden, hidden, mean, inverse, columns[peers : peers + 1, :], width)
    payload[:, 4 * rank :] = to_all(stats, peers)


def stash_kernel(evict, stash, arrived, partner1, stash_out, done):
    partner = lax.axis_size("section") - 1 - lax.axis_index("section")
    early, late = evict[0, partner], evict[1, partner]
    for i in range(stash.shape[1]):
        stash_out[0, i] = jnp.where(late == i, partner1[...], jnp.where(early == i, arrived[1], stash[0, i]))
    done[...] = jnp.zeros_like(done)


def last_kernel(
    kept_in, tokens_in, done, got, got0, upstream0, gain_term0, gain, down, up,
    up_grad_out, out_out, grad_out, gain_grad, down_grad_out, kept, tokens, up_grad, out, grad, down_grad,
    sems, up_sems, down_sems, *, rank
):
    rows = upstream0.shape[0]
    span = pl.ds(2 * rows, rows)
    loads = copies(
        [
            (kept_in.at[span], kept.at[span]),
            (tokens_in, tokens),
            (kept_in.at[pl.ds(0, 2 * rows)], kept.at[pl.ds(0, 2 * rows)]),
        ],
        sems,
    )
    product = jnp.dot(got[:, :rank], up[...], preferred_element_type=F32)
    loads[0].wait()
    upstream = kept[2 * rows : 3 * rows]
    up_grad[...] = transposed_times(
        jnp.concatenate([got[:, 3 * rank : 4 * rank], got[:, 2 * rank : 3 * rank]], axis=0),
        jnp.concatenate([upstream0[...], upstream], axis=0),
    ).astype(BF16)
    loads[1].wait()
    out[...] = (tokens[...].astype(F32) + product).astype(BF16)
    loads[2].wait()
    up_stores = copies(chunks(up_grad, up_grad_out, CHUNKS), up_sems)
    out_store = pltpu.make_async_copy(out, out_out, sems.at[3])
    out_store.start()
    grad[...], scaled, gain_term = backward(
        kept[:rows], upstream, got[:, rank : 2 * rank], got[:, 4 * rank :].astype(F32), gain[...].astype(F32), down[...]
    )
    grad_store = pltpu.make_async_copy(grad, grad_out, sems.at[4])
    grad_store.start()
    gain_grad[...] = gain_term0[...] + gain_term
    tokens_both = jnp.concatenate([kept[rows : 2 * rows], scaled], axis=0)
    hidden_both = jnp.concatenate([got0[:, rank : 2 * rank], got[:, rank : 2 * rank]], axis=0)
    down_stores = []
    step = down_grad.shape[0] // 2
    for i, (part, target) in enumerate(chunks(down_grad, down_grad_out, 2)):
        part[...] = transposed_times(tokens_both[:, i * step : (i + 1) * step], hidden_both).astype(BF16)
        for j, (source, place) in enumerate(chunks(part, target, CHUNKS // 2)):
            down_stores.append(pltpu.make_async_copy(source, place, down_sems.at[i * (CHUNKS // 2) + j]))
            down_stores[-1].start()
    for one in up_stores + down_stores + [out_store, grad_store]:
        one.wait()


def call(body, outs, operands, cost=1, smem=(), left=(), left_outs=(), scratch=(), aliases=(), name=None):
    spaces = [pltpu.SMEM if i in smem else pltpu.HBM if i in left else pltpu.VMEM for i in range(len(operands))]
    out_spaces = [pltpu.HBM if i in left_outs else pltpu.VMEM for i in range(len(outs))]
    return pl.pallas_call(
        body,
        out_shape=tuple(outs),
        in_specs=[pl.BlockSpec(memory_space=s) for s in spaces],
        out_specs=tuple(pl.BlockSpec(memory_space=s) for s in out_spaces),
        scratch_shapes=list(scratch),
        compiler_params=pltpu.CompilerParams(vmem_limit_bytes=16 * 2**20),
        cost_estimate=pl.CostEstimate(flops=cost * 2**31, bytes_accessed=cost * 2**20, transcendentals=0),
        input_output_aliases=dict(aliases),
        name=name,
    )(*operands)


def bound(body, **sizes):
    def run(*refs):
        body(*refs, **sizes)

    return run


def on_device(layer_input, fresh_input, out_grad, held_stash, norm_gain, down_proj, up_proj, fetch_slot, evict_slot):
    peers = lax.axis_size("dp")
    tokens0, grad0 = layer_input[0], out_grad[0]
    down, up = down_proj[0], up_proj[0]
    rows, features = tokens0.shape
    rank = up.shape[0]
    width = features * peers
    own = rows // peers

    def shape(*dims, dtype=BF16):
        return jax.ShapeDtypeStruct(dims, dtype)

    half = rank // 2
    tile = pltpu.VMEM((rows, features), BF16)
    sems = pltpu.SemaphoreType.DMA
    fetch, evict = fetch_slot.T, evict_slot.T

    picked, other = call(
        pick_kernel,
        [shape(rows, features), shape(rows, features)],
        [fetch, held_stash],
        smem=(0,),
        name="pick",
    )
    fetched0 = mirrored(picked)
    early, weight, column_sum, both = call(
        bound(start_kernel, peers=peers, rank=rank),
        [shape(rows, 2 * rank + half + LANES), shape(features, rank), shape(1, rank, dtype=F32), shape(2, rows, features)],
        [tokens0, grad0, norm_gain, down, up, other],
        name="start",
    )
    (payload,) = call(
        bound(fetched_kernel, rank=rank),
        [shape(rows, 3 * rank + half + LANES)],
        [fetched0, weight, column_sum, early],
        name="fetched",
    )
    got = across(payload)
    both = mirrored(both)
    payload, columns, active_back = call(
        bound(middle_kernel, peers=peers, rank=rank, width=width),
        [shape(rows, 2 * rank + LANES), shape(peers + 8, rank, dtype=F32), shape(own, rank, dtype=F32)],
        [got],
        left_outs=(1,),
        scratch=[pltpu.VMEM((peers + 8, rank), F32), sems((1,))],
        name="middle",
    )
    got0 = across(payload)
    other, kept = call(
        bound(other_kernel, rank=rank),
        [shape(rows, rank + LANES), shape(rank, features)],
        [fetch, evict, both, tokens0, weight, column_sum],
        smem=(0, 1),
        left_outs=(1,),
        scratch=[tile, sems((1,))],
        cost=LONG,
        name="other",
    )
    first_out, first_grad = call(
        bound(first_kernel, rank=rank),
        [shape(rows, features)] * 2,
        [got0, tokens0, fetched0, grad0, norm_gain, down, up, other],
        left=(7,),
        name="first",
    )
    before_out = shifted(first_out, 1)
    after_grad = shifted(first_grad, -1)
    kept, gain_term0 = call(
        bound(terms_kernel, rank=rank),
        [shape(rank, features), shape(1, features, dtype=F32)],
        [kept, got0, fetched0, grad0, norm_gain, down],
        left=(0,),
        left_outs=(0,),
        aliases=[(0, 0)],
        scratch=[tile, sems((1,))],
        cost=LONG,
        name="terms",
    )
    payload, kept, tokens1 = call(
        bound(second_kernel, rank=rank),
        [shape(rows, 3 * rank + LANES), shape(rank, features), shape(rows, features)],
        [kept, before_out, after_grad, fresh_input, first_out, weight, column_sum, up, other],
        left=(0,),
        left_outs=(1, 2),
        aliases=[(0, 1)],
        scratch=[tile, tile, sems((2,))],
        name="second",
    )
    got = across(payload)
    partner1 = mirrored(tokens1)
    (payload,) = call(
        bound(late_kernel, peers=peers, rank=rank, width=width),
        [shape(rows, 4 * rank + LANES)],
        [got, columns, active_back],
        name="late",
    )
    got1 = across(payload)
    stash, done = call(
        stash_kernel,
        [shape(*held_stash.shape), shape(8, LANES, dtype=F32)],
        [evict, held_stash, both, partner1],
        smem=(0,),
        cost=LONG,
        name="stash",
    )
    up_grad, next_output, input_grad, gain_grad, down_grad = call(
        bound(last_kernel, rank=rank),
        [
            shape(rank, features),
            shape(rows, features),
            shape(rows, features),
            shape(1, features, dtype=F32),
            shape(features, rank),
        ],
        [kept, tokens1, done, got1, got0, grad0, gain_term0, norm_gain, down, up],
        left=(0, 1, 2),
        left_outs=(0, 1, 2, 4),
        aliases=[(0, 0), (1, 1)],
        scratch=[
            pltpu.VMEM((3 * rows, features), BF16),
            tile,
            pltpu.VMEM((rank, features), BF16),
            tile,
            tile,
            pltpu.VMEM((features, rank), BF16),
            sems((5,)),
            sems((CHUNKS,)),
            sems((CHUNKS,)),
        ],
        name="last",
    )
    return (next_output[None], input_grad[None], stash, gain_grad, down_grad[None], up_grad[None])


def solution(mesh):
    placed = (
        P("section", None, "dp"),
        P(None, "dp"),
        P("section", None, "dp"),
        P("section", None, None, "dp"),
        P("section", "dp"),
        P("section", "dp", None),
        P("section", None, "dp"),
        P(),
        P(),
    )
    return jax.shard_map(
        on_device,
        mesh=mesh,
        in_specs=placed,
        out_specs=(
            P("section", None, "dp"),
            P("section", None, "dp"),
            P("section", None, None, "dp"),
            P("section", "dp"),
            P("section", "dp", None),
            P("section", None, "dp"),
        ),
        check_vma=False,
    )
```

```python
import math

import jax
import jax.numpy as jnp
from jax import lax
from jax.experimental import pallas as pl
from jax.experimental.pallas import tpu as pltpu
from jax.sharding import PartitionSpec as P

BF16 = jnp.bfloat16
F32 = jnp.float32
EPS = 1e-05
LANES = 128
LONG = 6
CHUNKS = 4
ROOT = math.sqrt(2 / math.pi)
CUBE = 0.044715


def across(block):
    return lax.all_to_all(block, "dp", 0, 0, tiled=True)


def mirrored(value):
    sections = lax.axis_size("section")
    return lax.ppermute(value, "section", [(i, sections - 1 - i) for i in range(sections)])


def shifted(value, by):
    sections = lax.axis_size("section")
    pairs = [(i, i + by) for i in range(sections) if 0 <= i + by < sections]
    return lax.ppermute(value, "section", pairs)


def pieces(value):
    high = value.astype(BF16).astype(F32)
    middle = (value - high).astype(BF16).astype(F32)
    return [high, middle, value - high - middle]


def in_lanes(columns):
    rows = columns[-1].shape[0]
    lane = lax.broadcasted_iota(jnp.int32, (rows, LANES), 1)
    block = jnp.zeros((rows, LANES), F32)
    for i, column in enumerate(columns):
        block = jnp.where(lane == i, column, block)
    return block


def from_lanes(block, first):
    lane = lax.broadcasted_iota(jnp.int32, block.shape, 1)
    return jnp.sum(jnp.where((lane >= first) & (lane < first + 3), block, 0.0), axis=1, keepdims=True)


def row_sums(values):
    one = jnp.sum(values, axis=1, keepdims=True)
    two = jnp.sum(values * values, axis=1, keepdims=True)
    return one, two


def hidden_part(tokens, weight, column_sum):
    values = tokens.astype(F32)
    one, two = row_sums(values)
    part = jnp.dot(tokens, weight, preferred_element_type=F32)
    return part - (one / values.shape[1]) * column_sum, pieces(one) + pieces(two)


def times_transposed(left, right):
    return lax.dot_general(left, right, (((1,), (1,)), ((), ())), preferred_element_type=F32)


def transposed_times(left, right):
    return lax.dot_general(left, right, (((0,), (0,)), ((), ())), preferred_element_type=F32)


def summed(block, peers):
    return jnp.sum(block.astype(F32).reshape(peers, -1, block.shape[1]), axis=0)


def finish_hidden(part, sums, first, column_sums, width):
    peers = len(column_sums)
    one = from_lanes(sums, first).reshape(peers, -1, 1)
    two = from_lanes(sums, first + 3).reshape(peers, -1, 1)
    mean = jnp.sum(one, axis=0) / width
    inverse = lax.rsqrt(jnp.sum(two, axis=0) / width - mean * mean + EPS)
    total = summed(part, peers)
    for peer in range(peers):
        total = total + (one[peer] / (width // peers) - mean) * column_sums[peer]
    return total * inverse, mean, inverse


def gelu(hidden):
    return hidden * (0.5 * (1.0 + jnp.tanh(ROOT * (hidden + CUBE * (hidden * hidden * hidden)))))


def gelu_and_slope(hidden):
    bent = jnp.tanh(ROOT * (hidden + CUBE * (hidden * hidden * hidden)))
    half = 0.5 * (1.0 + bent)
    slope = half + hidden * (0.5 * (1.0 - bent * bent)) * (ROOT * (1.0 + 3.0 * CUBE * (hidden * hidden)))
    return hidden * half, slope


def back_stats(grad_hidden, hidden, mean, inverse, column_exact, width):
    grad = grad_hidden.astype(F32)
    first = jnp.sum(grad * column_exact, axis=1, keepdims=True) / width
    second = jnp.sum(grad * hidden, axis=1, keepdims=True) / width
    return in_lanes(pieces(mean) + pieces(inverse) + pieces(first) + pieces(second))


def to_all(block, peers):
    rows, columns = block.shape
    return jnp.broadcast_to(block[None], (peers, rows, columns)).reshape(peers * rows, columns).astype(BF16)


def backward(tokens, upstream, grad_hidden, sums, gain, down_weight):
    mean, inverse, first, second = [from_lanes(sums, 3 * i) for i in range(4)]
    normed = (tokens.astype(F32) - mean) * inverse
    grad_scaled = times_transposed(grad_hidden, down_weight)
    grad_rows = inverse * (grad_scaled * gain - first - normed * second)
    tokens_grad = (upstream.astype(F32) + grad_rows).astype(BF16)
    gain_term = jnp.sum(grad_scaled * normed, axis=0, keepdims=True)
    return tokens_grad, (normed * gain).astype(BF16), gain_term


def copies(pairs, sems):
    started = [pltpu.make_async_copy(source, target, sems.at[i]) for i, (source, target) in enumerate(pairs)]
    for one in started:
        one.start()
    return started


def pick_kernel(fetch, stash, first, second):
    partner = lax.axis_size("section") - 1 - lax.axis_index("section")
    first[...] = stash[0, fetch[0, partner]]
    second[...] = stash[0, fetch[1, partner]]


def chunks(source, target, count):
    step = source.shape[0] // count
    return [(source.at[pl.ds(i * step, step)], target.at[pl.ds(i * step, step)]) for i in range(count)]


def scaled_weight(gain, down):
    features, rank = down.shape
    tall = jnp.broadcast_to(gain[...].astype(F32), (LANES, features)).T
    return down[...].astype(F32) * jnp.concatenate([tall] * (rank // LANES), axis=1)


def start_kernel(tokens, upstream, gain, down, up, other, payload, weight, column_sum, both, *, peers, rank):
    both[0] = other[...]
    both[1] = tokens[...]
    rows = tokens.shape[0]
    exact = scaled_weight(gain, down)
    rounded = exact.astype(BF16)
    weight[...] = rounded
    one = jnp.sum(rounded.astype(F32), axis=0, keepdims=True)
    column_sum[...] = one
    two = jnp.sum(exact, axis=0, keepdims=True)
    half = rank // 2
    row = lax.broadcasted_iota(jnp.int32, (rows // peers, half), 0)
    block = jnp.zeros((rows // peers, half), F32)
    for i, piece in enumerate(pieces(one)[:2] + pieces(two)[:2]):
        block = jnp.where(row == 2 * i, piece[:, :half], block)
        block = jnp.where(row == 2 * i + 1, piece[:, half:], block)
    part, sums = hidden_part(tokens[...], rounded, one)
    payload[:, :rank] = part.astype(BF16)
    payload[:, rank : 2 * rank] = times_transposed(upstream[...], up[...]).astype(BF16)
    payload[:, 2 * rank : 2 * rank + half] = to_all(block, peers)
    payload[:, 2 * rank + half :] = in_lanes(sums).astype(BF16)


def fetched_kernel(tokens, weight, column_sum, early, payload, *, rank):
    part, sums = hidden_part(tokens[...], weight[...], column_sum[...])
    block = early.shape[1] - LANES
    payload[:, :block] = early[:, :block]
    payload[:, block : block + rank] = part.astype(BF16)
    payload[:, block + rank :] = (early[:, block:].astype(F32) + in_lanes([0.0] * 6 + sums)).astype(BF16)


def middle_kernel(got, payload, columns_out, active_back, columns, sems, *, peers, rank, width):
    half = rank // 2
    blocks = got[:, 2 * rank : 2 * rank + half].astype(F32).reshape(peers, -1, half)
    row = lax.broadcasted_iota(jnp.int32, blocks.shape[1:], 0)

    def joined(block, first):
        left = jnp.sum(jnp.where((row == first) | (row == first + 2), block, 0.0), axis=0, keepdims=True)
        right = jnp.sum(jnp.where((row == first + 1) | (row == first + 3), block, 0.0), axis=0, keepdims=True)
        return jnp.concatenate([left, right], axis=1)

    column_sums = []
    for peer in range(peers):
        column_sums.append(joined(blocks[peer], 0))
        columns[peer : peer + 1, :] = column_sums[peer]
    column_exact = joined(jnp.sum(blocks, axis=0), 4)
    columns[peers : peers + 1, :] = column_exact
    columns[peers + 1 :, :] = jnp.zeros((7, rank), F32)
    (saved,) = copies([(columns, columns_out)], sems)
    sums = got[:, 3 * rank + half :].astype(F32)
    hidden_f = finish_hidden(got[:, :rank], sums, 0, column_sums, width)[0]
    slope = summed(got[:, rank : 2 * rank], peers)
    hidden, mean, inverse = finish_hidden(
        got[:, 2 * rank + half : 3 * rank + half], sums, 6, column_sums, width
    )
    active, bent = gelu_and_slope(hidden)
    active_back[...] = active
    grad_hidden = (slope * bent).astype(BF16)
    payload[:, :rank] = to_all(gelu(hidden_f), peers)
    payload[:, rank : 2 * rank] = to_all(grad_hidden.astype(F32), peers)
    payload[:, 2 * rank :] = to_all(back_stats(grad_hidden, hidden, mean, inverse, column_exact, width), peers)
    saved.wait()


def first_kernel(got, tokens, fetched, upstream, gain, down, up, after, out, grad, *, rank):
    out[...] = (
        tokens[...].astype(F32) + jnp.dot(got[:, :rank], up[...], preferred_element_type=F32)
    ).astype(BF16)
    grad[...] = backward(
        fetched[...], upstream[...], got[:, rank : 2 * rank], got[:, 2 * rank :].astype(F32), gain[...].astype(F32), down[...]
    )[0]


def other_kernel(fetch, evict, arrived, tokens, weight, column_sum, part, sums, kept, chosen, sems):
    place = lax.axis_index("section")
    chosen[...] = jnp.where(fetch[1, place] == evict[0, place], tokens[...], arrived[0])
    (saved,) = copies([(chosen, kept.at[pl.ds(0, tokens.shape[0])])], sems)
    part[...], columns = hidden_part(chosen[...], weight[...], column_sum[...])
    sums[...] = in_lanes(columns)
    saved.wait()


def terms_kernel(
    kept_in, got, fetched, upstream, gain, down, part, sums, active_back, after, payload, kept, gain_term, scaled, sems,
    *, peers, rank
):
    scaled[...], gain_term[...] = backward(
        fetched[...], upstream[...], got[:, rank : 2 * rank], got[:, 2 * rank :].astype(F32), gain[...].astype(F32), down[...]
    )[1:]
    rows = scaled.shape[0]
    saved = copies([(scaled, kept.at[pl.ds(rows, rows)]), (upstream, kept.at[pl.ds(3 * rows, rows)])], sems)
    payload[:, :rank] = part[...].astype(BF16)
    payload[:, rank : 2 * rank] = to_all(active_back[...], peers)
    payload[:, 2 * rank :] = sums[...].astype(BF16)
    for one in saved:
        one.wait()


def second_kernel(
    kept_in, before, after, fresh, own, gain, down, column_sum, up, prior, payload, kept, tokens_out, tokens, upstream, sems,
    *, rank
):
    place = lax.axis_index("section")
    rows = before.shape[0]
    tokens[...] = jnp.where(place == 0, fresh[...], before[...])
    first = pltpu.make_async_copy(tokens, tokens_out, sems.at[0])
    first.start()
    upstream[...] = jnp.where(place == lax.axis_size("section") - 1, own[...], after[...])
    second = pltpu.make_async_copy(upstream, kept.at[pl.ds(2 * rows, rows)], sems.at[1])
    second.start()
    payload[:, rank : 2 * rank] = times_transposed(upstream[...], up[...]).astype(BF16)
    part, sums = hidden_part(tokens[...], scaled_weight(gain, down).astype(BF16), column_sum[...])
    payload[:, :rank] = part.astype(BF16)
    payload[:, 2 * rank :] = in_lanes(sums).astype(BF16)
    first.wait()
    second.wait()


def late_kernel(got, side, columns, payload, *, peers, rank, width):
    column_sums = [columns[peer : peer + 1, :] for peer in range(peers)]
    hidden_f = finish_hidden(got[:, :rank], got[:, 2 * rank :].astype(F32), 0, column_sums, width)[0]
    slope = summed(got[:, rank : 2 * rank], peers)
    hidden, mean, inverse = finish_hidden(side[:, :rank], side[:, 2 * rank :].astype(F32), 0, column_sums, width)
    active, bent = gelu_and_slope(hidden)
    grad_hidden = (slope * bent).astype(BF16)
    payload[:, :rank] = to_all(gelu(hidden_f), peers)
    payload[:, rank : 2 * rank] = to_all(grad_hidden.astype(F32), peers)
    payload[:, 2 * rank : 3 * rank] = to_all(active, peers)
    stats = back_stats(grad_hidden, hidden, mean, inverse, columns[peers : peers + 1, :], width)
    payload[:, 3 * rank :] = to_all(stats, peers)


def stash_kernel(evict, stash, arrived, partner1, stash_out, done):
    partner = lax.axis_size("section") - 1 - lax.axis_index("section")
    early, late = evict[0, partner], evict[1, partner]
    for i in range(stash.shape[1]):
        stash_out[0, i] = jnp.where(late == i, partner1[...], jnp.where(early == i, arrived[1], stash[0, i]))
    done[...] = jnp.zeros_like(done)


def last_kernel(
    kept_in, tokens_in, done, got, side, got0, gain_term0, gain, down, up,
    up_grad_out, out_out, grad_out, gain_grad, down_grad_out, kept, tokens, up_grad, out, grad, down_grad,
    sems, up_sems, down_sems, *, rank
):
    rows = tokens.shape[0]
    span = pl.ds(2 * rows, 2 * rows)
    loads = copies(
        [
            (kept_in.at[span], kept.at[span]),
            (tokens_in, tokens),
            (kept_in.at[pl.ds(0, 2 * rows)], kept.at[pl.ds(0, 2 * rows)]),
        ],
        sems,
    )
    product = jnp.dot(got[:, :rank], up[...], preferred_element_type=F32)
    loads[0].wait()
    upstream = kept[2 * rows : 3 * rows]
    upstream0 = kept[3 * rows :]
    up_grad[...] = transposed_times(
        jnp.concatenate([side[:, rank : 2 * rank], got[:, 2 * rank : 3 * rank]], axis=0),
        jnp.concatenate([upstream0, upstream], axis=0),
    ).astype(BF16)
    loads[1].wait()
    out[...] = (tokens[...].astype(F32) + product).astype(BF16)
    loads[2].wait()
    up_stores = copies(chunks(up_grad, up_grad_out, CHUNKS), up_sems)
    out_store = pltpu.make_async_copy(out, out_out, sems.at[3])
    out_store.start()
    grad[...], scaled, gain_term = backward(
        kept[:rows], upstream, got[:, rank : 2 * rank], got[:, 3 * rank :].astype(F32), gain[...].astype(F32), down[...]
    )
    grad_store = pltpu.make_async_copy(grad, grad_out, sems.at[4])
    grad_store.start()
    gain_grad[...] = gain_term0[...] + gain_term
    tokens_both = jnp.concatenate([kept[rows : 2 * rows], scaled], axis=0)
    hidden_both = jnp.concatenate([got0[:, rank : 2 * rank], got[:, rank : 2 * rank]], axis=0)
    down_stores = []
    step = down_grad.shape[0] // 2
    for i, (part, target) in enumerate(chunks(down_grad, down_grad_out, 2)):
        part[...] = transposed_times(tokens_both[:, i * step : (i + 1) * step], hidden_both).astype(BF16)
        for j, (source, place) in enumerate(chunks(part, target, CHUNKS // 2)):
            down_stores.append(pltpu.make_async_copy(source, place, down_sems.at[i * (CHUNKS // 2) + j]))
            down_stores[-1].start()
    for one in up_stores + down_stores + [out_store, grad_store]:
        one.wait()


def call(body, outs, operands, cost=1, smem=(), left=(), left_outs=(), scratch=(), aliases=(), name=None):
    spaces = [pltpu.SMEM if i in smem else pltpu.HBM if i in left else pltpu.VMEM for i in range(len(operands))]
    out_spaces = [pltpu.HBM if i in left_outs else pltpu.VMEM for i in range(len(outs))]
    return pl.pallas_call(
        body,
        out_shape=tuple(outs),
        in_specs=[pl.BlockSpec(memory_space=s) for s in spaces],
        out_specs=tuple(pl.BlockSpec(memory_space=s) for s in out_spaces),
        scratch_shapes=list(scratch),
        compiler_params=pltpu.CompilerParams(vmem_limit_bytes=16 * 2**20),
        cost_estimate=pl.CostEstimate(flops=cost * 2**31, bytes_accessed=cost * 2**20, transcendentals=0),
        input_output_aliases=dict(aliases),
        name=name,
    )(*operands)


def bound(body, **sizes):
    def run(*refs):
        body(*refs, **sizes)

    return run


def on_device(layer_input, fresh_input, out_grad, held_stash, norm_gain, down_proj, up_proj, fetch_slot, evict_slot):
    peers = lax.axis_size("dp")
    tokens0, grad0 = layer_input[0], out_grad[0]
    down, up = down_proj[0], up_proj[0]
    rows, features = tokens0.shape
    rank = up.shape[0]
    width = features * peers
    own = rows // peers

    def shape(*dims, dtype=BF16):
        return jax.ShapeDtypeStruct(dims, dtype)

    half = rank // 2
    tile = pltpu.VMEM((rows, features), BF16)
    sems = pltpu.SemaphoreType.DMA
    fetch, evict = fetch_slot.T, evict_slot.T

    picked, other = call(
        pick_kernel,
        [shape(rows, features), shape(rows, features)],
        [fetch, held_stash],
        smem=(0,),
        name="pick",
    )
    fetched0 = mirrored(picked)
    early, weight, column_sum, both = call(
        bound(start_kernel, peers=peers, rank=rank),
        [shape(rows, 2 * rank + half + LANES), shape(features, rank), shape(1, rank, dtype=F32), shape(2, rows, features)],
        [tokens0, grad0, norm_gain, down, up, other],
        name="start",
    )
    (payload,) = call(
        bound(fetched_kernel, rank=rank),
        [shape(rows, 3 * rank + half + LANES)],
        [fetched0, weight, column_sum, early],
        name="fetched",
    )
    got = across(payload)
    both = mirrored(both)
    payload, columns, active_back = call(
        bound(middle_kernel, peers=peers, rank=rank, width=width),
        [shape(rows, 2 * rank + LANES), shape(peers + 8, rank, dtype=F32), shape(own, rank, dtype=F32)],
        [got],
        left_outs=(1,),
        scratch=[pltpu.VMEM((peers + 8, rank), F32), sems((1,))],
        name="middle",
    )
    got0 = across(payload)
    part1, sums1, kept = call(
        other_kernel,
        [shape(rows, rank, dtype=F32), shape(rows, LANES, dtype=F32), shape(rank, features)],
        [fetch, evict, both, tokens0, weight, column_sum],
        smem=(0, 1),
        left_outs=(2,),
        scratch=[tile, sems((1,))],
        cost=LONG,
        name="other",
    )
    first_out, first_grad = call(
        bound(first_kernel, rank=rank),
        [shape(rows, features)] * 2,
        [got0, tokens0, fetched0, grad0, norm_gain, down, up, sums1],
        left=(7,),
        name="first",
    )
    before_out = shifted(first_out, 1)
    after_grad = shifted(first_grad, -1)
    payload, kept, gain_term0 = call(
        bound(terms_kernel, peers=peers, rank=rank),
        [shape(rows, 2 * rank + LANES), shape(rank, features), shape(1, features, dtype=F32)],
        [kept, got0, fetched0, grad0, norm_gain, down, part1, sums1, active_back, first_grad],
        left=(0, 9),
        left_outs=(1,),
        aliases=[(0, 1)],
        scratch=[tile, sems((2,))],
        cost=LONG,
        name="terms",
    )
    side = across(payload)
    payload, kept, tokens1 = call(
        bound(second_kernel, rank=rank),
        [shape(rows, 2 * rank + LANES), shape(rank, features), shape(rows, features)],
        [kept, before_out, after_grad, fresh_input, first_out, norm_gain, down, column_sum, up, gain_term0],
        left=(0, 9),
        left_outs=(1, 2),
        aliases=[(0, 1)],
        scratch=[tile, tile, sems((2,))],
        cost=2,
        name="second",
    )
    got = across(payload)
    partner1 = mirrored(tokens1)
    (payload,) = call(
        bound(late_kernel, peers=peers, rank=rank, width=width),
        [shape(rows, 3 * rank + LANES)],
        [got, side, columns],
        name="late",
    )
    got1 = across(payload)
    stash, done = call(
        stash_kernel,
        [shape(*held_stash.shape), shape(8, LANES, dtype=F32)],
        [evict, held_stash, both, partner1],
        smem=(0,),
        cost=LONG,
        name="stash",
    )
    up_grad, next_output, input_grad, gain_grad, down_grad = call(
        bound(last_kernel, rank=rank),
        [
            shape(rank, features),
            shape(rows, features),
            shape(rows, features),
            shape(1, features, dtype=F32),
            shape(features, rank),
        ],
        [kept, tokens1, done, got1, side, got0, gain_term0, norm_gain, down, up],
        left=(0, 1, 2),
        left_outs=(0, 1, 2, 4),
        aliases=[(0, 0), (1, 1)],
        scratch=[
            pltpu.VMEM((4 * rows, features), BF16),
            tile,
            pltpu.VMEM((rank, features), BF16),
            tile,
            tile,
            pltpu.VMEM((features, rank), BF16),
            sems((5,)),
            sems((CHUNKS,)),
            sems((CHUNKS,)),
        ],
        name="last",
    )
    return (next_output[None], input_grad[None], stash, gain_grad, down_grad[None], up_grad[None])


def solution(mesh):
    placed = (
        P("section", None, "dp"),
        P(None, "dp"),
        P("section", None, "dp"),
        P("section", None, None, "dp"),
        P("section", "dp"),
        P("section", "dp", None),
        P("section", None, "dp"),
        P(),
        P(),
    )
    return jax.shard_map(
        on_device,
        mesh=mesh,
        in_specs=placed,
        out_specs=(
            P("section", None, "dp"),
            P("section", None, "dp"),
            P("section", None, None, "dp"),
            P("section", "dp"),
            P("section", "dp", None),
            P("section", None, "dp"),
        ),
        check_vma=False,
    )
```

```python
import math

import jax
import jax.numpy as jnp
from jax import lax
from jax.experimental import pallas as pl
from jax.experimental.pallas import tpu as pltpu
from jax.sharding import PartitionSpec as P

BF16 = jnp.bfloat16
F32 = jnp.float32
EPS = 1e-05
LANES = 128
LONG = 6
CHUNKS = 4
ROOT = math.sqrt(2 / math.pi)
CUBE = 0.044715


def across(block):
    return lax.all_to_all(block, "dp", 0, 0, tiled=True)


def mirrored(value):
    sections = lax.axis_size("section")
    return lax.ppermute(value, "section", [(i, sections - 1 - i) for i in range(sections)])


def swapped(value, first):
    sections = lax.axis_size("section")
    pairs = [(i, i + 1) for i in range(first, sections - 1, 2)]
    alone = [(sections - 1, sections - 1)] if (sections - first) % 2 else []
    return lax.ppermute(value, "section", pairs + [(j, i) for i, j in pairs] + alone)


def pieces(value):
    high = value.astype(BF16).astype(F32)
    middle = (value - high).astype(BF16).astype(F32)
    return [high, middle, value - high - middle]


def in_lanes(columns):
    rows = columns[-1].shape[0]
    lane = lax.broadcasted_iota(jnp.int32, (rows, LANES), 1)
    block = jnp.zeros((rows, LANES), F32)
    for i, column in enumerate(columns):
        block = jnp.where(lane == i, column, block)
    return block


def from_lanes(block, first):
    lane = lax.broadcasted_iota(jnp.int32, block.shape, 1)
    return jnp.sum(jnp.where((lane >= first) & (lane < first + 3), block, 0.0), axis=1, keepdims=True)


def row_sums(values):
    one = jnp.sum(values, axis=1, keepdims=True)
    two = jnp.sum(values * values, axis=1, keepdims=True)
    return one, two


def hidden_part(tokens, weight, column_sum):
    values = tokens.astype(F32)
    one, two = row_sums(values)
    part = jnp.dot(tokens, weight, preferred_element_type=F32)
    return part - (one / values.shape[1]) * column_sum, pieces(one) + pieces(two)


def times_transposed(left, right):
    return lax.dot_general(left, right, (((1,), (1,)), ((), ())), preferred_element_type=F32)


def transposed_times(left, right):
    return lax.dot_general(left, right, (((0,), (0,)), ((), ())), preferred_element_type=F32)


def summed(block, peers):
    return jnp.sum(block.astype(F32).reshape(peers, -1, block.shape[1]), axis=0)


def finish_hidden(part, sums, first, column_sums, width):
    peers = len(column_sums)
    one = from_lanes(sums, first).reshape(peers, -1, 1)
    two = from_lanes(sums, first + 3).reshape(peers, -1, 1)
    mean = jnp.sum(one, axis=0) / width
    inverse = lax.rsqrt(jnp.sum(two, axis=0) / width - mean * mean + EPS)
    total = summed(part, peers)
    for peer in range(peers):
        total = total + (one[peer] / (width // peers) - mean) * column_sums[peer]
    return total * inverse, mean, inverse


def gelu(hidden):
    return hidden * (0.5 * (1.0 + jnp.tanh(ROOT * (hidden + CUBE * (hidden * hidden * hidden)))))


def gelu_and_slope(hidden):
    bent = jnp.tanh(ROOT * (hidden + CUBE * (hidden * hidden * hidden)))
    half = 0.5 * (1.0 + bent)
    slope = half + hidden * (0.5 * (1.0 - bent * bent)) * (ROOT * (1.0 + 3.0 * CUBE * (hidden * hidden)))
    return hidden * half, slope


def back_stats(grad_hidden, hidden, mean, inverse, column_exact, width):
    grad = grad_hidden.astype(F32)
    first = jnp.sum(grad * column_exact, axis=1, keepdims=True) / width
    second = jnp.sum(grad * hidden, axis=1, keepdims=True) / width
    return in_lanes(pieces(mean) + pieces(inverse) + pieces(first) + pieces(second))


def to_all(block, peers):
    rows, columns = block.shape
    return jnp.broadcast_to(block[None], (peers, rows, columns)).reshape(peers * rows, columns).astype(BF16)


def backward(tokens, upstream, grad_hidden, sums, gain, down_weight):
    mean, inverse, first, second = [from_lanes(sums, 3 * i) for i in range(4)]
    normed = (tokens.astype(F32) - mean) * inverse
    grad_scaled = times_transposed(grad_hidden, down_weight)
    grad_rows = inverse * (grad_scaled * gain - first - normed * second)
    tokens_grad = (upstream.astype(F32) + grad_rows).astype(BF16)
    gain_term = jnp.sum(grad_scaled * normed, axis=0, keepdims=True)
    return tokens_grad, (normed * gain).astype(BF16), gain_term


def copies(pairs, sems):
    started = [pltpu.make_async_copy(source, target, sems.at[i]) for i, (source, target) in enumerate(pairs)]
    for one in started:
        one.start()
    return started


def pick_kernel(fetch, stash, first, second):
    partner = lax.axis_size("section") - 1 - lax.axis_index("section")
    first[...] = stash[0, fetch[0, partner]]
    second[...] = stash[0, fetch[1, partner]]


def chunks(source, target, count):
    step = source.shape[0] // count
    return [(source.at[pl.ds(i * step, step)], target.at[pl.ds(i * step, step)]) for i in range(count)]


def scaled_weight(gain, down):
    features, rank = down.shape
    tall = jnp.broadcast_to(gain[...].astype(F32), (LANES, features)).T
    return down[...].astype(F32) * jnp.concatenate([tall] * (rank // LANES), axis=1)


def start_kernel(
    tokens, upstream, gain, down, up, other, payload, weight, column_sum, sums, both, parts, sems, *, peers, rank
):
    both[0] = other[...]
    both[1] = tokens[...]
    rows = tokens.shape[0]
    parts[:, rank : 2 * rank] = times_transposed(upstream[...], up[...]).astype(BF16)
    exact = scaled_weight(gain, down)
    rounded = exact.astype(BF16)
    weight[...] = rounded
    one = jnp.sum(rounded.astype(F32), axis=0, keepdims=True)
    column_sum[...] = one
    row = lax.broadcasted_iota(jnp.int32, (rows // peers, LANES), 0)
    block = jnp.zeros((rows // peers, LANES), F32)
    quarters = rank // LANES
    for i, piece in enumerate(pieces(jnp.sum(exact, axis=0, keepdims=True))[:2]):
        for j in range(quarters):
            block = jnp.where(row == i * quarters + j, piece[:, j * LANES : (j + 1) * LANES], block)
    parts[:, 2 * rank :] = to_all(block, peers)
    part, columns = hidden_part(tokens[...], rounded, one)
    sums[...] = in_lanes(columns)
    parts[:, :rank] = part.astype(BF16)
    (saved,) = copies([(parts, payload.at[:, pl.ds(0, 2 * rank + LANES)])], sems)
    saved.wait()


def fetched_kernel(early, tokens, weight, column_sum, sums0, payload, parts, sums, sems, *, rank):
    first = 2 * rank + LANES
    part, columns = hidden_part(tokens[...], weight[...], column_sum[...])
    parts[...] = part.astype(BF16)
    sums[...] = (sums0[...] + in_lanes([0.0] * 6 + columns)).astype(BF16)
    for one in copies(
        [
            (parts, payload.at[:, pl.ds(first, rank)]),
            (sums, payload.at[:, pl.ds(first + rank, LANES)]),
        ],
        sems,
    ):
        one.wait()


def middle_kernel(got, payload, columns_out, active_back, columns, sems, *, peers, rank, width):
    first = 2 * rank + LANES
    blocks = got[:, 2 * rank : first].astype(F32).reshape(peers, -1, LANES)
    row = lax.broadcasted_iota(jnp.int32, blocks.shape[1:], 0)
    quarters = rank // LANES

    def joined(block):
        return jnp.concatenate(
            [
                jnp.sum(jnp.where((row == i) | (row == quarters + i), block, 0.0), axis=0, keepdims=True)
                for i in range(quarters)
            ],
            axis=1,
        )

    column_sums = []
    for peer in range(peers):
        column_sums.append(joined(blocks[peer]))
        columns[peer : peer + 1, :] = column_sums[peer]
    column_exact = joined(jnp.sum(blocks, axis=0))
    columns[peers : peers + 1, :] = column_exact
    columns[peers + 1 :, :] = jnp.zeros((7, rank), F32)
    (saved,) = copies([(columns, columns_out)], sems)
    sums = got[:, first + rank :].astype(F32)
    hidden_f = finish_hidden(got[:, :rank], sums, 0, column_sums, width)[0]
    slope = summed(got[:, rank : 2 * rank], peers)
    hidden, mean, inverse = finish_hidden(
        got[:, first : first + rank], sums, 6, column_sums, width
    )
    active, bent = gelu_and_slope(hidden)
    active_back[...] = active
    grad_hidden = (slope * bent).astype(BF16)
    payload[:, :rank] = to_all(gelu(hidden_f), peers)
    payload[:, rank : 2 * rank] = to_all(grad_hidden.astype(F32), peers)
    payload[:, 2 * rank :] = to_all(back_stats(grad_hidden, hidden, mean, inverse, column_exact, width), peers)
    saved.wait()


def first_kernel(got, tokens, fetched, upstream, gain, down, up, after, beside_out, across_out, *, rank):
    out = (tokens[...].astype(F32) + jnp.dot(got[:, :rank], up[...], preferred_element_type=F32)).astype(BF16)
    grad = backward(
        fetched[...], upstream[...], got[:, rank : 2 * rank], got[:, 2 * rank :].astype(F32), gain[...].astype(F32), down[...]
    )[0]
    odd = lax.rem(lax.axis_index("section"), 2) == 1
    across_out[...] = jnp.where(odd, out, grad)
    beside_out[...] = jnp.where(odd, grad, out)


def other_kernel(
    fetch, evict, arrived, tokens, weight, column_sum, payload, kept, chosen, sems, *, rank
):
    place = lax.axis_index("section")
    chosen[...] = jnp.where(fetch[1, place] == evict[0, place], tokens[...], arrived[0])
    (saved,) = copies([(chosen, kept.at[pl.ds(0, tokens.shape[0])])], sems)
    part, sums = hidden_part(chosen[...], weight[...], column_sum[...])
    payload[:, :rank] = part.astype(BF16)
    payload[:, rank:] = in_lanes([0.0] * 6 + sums).astype(BF16)
    saved.wait()


def terms_kernel(
    kept_in, got, fetched, upstream, gain, down, active_back, kept, gain_term, payload, scaled, active, sems, *, peers, rank
):
    active[...] = to_all(active_back[...], peers)
    (ready,) = copies([(active, payload.at[:, pl.ds(3 * rank, rank)])], sems.at[pl.ds(1, 1)])
    scaled[...], gain_term[...] = backward(
        fetched[...], upstream[...], got[:, rank : 2 * rank], got[:, 2 * rank :].astype(F32), gain[...].astype(F32), down[...]
    )[1:]
    rows = scaled.shape[0]
    (saved,) = copies([(scaled, kept.at[pl.ds(rows, rows)])], sems)
    saved.wait()
    ready.wait()


def second_kernel(
    kept_in, beside_in, across_in, fresh, still, weight, column_sum, up, side, payload, kept, tokens_out, tokens, upstream, parts, sems,
    *, rank
):
    place = lax.axis_index("section")
    odd = lax.rem(place, 2) == 1
    rows = fresh.shape[0]
    tokens[...] = jnp.where(place == 0, fresh[...], jnp.where(odd, beside_in[...], across_in[...]))
    first = pltpu.make_async_copy(tokens, tokens_out, sems.at[0])
    first.start()
    upstream[...] = jnp.where(odd, across_in[...], beside_in[...])
    second = pltpu.make_async_copy(upstream, kept.at[pl.ds(2 * rows, rows)], sems.at[1])
    second.start()
    parts[:, 2 * rank : 3 * rank] = side[:, :rank]
    parts[:, rank : 2 * rank] = times_transposed(upstream[...], up[...]).astype(BF16)
    span = pl.ds(rank, 2 * rank)
    third = pltpu.make_async_copy(parts.at[:, span], payload.at[:, span], sems.at[2])
    third.start()
    part, sums = hidden_part(tokens[...], weight[...], column_sum[...])
    parts[:, :rank] = part.astype(BF16)
    span = pl.ds(0, rank)
    fourth = pltpu.make_async_copy(parts.at[:, span], payload.at[:, span], sems.at[3])
    fourth.start()
    parts[:, 3 * rank :] = (side[:, rank:].astype(F32) + in_lanes(sums)).astype(BF16)
    span = pl.ds(3 * rank, LANES)
    fifth = pltpu.make_async_copy(parts.at[:, span], payload.at[:, span], sems.at[4])
    fifth.start()
    for one in (first, second, third, fourth, fifth):
        one.wait()


def late_kernel(filled, got, columns, payload, parts, last, sems, *, peers, rank, width):
    column_sums = [columns[peer : peer + 1, :] for peer in range(peers)]
    sums = got[:, 3 * rank :].astype(F32)
    stores = []

    def store(source, first, lanes):
        stores.append(pltpu.make_async_copy(source, payload.at[:, pl.ds(first, lanes)], sems.at[len(stores)]))
        stores[-1].start()

    hidden, mean, inverse = finish_hidden(got[:, 2 * rank : 3 * rank], sums, 6, column_sums, width)
    active, bent = gelu_and_slope(hidden)
    parts[0] = to_all(active, peers)
    store(parts.at[0], 2 * rank, rank)
    slope = summed(got[:, rank : 2 * rank], peers)
    grad_hidden = (slope * bent).astype(BF16)
    parts[1] = to_all(grad_hidden.astype(F32), peers)
    store(parts.at[1], rank, rank)
    last[...] = to_all(
        back_stats(grad_hidden, hidden, mean, inverse, columns[peers : peers + 1, :], width), peers
    )
    store(last, 4 * rank, LANES)
    hidden_f = finish_hidden(got[:, :rank], sums, 0, column_sums, width)[0]
    parts[2] = to_all(gelu(hidden_f), peers)
    store(parts.at[2], 0, rank)
    for one in stores:
        one.wait()


def stash_kernel(evict, stash, arrived, partner1, stash_out, done):
    partner = lax.axis_size("section") - 1 - lax.axis_index("section")
    early, late = evict[0, partner], evict[1, partner]
    for i in range(stash.shape[1]):
        stash_out[0, i] = jnp.where(late == i, partner1[...], jnp.where(early == i, arrived[1], stash[0, i]))
    done[...] = jnp.zeros_like(done)


def last_kernel(
    kept_in, tokens_in, done, got, got0, upstream0_in, gain_term0, gain, down, up,
    up_grad_out, out_out, grad_out, gain_grad, down_grad_out, tiles, up_grad, out, grad, down_grad,
    load_sems, sems, up_sems, down_sems, *, rank
):
    rows = tokens_in.shape[0]
    loads = copies(
        [
            (kept_in.at[pl.ds(2 * rows, rows)], tiles.at[0]),
            (tokens_in, tiles.at[1]),
            (kept_in.at[pl.ds(0, rows)], tiles.at[2]),
            (kept_in.at[pl.ds(rows, rows)], tiles.at[3]),
        ],
        load_sems,
    )
    grad_hidden = got[:, rank : 2 * rank]
    product = jnp.dot(got[:, :rank], up[...], preferred_element_type=F32)
    grad_scaled = times_transposed(grad_hidden, down[...])
    sums = got[:, 4 * rank :].astype(F32)
    mean, inverse, first, second = [from_lanes(sums, 3 * i) for i in range(4)]
    grad_normed = grad_scaled * gain[...].astype(F32)
    active_both = jnp.concatenate([got[:, 3 * rank : 4 * rank], got[:, 2 * rank : 3 * rank]], axis=0)
    hidden_both = jnp.concatenate([got0[:, rank : 2 * rank], grad_hidden], axis=0)
    stores = []

    def store(source, target, sem):
        stores.append(pltpu.make_async_copy(source, target, sem))
        stores[-1].start()

    loads[0].wait()
    upstream = tiles[0]
    upstream_both = jnp.concatenate([upstream0_in[...], upstream], axis=0)
    step = rank // CHUNKS
    for i, (part, target) in enumerate(chunks(up_grad, up_grad_out, CHUNKS)):
        part[...] = transposed_times(active_both[:, i * step : (i + 1) * step], upstream_both).astype(BF16)
        if i == 0:
            loads[1].wait()
            loads[2].wait()
            loads[3].wait()
        store(part, target, up_sems.at[i])
    out[...] = (tiles[1].astype(F32) + product).astype(BF16)
    store(out, out_out, sems.at[0])
    normed = (tiles[2].astype(F32) - mean) * inverse
    grad[...] = (upstream.astype(F32) + inverse * (grad_normed - first - normed * second)).astype(BF16)
    store(grad, grad_out, sems.at[1])
    gain_grad[...] = gain_term0[...] + jnp.sum(grad_scaled * normed, axis=0, keepdims=True)
    scaled_both = jnp.concatenate([tiles[3], (normed * gain[...].astype(F32)).astype(BF16)], axis=0)
    step = down_grad.shape[0] // CHUNKS
    for i, (part, target) in enumerate(chunks(down_grad, down_grad_out, CHUNKS)):
        part[...] = transposed_times(scaled_both[:, i * step : (i + 1) * step], hidden_both).astype(BF16)
        store(part, target, down_sems.at[i])
    for one in stores:
        one.wait()


def call(body, outs, operands, cost=1, smem=(), left=(), left_outs=(), scratch=(), aliases=(), name=None):
    spaces = [pltpu.SMEM if i in smem else pltpu.HBM if i in left else pltpu.VMEM for i in range(len(operands))]
    out_spaces = [pltpu.HBM if i in left_outs else pltpu.VMEM for i in range(len(outs))]
    return pl.pallas_call(
        body,
        out_shape=tuple(outs),
        in_specs=[pl.BlockSpec(memory_space=s) for s in spaces],
        out_specs=tuple(pl.BlockSpec(memory_space=s) for s in out_spaces),
        scratch_shapes=list(scratch),
        compiler_params=pltpu.CompilerParams(vmem_limit_bytes=16 * 2**20),
        cost_estimate=pl.CostEstimate(flops=cost * 2**31, bytes_accessed=cost * 2**20, transcendentals=0),
        input_output_aliases=dict(aliases),
        name=name,
    )(*operands)


def bound(body, **sizes):
    def run(*refs):
        body(*refs, **sizes)

    return run


def on_device(layer_input, fresh_input, out_grad, held_stash, norm_gain, down_proj, up_proj, fetch_slot, evict_slot):
    peers = lax.axis_size("dp")
    tokens0, grad0 = layer_input[0], out_grad[0]
    down, up = down_proj[0], up_proj[0]
    rows, features = tokens0.shape
    rank = up.shape[0]
    width = features * peers
    own = rows // peers

    def shape(*dims, dtype=BF16):
        return jax.ShapeDtypeStruct(dims, dtype)

    tile = pltpu.VMEM((rows, features), BF16)
    sems = pltpu.SemaphoreType.DMA
    fetch, evict = fetch_slot.T, evict_slot.T

    picked, other = call(
        pick_kernel,
        [shape(rows, features), shape(rows, features)],
        [fetch, held_stash],
        smem=(0,),
        name="pick",
    )
    fetched0 = mirrored(picked)
    early, weight, column_sum, sums0, both = call(
        bound(start_kernel, peers=peers, rank=rank),
        [
            shape(rows, 3 * rank + 2 * LANES),
            shape(features, rank),
            shape(1, rank, dtype=F32),
            shape(rows, LANES, dtype=F32),
            shape(2, rows, features),
        ],
        [tokens0, grad0, norm_gain, down, up, other],
        left_outs=(0,),
        scratch=[pltpu.VMEM((rows, 2 * rank + LANES), BF16), sems((1,))],
        name="start",
    )
    (payload,) = call(
        bound(fetched_kernel, rank=rank),
        [shape(rows, 3 * rank + 2 * LANES)],
        [early, fetched0, weight, column_sum, sums0],
        left=(0,),
        left_outs=(0,),
        aliases=[(0, 0)],
        scratch=[pltpu.VMEM((rows, rank), BF16), pltpu.VMEM((rows, LANES), BF16), sems((2,))],
        name="fetched",
    )
    got = across(payload)
    both = mirrored(both)
    payload, columns, active_back = call(
        bound(middle_kernel, peers=peers, rank=rank, width=width),
        [shape(rows, 2 * rank + LANES), shape(peers + 8, rank, dtype=F32), shape(own, rank, dtype=F32)],
        [got],
        left_outs=(1,),
        scratch=[pltpu.VMEM((peers + 8, rank), F32), sems((1,))],
        name="middle",
    )
    got0 = across(payload)
    other, kept = call(
        bound(other_kernel, rank=rank),
        [shape(rows, rank + LANES), shape(rank, features)],
        [fetch, evict, both, tokens0, weight, column_sum],
        smem=(0, 1),
        left_outs=(1,),
        scratch=[tile, sems((1,))],
        cost=LONG,
        name="other",
    )
    beside_out, across_out = call(
        bound(first_kernel, rank=rank),
        [shape(rows, features)] * 2,
        [got0, tokens0, fetched0, grad0, norm_gain, down, up, other],
        left=(7,),
        name="first",
    )
    beside_in = swapped(beside_out, 0)
    across_in = swapped(across_out, 1)
    kept, gain_term0, filled = call(
        bound(terms_kernel, peers=peers, rank=rank),
        [shape(rank, features), shape(1, features, dtype=F32), shape(rows, 4 * rank + LANES)],
        [kept, got0, fetched0, grad0, norm_gain, down, active_back],
        left=(0,),
        left_outs=(0, 2),
        aliases=[(0, 0)],
        scratch=[tile, pltpu.VMEM((rows, rank), BF16), sems((2,))],
        cost=LONG,
        name="terms",
    )
    payload, kept, tokens1 = call(
        bound(second_kernel, rank=rank),
        [shape(rows, 3 * rank + LANES), shape(rank, features), shape(rows, features)],
        [kept, beside_in, across_in, fresh_input, beside_out, weight, column_sum, up, other],
        left=(0, 4),
        left_outs=(0, 1, 2),
        aliases=[(0, 1)],
        scratch=[tile, tile, pltpu.VMEM((rows, 3 * rank + LANES), BF16), sems((5,))],
        name="second",
    )
    got = across(payload)
    partner1 = mirrored(tokens1)
    (payload,) = call(
        bound(late_kernel, peers=peers, rank=rank, width=width),
        [shape(rows, 4 * rank + LANES)],
        [filled, got, columns],
        left=(0,),
        left_outs=(0,),
        aliases=[(0, 0)],
        scratch=[pltpu.VMEM((3, rows, rank), BF16), pltpu.VMEM((rows, LANES), BF16), sems((4,))],
        name="late",
    )
    got1 = across(payload)
    stash, done = call(
        stash_kernel,
        [shape(*held_stash.shape), shape(8, LANES, dtype=F32)],
        [evict, held_stash, both, partner1],
        smem=(0,),
        cost=LONG,
        name="stash",
    )
    up_grad, next_output, input_grad, gain_grad, down_grad = call(
        bound(last_kernel, rank=rank),
        [
            shape(rank, features),
            shape(rows, features),
            shape(rows, features),
            shape(1, features, dtype=F32),
            shape(features, rank),
        ],
        [kept, tokens1, done, got1, got0, grad0, gain_term0, norm_gain, down, up],
        left=(0, 1, 2),
        left_outs=(0, 1, 2, 4),
        aliases=[(0, 0), (1, 1)],
        scratch=[
            pltpu.VMEM((4, rows, features), BF16),
            pltpu.VMEM((rank, features), BF16),
            tile,
            tile,
            pltpu.VMEM((features, rank), BF16),
            sems((4,)),
            sems((2,)),
            sems((CHUNKS,)),
            sems((CHUNKS,)),
        ],
        name="last",
    )
    return (next_output[None], input_grad[None], stash, gain_grad, down_grad[None], up_grad[None])


def solution(mesh):
    placed = (
        P("section", None, "dp"),
        P(None, "dp"),
        P("section", None, "dp"),
        P("section", None, None, "dp"),
        P("section", "dp"),
        P("section", "dp", None),
        P("section", None, "dp"),
        P(),
        P(),
    )
    return jax.shard_map(
        on_device,
        mesh=mesh,
        in_specs=placed,
        out_specs=(
            P("section", None, "dp"),
            P("section", None, "dp"),
            P("section", None, None, "dp"),
            P("section", "dp"),
            P("section", "dp", None),
            P("section", None, "dp"),
        ),
        check_vma=False,
    )
```

```python
import math

import jax
import jax.numpy as jnp
from jax import lax
from jax.experimental import pallas as pl
from jax.experimental.pallas import tpu as pltpu
from jax.sharding import PartitionSpec as P

BF16 = jnp.bfloat16
F32 = jnp.float32
EPS = 1e-05
LANES = 128
LONG = 6
CHUNKS = 4
ROOT = math.sqrt(2 / math.pi)
CUBE = 0.044715


def across(block):
    return lax.all_to_all(block, "dp", 0, 0, tiled=True)


def mirrored(value):
    sections = lax.axis_size("section")
    return lax.ppermute(value, "section", [(i, sections - 1 - i) for i in range(sections)])


def shifted(value, by):
    sections = lax.axis_size("section")
    pairs = [(i, i + by) for i in range(sections) if 0 <= i + by < sections]
    return lax.ppermute(value, "section", pairs)


def pieces(value):
    high = value.astype(BF16).astype(F32)
    middle = (value - high).astype(BF16).astype(F32)
    return [high, middle, value - high - middle]


def in_lanes(columns):
    rows = columns[-1].shape[0]
    lane = lax.broadcasted_iota(jnp.int32, (rows, LANES), 1)
    block = jnp.zeros((rows, LANES), F32)
    for i, column in enumerate(columns):
        block = jnp.where(lane == i, column, block)
    return block


def from_lanes(block, first):
    lane = lax.broadcasted_iota(jnp.int32, block.shape, 1)
    return jnp.sum(jnp.where((lane >= first) & (lane < first + 3), block, 0.0), axis=1, keepdims=True)


def row_sums(values):
    one = jnp.sum(values, axis=1, keepdims=True)
    two = jnp.sum(values * values, axis=1, keepdims=True)
    return one, two


def hidden_part(tokens, weight, column_sum):
    values = tokens.astype(F32)
    one, two = row_sums(values)
    part = jnp.dot(tokens, weight, preferred_element_type=F32)
    return part - (one / values.shape[1]) * column_sum, pieces(one) + pieces(two)


def times_transposed(left, right):
    return lax.dot_general(left, right, (((1,), (1,)), ((), ())), preferred_element_type=F32)


def transposed_times(left, right):
    return lax.dot_general(left, right, (((0,), (0,)), ((), ())), preferred_element_type=F32)


def summed(block, peers):
    return jnp.sum(block.astype(F32).reshape(peers, -1, block.shape[1]), axis=0)


def finish_hidden(part, sums, first, column_sums, width):
    peers = len(column_sums)
    one = from_lanes(sums, first).reshape(peers, -1, 1)
    two = from_lanes(sums, first + 3).reshape(peers, -1, 1)
    mean = jnp.sum(one, axis=0) / width
    inverse = lax.rsqrt(jnp.sum(two, axis=0) / width - mean * mean + EPS)
    total = summed(part, peers)
    for peer in range(peers):
        total = total + (one[peer] / (width // peers) - mean) * column_sums[peer]
    return total * inverse, mean, inverse


def gelu(hidden):
    return hidden * (0.5 * (1.0 + jnp.tanh(ROOT * (hidden + CUBE * (hidden * hidden * hidden)))))


def gelu_and_slope(hidden):
    bent = jnp.tanh(ROOT * (hidden + CUBE * (hidden * hidden * hidden)))
    half = 0.5 * (1.0 + bent)
    slope = half + hidden * (0.5 * (1.0 - bent * bent)) * (ROOT * (1.0 + 3.0 * CUBE * (hidden * hidden)))
    return hidden * half, slope


def back_stats(grad_hidden, hidden, mean, inverse, column_exact, width):
    grad = grad_hidden.astype(F32)
    first = jnp.sum(grad * column_exact, axis=1, keepdims=True) / width
    second = jnp.sum(grad * hidden, axis=1, keepdims=True) / width
    return in_lanes(pieces(mean) + pieces(inverse) + pieces(first) + pieces(second))


def to_all(block, peers):
    rows, columns = block.shape
    return jnp.broadcast_to(block[None], (peers, rows, columns)).reshape(peers * rows, columns).astype(BF16)


def backward(tokens, upstream, grad_hidden, sums, gain, down_weight):
    mean, inverse, first, second = [from_lanes(sums, 3 * i) for i in range(4)]
    normed = (tokens.astype(F32) - mean) * inverse
    grad_scaled = times_transposed(grad_hidden, down_weight)
    grad_rows = inverse * (grad_scaled * gain - first - normed * second)
    tokens_grad = (upstream.astype(F32) + grad_rows).astype(BF16)
    gain_term = jnp.sum(grad_scaled * normed, axis=0, keepdims=True)
    return tokens_grad, (normed * gain).astype(BF16), gain_term


def copies(pairs, sems):
    started = [pltpu.make_async_copy(source, target, sems.at[i]) for i, (source, target) in enumerate(pairs)]
    for one in started:
        one.start()
    return started


def pick_kernel(fetch, stash, first, second):
    partner = lax.axis_size("section") - 1 - lax.axis_index("section")
    first[...] = stash[0, fetch[0, partner]]
    second[...] = stash[0, fetch[1, partner]]


def chunks(source, target, count):
    step = source.shape[0] // count
    return [(source.at[pl.ds(i * step, step)], target.at[pl.ds(i * step, step)]) for i in range(count)]


def scaled_weight(gain, down):
    features, rank = down.shape
    tall = jnp.broadcast_to(gain[...].astype(F32), (LANES, features)).T
    return down[...].astype(F32) * jnp.concatenate([tall] * (rank // LANES), axis=1)


def start_kernel(
    tokens, upstream, gain, down, up, other, payload, weight, column_sum, sums, both, parts, sems, *, peers, rank
):
    both[0] = other[...]
    both[1] = tokens[...]
    rows = tokens.shape[0]
    parts[:, rank : 2 * rank] = times_transposed(upstream[...], up[...]).astype(BF16)
    exact = scaled_weight(gain, down)
    rounded = exact.astype(BF16)
    weight[...] = rounded
    one = jnp.sum(rounded.astype(F32), axis=0, keepdims=True)
    column_sum[...] = one
    row = lax.broadcasted_iota(jnp.int32, (rows // peers, LANES), 0)
    block = jnp.zeros((rows // peers, LANES), F32)
    quarters = rank // LANES
    for i, piece in enumerate(pieces(jnp.sum(exact, axis=0, keepdims=True))[:2]):
        for j in range(quarters):
            block = jnp.where(row == i * quarters + j, piece[:, j * LANES : (j + 1) * LANES], block)
    parts[:, 2 * rank :] = to_all(block, peers)
    part, columns = hidden_part(tokens[...], rounded, one)
    sums[...] = in_lanes(columns)
    parts[:, :rank] = part.astype(BF16)
    (saved,) = copies([(parts, payload.at[:, pl.ds(0, 2 * rank + LANES)])], sems)
    saved.wait()


def fetched_kernel(early, tokens, weight, column_sum, sums0, payload, parts, sums, sems, *, rank):
    first = 2 * rank + LANES
    part, columns = hidden_part(tokens[...], weight[...], column_sum[...])
    parts[...] = part.astype(BF16)
    sums[...] = (sums0[...] + in_lanes([0.0] * 6 + columns)).astype(BF16)
    for one in copies(
        [
            (parts, payload.at[:, pl.ds(first, rank)]),
            (sums, payload.at[:, pl.ds(first + rank, LANES)]),
        ],
        sems,
    ):
        one.wait()


def middle_kernel(got, payload, columns_out, active_back, columns, sems, *, peers, rank, width):
    first = 2 * rank + LANES
    blocks = got[:, 2 * rank : first].astype(F32).reshape(peers, -1, LANES)
    row = lax.broadcasted_iota(jnp.int32, blocks.shape[1:], 0)
    quarters = rank // LANES

    def joined(block):
        return jnp.concatenate(
            [
                jnp.sum(jnp.where((row == i) | (row == quarters + i), block, 0.0), axis=0, keepdims=True)
                for i in range(quarters)
            ],
            axis=1,
        )

    column_sums = []
    for peer in range(peers):
        column_sums.append(joined(blocks[peer]))
        columns[peer : peer + 1, :] = column_sums[peer]
    column_exact = joined(jnp.sum(blocks, axis=0))
    columns[peers : peers + 1, :] = column_exact
    columns[peers + 1 :, :] = jnp.zeros((7, rank), F32)
    (saved,) = copies([(columns, columns_out)], sems)
    sums = got[:, first + rank :].astype(F32)
    hidden_f = finish_hidden(got[:, :rank], sums, 0, column_sums, width)[0]
    slope = summed(got[:, rank : 2 * rank], peers)
    hidden, mean, inverse = finish_hidden(
        got[:, first : first + rank], sums, 6, column_sums, width
    )
    active, bent = gelu_and_slope(hidden)
    active_back[...] = active
    grad_hidden = (slope * bent).astype(BF16)
    payload[:, :rank] = to_all(gelu(hidden_f), peers)
    payload[:, rank : 2 * rank] = to_all(grad_hidden.astype(F32), peers)
    payload[:, 2 * rank :] = to_all(back_stats(grad_hidden, hidden, mean, inverse, column_exact, width), peers)
    saved.wait()


def first_kernel(got, tokens, fetched, upstream, gain, down, up, after, out, grad, *, rank):
    out[...] = (
        tokens[...].astype(F32) + jnp.dot(got[:, :rank], up[...], preferred_element_type=F32)
    ).astype(BF16)
    grad[...] = backward(
        fetched[...], upstream[...], got[:, rank : 2 * rank], got[:, 2 * rank :].astype(F32), gain[...].astype(F32), down[...]
    )[0]


def other_kernel(
    fetch, evict, arrived, tokens, weight, column_sum, payload, kept, chosen, sems, *, rank
):
    place = lax.axis_index("section")
    chosen[...] = jnp.where(fetch[1, place] == evict[0, place], tokens[...], arrived[0])
    (saved,) = copies([(chosen, kept.at[pl.ds(0, tokens.shape[0])])], sems)
    part, sums = hidden_part(chosen[...], weight[...], column_sum[...])
    payload[:, :rank] = part.astype(BF16)
    payload[:, rank:] = in_lanes([0.0] * 6 + sums).astype(BF16)
    saved.wait()


def terms_kernel(
    kept_in, got, fetched, upstream, gain, down, active_back, kept, gain_term, payload, scaled, active, sems, *, peers, rank
):
    active[...] = to_all(active_back[...], peers)
    (ready,) = copies([(active, payload.at[:, pl.ds(3 * rank, rank)])], sems.at[pl.ds(1, 1)])
    scaled[...], gain_term[...] = backward(
        fetched[...], upstream[...], got[:, rank : 2 * rank], got[:, 2 * rank :].astype(F32), gain[...].astype(F32), down[...]
    )[1:]
    rows = scaled.shape[0]
    (saved,) = copies([(scaled, kept.at[pl.ds(rows, rows)])], sems)
    saved.wait()
    ready.wait()


def second_kernel(
    kept_in, before, after, fresh, own, weight, column_sum, up, side, payload, kept, tokens_out, tokens, upstream, parts, sems,
    *, rank
):
    place = lax.axis_index("section")
    rows = before.shape[0]
    tokens[...] = jnp.where(place == 0, fresh[...], before[...])
    first = pltpu.make_async_copy(tokens, tokens_out, sems.at[0])
    first.start()
    upstream[...] = jnp.where(place == lax.axis_size("section") - 1, own[...], after[...])
    second = pltpu.make_async_copy(upstream, kept.at[pl.ds(2 * rows, rows)], sems.at[1])
    second.start()
    parts[:, 2 * rank : 3 * rank] = side[:, :rank]
    parts[:, rank : 2 * rank] = times_transposed(upstream[...], up[...]).astype(BF16)
    span = pl.ds(rank, 2 * rank)
    third = pltpu.make_async_copy(parts.at[:, span], payload.at[:, span], sems.at[2])
    third.start()
    part, sums = hidden_part(tokens[...], weight[...], column_sum[...])
    parts[:, :rank] = part.astype(BF16)
    span = pl.ds(0, rank)
    fourth = pltpu.make_async_copy(parts.at[:, span], payload.at[:, span], sems.at[3])
    fourth.start()
    parts[:, 3 * rank :] = (side[:, rank:].astype(F32) + in_lanes(sums)).astype(BF16)
    span = pl.ds(3 * rank, LANES)
    fifth = pltpu.make_async_copy(parts.at[:, span], payload.at[:, span], sems.at[4])
    fifth.start()
    for one in (first, second, third, fourth, fifth):
        one.wait()


def late_kernel(filled, got, columns, payload, parts, last, sems, *, peers, rank, width):
    column_sums = [columns[peer : peer + 1, :] for peer in range(peers)]
    sums = got[:, 3 * rank :].astype(F32)
    stores = []

    def store(source, first, lanes):
        stores.append(pltpu.make_async_copy(source, payload.at[:, pl.ds(first, lanes)], sems.at[len(stores)]))
        stores[-1].start()

    hidden, mean, inverse = finish_hidden(got[:, 2 * rank : 3 * rank], sums, 6, column_sums, width)
    active, bent = gelu_and_slope(hidden)
    parts[0] = to_all(active, peers)
    store(parts.at[0], 2 * rank, rank)
    slope = summed(got[:, rank : 2 * rank], peers)
    grad_hidden = (slope * bent).astype(BF16)
    parts[1] = to_all(grad_hidden.astype(F32), peers)
    store(parts.at[1], rank, rank)
    last[...] = to_all(
        back_stats(grad_hidden, hidden, mean, inverse, columns[peers : peers + 1, :], width), peers
    )
    store(last, 4 * rank, LANES)
    hidden_f = finish_hidden(got[:, :rank], sums, 0, column_sums, width)[0]
    parts[2] = to_all(gelu(hidden_f), peers)
    store(parts.at[2], 0, rank)
    for one in stores:
        one.wait()


def stash_kernel(evict, stash, arrived, partner1, stash_out, done):
    partner = lax.axis_size("section") - 1 - lax.axis_index("section")
    early, late = evict[0, partner], evict[1, partner]
    for i in range(stash.shape[1]):
        stash_out[0, i] = jnp.where(late == i, partner1[...], jnp.where(early == i, arrived[1], stash[0, i]))
    done[...] = jnp.zeros_like(done)


def last_kernel(
    kept_in, tokens_in, done, got, got0, upstream0_in, gain_term0, gain, down, up,
    up_grad_out, out_out, grad_out, gain_grad, down_grad_out, tiles, up_grad, out, grad, down_grad,
    load_sems, sems, up_sems, down_sems, *, rank
):
    rows = tokens_in.shape[0]
    loads = copies(
        [
            (kept_in.at[pl.ds(2 * rows, rows)], tiles.at[0]),
            (tokens_in, tiles.at[1]),
            (kept_in.at[pl.ds(0, rows)], tiles.at[2]),
            (kept_in.at[pl.ds(rows, rows)], tiles.at[3]),
        ],
        load_sems,
    )
    grad_hidden = got[:, rank : 2 * rank]
    product = jnp.dot(got[:, :rank], up[...], preferred_element_type=F32)
    grad_scaled = times_transposed(grad_hidden, down[...])
    sums = got[:, 4 * rank :].astype(F32)
    mean, inverse, first, second = [from_lanes(sums, 3 * i) for i in range(4)]
    grad_normed = grad_scaled * gain[...].astype(F32)
    active_both = jnp.concatenate([got[:, 3 * rank : 4 * rank], got[:, 2 * rank : 3 * rank]], axis=0)
    hidden_both = jnp.concatenate([got0[:, rank : 2 * rank], grad_hidden], axis=0)
    stores = []

    def store(source, target, sem):
        stores.append(pltpu.make_async_copy(source, target, sem))
        stores[-1].start()

    loads[0].wait()
    upstream = tiles[0]
    upstream_both = jnp.concatenate([upstream0_in[...], upstream], axis=0)
    step = rank // CHUNKS
    for i, (part, target) in enumerate(chunks(up_grad, up_grad_out, CHUNKS)):
        part[...] = transposed_times(active_both[:, i * step : (i + 1) * step], upstream_both).astype(BF16)
        if i == 0:
            loads[1].wait()
            loads[2].wait()
            loads[3].wait()
        store(part, target, up_sems.at[i])
    out[...] = (tiles[1].astype(F32) + product).astype(BF16)
    store(out, out_out, sems.at[0])
    normed = (tiles[2].astype(F32) - mean) * inverse
    grad[...] = (upstream.astype(F32) + inverse * (grad_normed - first - normed * second)).astype(BF16)
    store(grad, grad_out, sems.at[1])
    gain_grad[...] = gain_term0[...] + jnp.sum(grad_scaled * normed, axis=0, keepdims=True)
    scaled_both = jnp.concatenate([tiles[3], (normed * gain[...].astype(F32)).astype(BF16)], axis=0)
    step = down_grad.shape[0] // CHUNKS
    for i, (part, target) in enumerate(chunks(down_grad, down_grad_out, CHUNKS)):
        part[...] = transposed_times(scaled_both[:, i * step : (i + 1) * step], hidden_both).astype(BF16)
        store(part, target, down_sems.at[i])
    for one in stores:
        one.wait()


def call(body, outs, operands, cost=1, smem=(), left=(), left_outs=(), scratch=(), aliases=(), name=None):
    spaces = [pltpu.SMEM if i in smem else pltpu.HBM if i in left else pltpu.VMEM for i in range(len(operands))]
    out_spaces = [pltpu.HBM if i in left_outs else pltpu.VMEM for i in range(len(outs))]
    return pl.pallas_call(
        body,
        out_shape=tuple(outs),
        in_specs=[pl.BlockSpec(memory_space=s) for s in spaces],
        out_specs=tuple(pl.BlockSpec(memory_space=s) for s in out_spaces),
        scratch_shapes=list(scratch),
        compiler_params=pltpu.CompilerParams(vmem_limit_bytes=16 * 2**20),
        cost_estimate=pl.CostEstimate(flops=cost * 2**31, bytes_accessed=cost * 2**20, transcendentals=0),
        input_output_aliases=dict(aliases),
        name=name,
    )(*operands)


def bound(body, **sizes):
    def run(*refs):
        body(*refs, **sizes)

    return run


def on_device(layer_input, fresh_input, out_grad, held_stash, norm_gain, down_proj, up_proj, fetch_slot, evict_slot):
    peers = lax.axis_size("dp")
    tokens0, grad0 = layer_input[0], out_grad[0]
    down, up = down_proj[0], up_proj[0]
    rows, features = tokens0.shape
    rank = up.shape[0]
    width = features * peers
    own = rows // peers

    def shape(*dims, dtype=BF16):
        return jax.ShapeDtypeStruct(dims, dtype)

    tile = pltpu.VMEM((rows, features), BF16)
    sems = pltpu.SemaphoreType.DMA
    fetch, evict = fetch_slot.T, evict_slot.T

    picked, other = call(
        pick_kernel,
        [shape(rows, features), shape(rows, features)],
        [fetch, held_stash],
        smem=(0,),
        name="pick",
    )
    fetched0 = mirrored(picked)
    early, weight, column_sum, sums0, both = call(
        bound(start_kernel, peers=peers, rank=rank),
        [
            shape(rows, 3 * rank + 2 * LANES),
            shape(features, rank),
            shape(1, rank, dtype=F32),
            shape(rows, LANES, dtype=F32),
            shape(2, rows, features),
        ],
        [tokens0, grad0, norm_gain, down, up, other],
        left_outs=(0,),
        scratch=[pltpu.VMEM((rows, 2 * rank + LANES), BF16), sems((1,))],
        name="start",
    )
    (payload,) = call(
        bound(fetched_kernel, rank=rank),
        [shape(rows, 3 * rank + 2 * LANES)],
        [early, fetched0, weight, column_sum, sums0],
        left=(0,),
        left_outs=(0,),
        aliases=[(0, 0)],
        scratch=[pltpu.VMEM((rows, rank), BF16), pltpu.VMEM((rows, LANES), BF16), sems((2,))],
        name="fetched",
    )
    got = across(payload)
    both = mirrored(both)
    payload, columns, active_back = call(
        bound(middle_kernel, peers=peers, rank=rank, width=width),
        [shape(rows, 2 * rank + LANES), shape(peers + 8, rank, dtype=F32), shape(own, rank, dtype=F32)],
        [got],
        left_outs=(1,),
        scratch=[pltpu.VMEM((peers + 8, rank), F32), sems((1,))],
        name="middle",
    )
    got0 = across(payload)
    other, kept = call(
        bound(other_kernel, rank=rank),
        [shape(rows, rank + LANES), shape(rank, features)],
        [fetch, evict, both, tokens0, weight, column_sum],
        smem=(0, 1),
        left_outs=(1,),
        scratch=[tile, sems((1,))],
        cost=LONG,
        name="other",
    )
    first_out, first_grad = call(
        bound(first_kernel, rank=rank),
        [shape(rows, features)] * 2,
        [got0, tokens0, fetched0, grad0, norm_gain, down, up, other],
        left=(7,),
        name="first",
    )
    before_out = shifted(first_out, 1)
    after_grad = shifted(first_grad, -1)
    kept, gain_term0, filled = call(
        bound(terms_kernel, peers=peers, rank=rank),
        [shape(rank, features), shape(1, features, dtype=F32), shape(rows, 4 * rank + LANES)],
        [kept, got0, fetched0, grad0, norm_gain, down, active_back],
        left=(0,),
        left_outs=(0, 2),
        aliases=[(0, 0)],
        scratch=[tile, pltpu.VMEM((rows, rank), BF16), sems((2,))],
        cost=LONG,
        name="terms",
    )
    payload, kept, tokens1 = call(
        bound(second_kernel, rank=rank),
        [shape(rows, 3 * rank + LANES), shape(rank, features), shape(rows, features)],
        [kept, before_out, after_grad, fresh_input, first_out, weight, column_sum, up, other],
        left=(0,),
        left_outs=(0, 1, 2),
        aliases=[(0, 1)],
        scratch=[tile, tile, pltpu.VMEM((rows, 3 * rank + LANES), BF16), sems((5,))],
        name="second",
    )
    got = across(payload)
    partner1 = mirrored(tokens1)
    (payload,) = call(
        bound(late_kernel, peers=peers, rank=rank, width=width),
        [shape(rows, 4 * rank + LANES)],
        [filled, got, columns],
        left=(0,),
        left_outs=(0,),
        aliases=[(0, 0)],
        scratch=[pltpu.VMEM((3, rows, rank), BF16), pltpu.VMEM((rows, LANES), BF16), sems((4,))],
        name="late",
    )
    got1 = across(payload)
    stash, done = call(
        stash_kernel,
        [shape(*held_stash.shape), shape(8, LANES, dtype=F32)],
        [evict, held_stash, both, partner1],
        smem=(0,),
        cost=LONG,
        name="stash",
    )
    up_grad, next_output, input_grad, gain_grad, down_grad = call(
        bound(last_kernel, rank=rank),
        [
            shape(rank, features),
            shape(rows, features),
            shape(rows, features),
            shape(1, features, dtype=F32),
            shape(features, rank),
        ],
        [kept, tokens1, done, got1, got0, grad0, gain_term0, norm_gain, down, up],
        left=(0, 1, 2),
        left_outs=(0, 1, 2, 4),
        aliases=[(0, 0), (1, 1)],
        scratch=[
            pltpu.VMEM((4, rows, features), BF16),
            pltpu.VMEM((rank, features), BF16),
            tile,
            tile,
            pltpu.VMEM((features, rank), BF16),
            sems((4,)),
            sems((2,)),
            sems((CHUNKS,)),
            sems((CHUNKS,)),
        ],
        name="last",
    )
    return (next_output[None], input_grad[None], stash, gain_grad, down_grad[None], up_grad[None])


def solution(mesh):
    placed = (
        P("section", None, "dp"),
        P(None, "dp"),
        P("section", None, "dp"),
        P("section", None, None, "dp"),
        P("section", "dp"),
        P("section", "dp", None),
        P("section", None, "dp"),
        P(),
        P(),
    )
    return jax.shard_map(
        on_device,
        mesh=mesh,
        in_specs=placed,
        out_specs=(
            P("section", None, "dp"),
            P("section", None, "dp"),
            P("section", None, None, "dp"),
            P("section", "dp"),
            P("section", "dp", None),
            P("section", None, "dp"),
        ),
        check_vma=False,
    )
```

```python
import math

import jax
import jax.numpy as jnp
from jax import lax
from jax.experimental import pallas as pl
from jax.experimental.pallas import tpu as pltpu
from jax.sharding import PartitionSpec as P

BF16 = jnp.bfloat16
F32 = jnp.float32
EPS = 1e-05
LANES = 128
LONG = 6
CHUNKS = 4
ROOT = math.sqrt(2 / math.pi)
CUBE = 0.044715


def across(block):
    return lax.all_to_all(block, "dp", 0, 0, tiled=True)


def mirrored(value):
    sections = lax.axis_size("section")
    return lax.ppermute(value, "section", [(i, sections - 1 - i) for i in range(sections)])


def swapped(value, first):
    sections = lax.axis_size("section")
    pairs = [(i, i + 1) for i in range(first, sections - 1, 2)]
    alone = [(sections - 1, sections - 1)] if (sections - first) % 2 else []
    return lax.ppermute(value, "section", pairs + [(j, i) for i, j in pairs] + alone)


def pieces(value):
    high = value.astype(BF16).astype(F32)
    middle = (value - high).astype(BF16).astype(F32)
    return [high, middle, value - high - middle]


def in_lanes(columns):
    rows = columns[-1].shape[0]
    lane = lax.broadcasted_iota(jnp.int32, (rows, LANES), 1)
    block = jnp.zeros((rows, LANES), F32)
    for i, column in enumerate(columns):
        block = jnp.where(lane == i, column, block)
    return block


def from_lanes(block, first):
    lane = lax.broadcasted_iota(jnp.int32, block.shape, 1)
    return jnp.sum(jnp.where((lane >= first) & (lane < first + 3), block, 0.0), axis=1, keepdims=True)


def row_sums(values):
    one = jnp.sum(values, axis=1, keepdims=True)
    two = jnp.sum(values * values, axis=1, keepdims=True)
    return one, two


def hidden_part(tokens, weight, column_sum):
    values = tokens.astype(F32)
    one, two = row_sums(values)
    part = jnp.dot(tokens, weight, preferred_element_type=F32)
    return part - (one / values.shape[1]) * column_sum, pieces(one) + pieces(two)


def times_transposed(left, right):
    return lax.dot_general(left, right, (((1,), (1,)), ((), ())), preferred_element_type=F32)


def transposed_times(left, right):
    return lax.dot_general(left, right, (((0,), (0,)), ((), ())), preferred_element_type=F32)


def summed(block, peers):
    return jnp.sum(block.astype(F32).reshape(peers, -1, block.shape[1]), axis=0)


def finish_hidden(part, sums, first, column_sums, width):
    peers = len(column_sums)
    one = from_lanes(sums, first).reshape(peers, -1, 1)
    two = from_lanes(sums, first + 3).reshape(peers, -1, 1)
    mean = jnp.sum(one, axis=0) / width
    inverse = lax.rsqrt(jnp.sum(two, axis=0) / width - mean * mean + EPS)
    total = summed(part, peers)
    for peer in range(peers):
        total = total + (one[peer] / (width // peers) - mean) * column_sums[peer]
    return total * inverse, mean, inverse


def gelu(hidden):
    return hidden * (0.5 * (1.0 + jnp.tanh(ROOT * (hidden + CUBE * (hidden * hidden * hidden)))))


def gelu_and_slope(hidden):
    bent = jnp.tanh(ROOT * (hidden + CUBE * (hidden * hidden * hidden)))
    half = 0.5 * (1.0 + bent)
    slope = half + hidden * (0.5 * (1.0 - bent * bent)) * (ROOT * (1.0 + 3.0 * CUBE * (hidden * hidden)))
    return hidden * half, slope


def back_stats(grad_hidden, hidden, mean, inverse, column_exact, width):
    grad = grad_hidden.astype(F32)
    first = jnp.sum(grad * column_exact, axis=1, keepdims=True) / width
    second = jnp.sum(grad * hidden, axis=1, keepdims=True) / width
    return in_lanes(pieces(mean) + pieces(inverse) + pieces(first) + pieces(second))


def to_all(block, peers):
    rows, columns = block.shape
    return jnp.broadcast_to(block[None], (peers, rows, columns)).reshape(peers * rows, columns).astype(BF16)


def backward(tokens, upstream, grad_hidden, sums, gain, down_weight):
    mean, inverse, first, second = [from_lanes(sums, 3 * i) for i in range(4)]
    normed = (tokens.astype(F32) - mean) * inverse
    grad_scaled = times_transposed(grad_hidden, down_weight)
    grad_rows = inverse * (grad_scaled * gain - first - normed * second)
    tokens_grad = (upstream.astype(F32) + grad_rows).astype(BF16)
    gain_term = jnp.sum(grad_scaled * normed, axis=0, keepdims=True)
    return tokens_grad, (normed * gain).astype(BF16), gain_term


def copies(pairs, sems):
    started = [pltpu.make_async_copy(source, target, sems.at[i]) for i, (source, target) in enumerate(pairs)]
    for one in started:
        one.start()
    return started


def pick_kernel(fetch, stash, first, second):
    partner = lax.axis_size("section") - 1 - lax.axis_index("section")
    first[...] = stash[0, fetch[0, partner]]
    second[...] = stash[0, fetch[1, partner]]


def chunks(source, target, count):
    step = source.shape[0] // count
    return [(source.at[pl.ds(i * step, step)], target.at[pl.ds(i * step, step)]) for i in range(count)]


def scaled_weight(gain, down):
    features, rank = down.shape
    tall = jnp.broadcast_to(gain[...].astype(F32), (LANES, features)).T
    return down[...].astype(F32) * jnp.concatenate([tall] * (rank // LANES), axis=1)


def start_kernel(
    tokens, upstream, gain, down, up, other, payload, weight, column_sum, sums, both, parts, sems, *, peers, rank
):
    both[0] = other[...]
    both[1] = tokens[...]
    rows = tokens.shape[0]
    parts[:, rank : 2 * rank] = times_transposed(upstream[...], up[...]).astype(BF16)
    exact = scaled_weight(gain, down)
    rounded = exact.astype(BF16)
    weight[...] = rounded
    one = jnp.sum(rounded.astype(F32), axis=0, keepdims=True)
    column_sum[...] = one
    row = lax.broadcasted_iota(jnp.int32, (rows // peers, LANES), 0)
    block = jnp.zeros((rows // peers, LANES), F32)
    quarters = rank // LANES
    for i, piece in enumerate(pieces(jnp.sum(exact, axis=0, keepdims=True))[:2]):
        for j in range(quarters):
            block = jnp.where(row == i * quarters + j, piece[:, j * LANES : (j + 1) * LANES], block)
    parts[:, 2 * rank :] = to_all(block, peers)
    part, columns = hidden_part(tokens[...], rounded, one)
    sums[...] = in_lanes(columns)
    parts[:, :rank] = part.astype(BF16)
    (saved,) = copies([(parts, payload.at[:, pl.ds(0, 2 * rank + LANES)])], sems)
    saved.wait()


def fetched_kernel(early, tokens, weight, column_sum, sums0, payload, parts, sums, sems, *, rank):
    first = 2 * rank + LANES
    part, columns = hidden_part(tokens[...], weight[...], column_sum[...])
    parts[...] = part.astype(BF16)
    sums[...] = (sums0[...] + in_lanes([0.0] * 6 + columns)).astype(BF16)
    for one in copies(
        [
            (parts, payload.at[:, pl.ds(first, rank)]),
            (sums, payload.at[:, pl.ds(first + rank, LANES)]),
        ],
        sems,
    ):
        one.wait()


def middle_kernel(got, payload, columns_out, columns, sems, *, peers, rank, width):
    first = 2 * rank + LANES
    blocks = got[:, 2 * rank : first].astype(F32).reshape(peers, -1, LANES)
    row = lax.broadcasted_iota(jnp.int32, blocks.shape[1:], 0)
    quarters = rank // LANES

    def joined(block):
        return jnp.concatenate(
            [
                jnp.sum(jnp.where((row == i) | (row == quarters + i), block, 0.0), axis=0, keepdims=True)
                for i in range(quarters)
            ],
            axis=1,
        )

    column_sums = []
    for peer in range(peers):
        column_sums.append(joined(blocks[peer]))
        columns[peer : peer + 1, :] = column_sums[peer]
    column_exact = joined(jnp.sum(blocks, axis=0))
    columns[peers : peers + 1, :] = column_exact
    columns[peers + 1 :, :] = jnp.zeros((7, rank), F32)
    (saved,) = copies([(columns, columns_out)], sems)
    sums = got[:, first + rank :].astype(F32)
    hidden_f = finish_hidden(got[:, :rank], sums, 0, column_sums, width)[0]
    slope = summed(got[:, rank : 2 * rank], peers)
    hidden, mean, inverse = finish_hidden(
        got[:, first : first + rank], sums, 6, column_sums, width
    )
    active, bent = gelu_and_slope(hidden)
    grad_hidden = (slope * bent).astype(BF16)
    payload[:, :rank] = to_all(gelu(hidden_f), peers)
    payload[:, rank : 2 * rank] = to_all(grad_hidden.astype(F32), peers)
    payload[:, 2 * rank : 3 * rank] = to_all(active, peers)
    payload[:, 3 * rank :] = to_all(back_stats(grad_hidden, hidden, mean, inverse, column_exact, width), peers)
    saved.wait()


def first_kernel(got, tokens, fetched, upstream, gain, down, up, after, beside_out, across_out, *, rank):
    out = (tokens[...].astype(F32) + jnp.dot(got[:, :rank], up[...], preferred_element_type=F32)).astype(BF16)
    grad = backward(
        fetched[...], upstream[...], got[:, rank : 2 * rank], got[:, 3 * rank :].astype(F32), gain[...].astype(F32), down[...]
    )[0]
    odd = lax.rem(lax.axis_index("section"), 2) == 1
    across_out[...] = jnp.where(odd, out, grad)
    beside_out[...] = jnp.where(odd, grad, out)


def other_kernel(
    fetch, evict, arrived, tokens, weight, column_sum, payload, kept, chosen, sems, *, rank
):
    place = lax.axis_index("section")
    chosen[...] = jnp.where(fetch[1, place] == evict[0, place], tokens[...], arrived[0])
    (saved,) = copies([(chosen, kept.at[pl.ds(0, tokens.shape[0])])], sems)
    part, sums = hidden_part(chosen[...], weight[...], column_sum[...])
    payload[:, :rank] = part.astype(BF16)
    payload[:, rank:] = in_lanes([0.0] * 6 + sums).astype(BF16)
    saved.wait()


def terms_kernel(
    kept_in, got, fetched, upstream, gain, down, kept, gain_term, scaled, sems, *, rank
):
    scaled[...], gain_term[...] = backward(
        fetched[...], upstream[...], got[:, rank : 2 * rank], got[:, 3 * rank :].astype(F32), gain[...].astype(F32), down[...]
    )[1:]
    rows = scaled.shape[0]
    (saved,) = copies([(scaled, kept.at[pl.ds(rows, rows)])], sems)
    saved.wait()


def second_kernel(
    kept_in, beside_in, across_in, fresh, still, weight, column_sum, up, side, payload, kept, tokens_out, tokens, upstream, parts, sems,
    *, rank
):
    place = lax.axis_index("section")
    odd = lax.rem(place, 2) == 1
    rows = fresh.shape[0]
    tokens[...] = jnp.where(place == 0, fresh[...], jnp.where(odd, beside_in[...], across_in[...]))
    first = pltpu.make_async_copy(tokens, tokens_out, sems.at[0])
    first.start()
    upstream[...] = jnp.where(odd, across_in[...], beside_in[...])
    second = pltpu.make_async_copy(upstream, kept.at[pl.ds(2 * rows, rows)], sems.at[1])
    second.start()
    parts[:, 2 * rank : 3 * rank] = side[:, :rank]
    parts[:, rank : 2 * rank] = times_transposed(upstream[...], up[...]).astype(BF16)
    span = pl.ds(rank, 2 * rank)
    third = pltpu.make_async_copy(parts.at[:, span], payload.at[:, span], sems.at[2])
    third.start()
    part, sums = hidden_part(tokens[...], weight[...], column_sum[...])
    parts[:, :rank] = part.astype(BF16)
    span = pl.ds(0, rank)
    fourth = pltpu.make_async_copy(parts.at[:, span], payload.at[:, span], sems.at[3])
    fourth.start()
    parts[:, 3 * rank :] = (side[:, rank:].astype(F32) + in_lanes(sums)).astype(BF16)
    span = pl.ds(3 * rank, LANES)
    fifth = pltpu.make_async_copy(parts.at[:, span], payload.at[:, span], sems.at[4])
    fifth.start()
    for one in (first, second, third, fourth, fifth):
        one.wait()


def late_kernel(got, columns, payload, parts, last, sems, *, peers, rank, width):
    column_sums = [columns[peer : peer + 1, :] for peer in range(peers)]
    sums = got[:, 3 * rank :].astype(F32)
    stores = []

    def store(source, first, lanes):
        stores.append(pltpu.make_async_copy(source, payload.at[:, pl.ds(first, lanes)], sems.at[len(stores)]))
        stores[-1].start()

    hidden, mean, inverse = finish_hidden(got[:, 2 * rank : 3 * rank], sums, 6, column_sums, width)
    active, bent = gelu_and_slope(hidden)
    parts[0] = to_all(active, peers)
    store(parts.at[0], 2 * rank, rank)
    slope = summed(got[:, rank : 2 * rank], peers)
    grad_hidden = (slope * bent).astype(BF16)
    parts[1] = to_all(grad_hidden.astype(F32), peers)
    store(parts.at[1], rank, rank)
    last[...] = to_all(
        back_stats(grad_hidden, hidden, mean, inverse, columns[peers : peers + 1, :], width), peers
    )
    store(last, 3 * rank, LANES)
    hidden_f = finish_hidden(got[:, :rank], sums, 0, column_sums, width)[0]
    parts[2] = to_all(gelu(hidden_f), peers)
    store(parts.at[2], 0, rank)
    for one in stores:
        one.wait()


def stash_kernel(evict, stash, arrived, partner1, stash_out, done):
    partner = lax.axis_size("section") - 1 - lax.axis_index("section")
    early, late = evict[0, partner], evict[1, partner]
    for i in range(stash.shape[1]):
        stash_out[0, i] = jnp.where(late == i, partner1[...], jnp.where(early == i, arrived[1], stash[0, i]))
    done[...] = jnp.zeros_like(done)


def last_kernel(
    kept_in, tokens_in, done, got, got0, upstream0_in, gain_term0, gain, down, up,
    up_grad_out, out_out, grad_out, gain_grad, down_grad_out, tiles, up_grad, out, grad, down_grad,
    load_sems, sems, up_sems, down_sems, *, rank
):
    rows = tokens_in.shape[0]
    loads = copies(
        [
            (kept_in.at[pl.ds(2 * rows, rows)], tiles.at[0]),
            (tokens_in, tiles.at[1]),
            (kept_in.at[pl.ds(0, rows)], tiles.at[2]),
            (kept_in.at[pl.ds(rows, rows)], tiles.at[3]),
        ],
        load_sems,
    )
    grad_hidden = got[:, rank : 2 * rank]
    product = jnp.dot(got[:, :rank], up[...], preferred_element_type=F32)
    grad_scaled = times_transposed(grad_hidden, down[...])
    sums = got[:, 3 * rank :].astype(F32)
    mean, inverse, first, second = [from_lanes(sums, 3 * i) for i in range(4)]
    grad_normed = grad_scaled * gain[...].astype(F32)
    active_both = jnp.concatenate([got0[:, 2 * rank : 3 * rank], got[:, 2 * rank : 3 * rank]], axis=0)
    hidden_both = jnp.concatenate([got0[:, rank : 2 * rank], grad_hidden], axis=0)
    stores = []

    def store(source, target, sem):
        stores.append(pltpu.make_async_copy(source, target, sem))
        stores[-1].start()

    loads[0].wait()
    upstream = tiles[0]
    upstream_both = jnp.concatenate([upstream0_in[...], upstream], axis=0)
    step = rank // CHUNKS
    for i, (part, target) in enumerate(chunks(up_grad, up_grad_out, CHUNKS)):
        part[...] = transposed_times(active_both[:, i * step : (i + 1) * step], upstream_both).astype(BF16)
        if i == 0:
            loads[1].wait()
            loads[2].wait()
            loads[3].wait()
        store(part, target, up_sems.at[i])
    out[...] = (tiles[1].astype(F32) + product).astype(BF16)
    store(out, out_out, sems.at[0])
    normed = (tiles[2].astype(F32) - mean) * inverse
    grad[...] = (upstream.astype(F32) + inverse * (grad_normed - first - normed * second)).astype(BF16)
    store(grad, grad_out, sems.at[1])
    gain_grad[...] = gain_term0[...] + jnp.sum(grad_scaled * normed, axis=0, keepdims=True)
    scaled_both = jnp.concatenate([tiles[3], (normed * gain[...].astype(F32)).astype(BF16)], axis=0)
    step = down_grad.shape[0] // CHUNKS
    for i, (part, target) in enumerate(chunks(down_grad, down_grad_out, CHUNKS)):
        part[...] = transposed_times(scaled_both[:, i * step : (i + 1) * step], hidden_both).astype(BF16)
        store(part, target, down_sems.at[i])
    for one in stores:
        one.wait()


def call(body, outs, operands, cost=1, smem=(), left=(), left_outs=(), scratch=(), aliases=(), name=None):
    spaces = [pltpu.SMEM if i in smem else pltpu.HBM if i in left else pltpu.VMEM for i in range(len(operands))]
    out_spaces = [pltpu.HBM if i in left_outs else pltpu.VMEM for i in range(len(outs))]
    return pl.pallas_call(
        body,
        out_shape=tuple(outs),
        in_specs=[pl.BlockSpec(memory_space=s) for s in spaces],
        out_specs=tuple(pl.BlockSpec(memory_space=s) for s in out_spaces),
        scratch_shapes=list(scratch),
        compiler_params=pltpu.CompilerParams(vmem_limit_bytes=16 * 2**20),
        cost_estimate=pl.CostEstimate(flops=cost * 2**31, bytes_accessed=cost * 2**20, transcendentals=0),
        input_output_aliases=dict(aliases),
        name=name,
    )(*operands)


def bound(body, **sizes):
    def run(*refs):
        body(*refs, **sizes)

    return run


def on_device(layer_input, fresh_input, out_grad, held_stash, norm_gain, down_proj, up_proj, fetch_slot, evict_slot):
    peers = lax.axis_size("dp")
    tokens0, grad0 = layer_input[0], out_grad[0]
    down, up = down_proj[0], up_proj[0]
    rows, features = tokens0.shape
    rank = up.shape[0]
    width = features * peers
    own = rows // peers

    def shape(*dims, dtype=BF16):
        return jax.ShapeDtypeStruct(dims, dtype)

    tile = pltpu.VMEM((rows, features), BF16)
    sems = pltpu.SemaphoreType.DMA
    fetch, evict = fetch_slot.T, evict_slot.T

    picked, other = call(
        pick_kernel,
        [shape(rows, features), shape(rows, features)],
        [fetch, held_stash],
        smem=(0,),
        name="pick",
    )
    fetched0 = mirrored(picked)
    early, weight, column_sum, sums0, both = call(
        bound(start_kernel, peers=peers, rank=rank),
        [
            shape(rows, 3 * rank + 2 * LANES),
            shape(features, rank),
            shape(1, rank, dtype=F32),
            shape(rows, LANES, dtype=F32),
            shape(2, rows, features),
        ],
        [tokens0, grad0, norm_gain, down, up, other],
        left_outs=(0,),
        scratch=[pltpu.VMEM((rows, 2 * rank + LANES), BF16), sems((1,))],
        name="start",
    )
    (payload,) = call(
        bound(fetched_kernel, rank=rank),
        [shape(rows, 3 * rank + 2 * LANES)],
        [early, fetched0, weight, column_sum, sums0],
        left=(0,),
        left_outs=(0,),
        aliases=[(0, 0)],
        scratch=[pltpu.VMEM((rows, rank), BF16), pltpu.VMEM((rows, LANES), BF16), sems((2,))],
        name="fetched",
    )
    got = across(payload)
    both = mirrored(both)
    payload, columns = call(
        bound(middle_kernel, peers=peers, rank=rank, width=width),
        [shape(rows, 3 * rank + LANES), shape(peers + 8, rank, dtype=F32)],
        [got],
        left_outs=(1,),
        scratch=[pltpu.VMEM((peers + 8, rank), F32), sems((1,))],
        name="middle",
    )
    got0 = across(payload)
    other, kept = call(
        bound(other_kernel, rank=rank),
        [shape(rows, rank + LANES), shape(rank, features)],
        [fetch, evict, both, tokens0, weight, column_sum],
        smem=(0, 1),
        left_outs=(1,),
        scratch=[tile, sems((1,))],
        cost=LONG,
        name="other",
    )
    beside_out, across_out = call(
        bound(first_kernel, rank=rank),
        [shape(rows, features)] * 2,
        [got0, tokens0, fetched0, grad0, norm_gain, down, up, other],
        left=(7,),
        name="first",
    )
    beside_in = swapped(beside_out, 0)
    across_in = swapped(across_out, 1)
    kept, gain_term0 = call(
        bound(terms_kernel, rank=rank),
        [shape(rank, features), shape(1, features, dtype=F32)],
        [kept, got0, fetched0, grad0, norm_gain, down],
        left=(0,),
        left_outs=(0,),
        aliases=[(0, 0)],
        scratch=[tile, sems((1,))],
        cost=LONG,
        name="terms",
    )
    payload, kept, tokens1 = call(
        bound(second_kernel, rank=rank),
        [shape(rows, 3 * rank + LANES), shape(rank, features), shape(rows, features)],
        [kept, beside_in, across_in, fresh_input, beside_out, weight, column_sum, up, other],
        left=(0, 4),
        left_outs=(0, 1, 2),
        aliases=[(0, 1)],
        scratch=[tile, tile, pltpu.VMEM((rows, 3 * rank + LANES), BF16), sems((5,))],
        name="second",
    )
    got = across(payload)
    partner1 = mirrored(tokens1)
    (payload,) = call(
        bound(late_kernel, peers=peers, rank=rank, width=width),
        [shape(rows, 3 * rank + LANES)],
        [got, columns],
        left_outs=(0,),
        scratch=[pltpu.VMEM((3, rows, rank), BF16), pltpu.VMEM((rows, LANES), BF16), sems((4,))],
        name="late",
    )
    got1 = across(payload)
    stash, done = call(
        stash_kernel,
        [shape(*held_stash.shape), shape(8, LANES, dtype=F32)],
        [evict, held_stash, both, partner1],
        smem=(0,),
        cost=LONG,
        name="stash",
    )
    up_grad, next_output, input_grad, gain_grad, down_grad = call(
        bound(last_kernel, rank=rank),
        [
            shape(rank, features),
            shape(rows, features),
            shape(rows, features),
            shape(1, features, dtype=F32),
            shape(features, rank),
        ],
        [kept, tokens1, done, got1, got0, grad0, gain_term0, norm_gain, down, up],
        left=(0, 1, 2),
        left_outs=(0, 1, 2, 4),
        aliases=[(0, 0), (1, 1)],
        scratch=[
            pltpu.VMEM((4, rows, features), BF16),
            pltpu.VMEM((rank, features), BF16),
            tile,
            tile,
            pltpu.VMEM((features, rank), BF16),
            sems((4,)),
            sems((2,)),
            sems((CHUNKS,)),
            sems((CHUNKS,)),
        ],
        name="last",
    )
    return (next_output[None], input_grad[None], stash, gain_grad, down_grad[None], up_grad[None])


def solution(mesh):
    placed = (
        P("section", None, "dp"),
        P(None, "dp"),
        P("section", None, "dp"),
        P("section", None, None, "dp"),
        P("section", "dp"),
        P("section", "dp", None),
        P("section", None, "dp"),
        P(),
        P(),
    )
    return jax.shard_map(
        on_device,
        mesh=mesh,
        in_specs=placed,
        out_specs=(
            P("section", None, "dp"),
            P("section", None, "dp"),
            P("section", None, None, "dp"),
            P("section", "dp"),
            P("section", "dp", None),
            P("section", None, "dp"),
        ),
        check_vma=False,
    )
```
